32 devices in a mesh: heads: 4 (over x, core), blk: 8 (over z, y).
Axes of the slice: x: 2, y: 2, z: 4, core: 2. Of those that a mesh axis runs over, the one named last changes fastest.
Arguments:
- tokens: bfloat16 [4096, 1536], P(('heads', 'blk')), may hold values from -8 to 8
- cotangent: bfloat16 [4096, 1536], P(('heads', 'blk')), may hold values from -8 to 8
- routes: int32 [4096, 2], P(('heads', 'blk')), may hold values from 0 to 3, all different within a row; in each aligned block of 128 rows (0 to 127, 128 to 255, ...) at most 96 rows name the same one
- doc_lengths: int32 [16], replicated, may hold values from 1 to 2048, 4096 in all
- attn_norm: float32 [1536], P(('heads', 'blk')), may hold values from 0.25 to 1.75
- w_query: float32 [1536, 1536], P(('heads', 'blk')), may hold values from -0.15625 to 0.15625
- key_weight: float32 [1536, 512], P(('heads', 'blk')), may hold values from -0.15625 to 0.15625
- value_weight: float32 [1536, 512], P(('heads', 'blk')), may hold values from -0.15625 to 0.15625
- w_output: float32 [1536, 1536], P(('heads', 'blk')), may hold values from -2.5 to 2.5
- ffn_norm: float32 [1536], P(('heads', 'blk')), may hold values from 0.25 to 1.75
- w_router: float32 [1536, 4], P(('heads', 'blk')), may hold values from -0.078125 to 0.078125
- w_gate: float32 [4, 1536, 1024], P('heads', 'blk'), may hold values from -0.15625 to 0.15625
- w_up: float32 [4, 1536, 1024], P('heads', 'blk'), may hold values from -0.15625 to 0.15625
- w_down: float32 [4, 1024, 1536], P('heads', 'blk'), may hold values from -0.1875 to 0.1875
Outputs:
- mixed: bfloat16 [4096, 1536], P(('heads', 'blk'))
- grad_tokens: bfloat16 [4096, 1536], P(('heads', 'blk'))
- grad_attn_norm: float32 [1536], P(('heads', 'blk'))
- grad_w_query: float32 [1536, 1536], P(('heads', 'blk'))
- grad_w_key: float32 [1536, 512], P(('heads', 'blk'))
- grad_w_value: float32 [1536, 512], P(('heads', 'blk'))
- grad_w_output: float32 [1536, 1536], P(('heads', 'blk'))
- grad_ffn_norm: float32 [1536], P(('heads', 'blk'))
- grad_w_router: float32 [1536, 4], P(('heads', 'blk'))
- grad_w_gate: float32 [4, 1536, 1024], P('heads', 'blk')
- grad_w_up: float32 [4, 1536, 1024], P('heads', 'blk')
- grad_w_down: float32 [4, 1024, 1536], P('heads', 'blk')
The draws below stay inside these ranges and needn't reach their ends.
Inputs may be any that keep to these rules, and one draw needn't show every extreme that they name: `routes`: among the rows of one device each expert is named by at most 96 rows; a row names two different experts. `doc_lengths`: the lengths sum to 4096; the longest is exactly 2048.
All inputs are finite; a program needn't handle non-finite values.
Results may differ from the reference program's by a relative error of at most 0.03.
Values may be sent and summed in bfloat16 or wider, within the bound.
No kernel may reach another device: no remote copies, remote signals or barrier semaphores. Data moves between devices by JAX's collectives and lax.ppermute only.
A program may use at most 192 MiB of HBM per device.

```python
import math
import jax
import jax.numpy as jnp
import numpy as np
from jax import lax

MODEL_WIDTH = 1536
QUERY_HEADS = 24
KEY_VALUE_HEADS = 8
HEAD_WIDTH = 64
FF = 1024
TOP = 2
DOCS = 16
TOK_DEV = 128
EXPERTS = 4
STREAM_TOKENS = 4096
CAP = 96
DOC_MOST = 2048


def with_spikes(values, rng, source, target, shards_of, factor):
    def block_of(position):
        return (jnp.arange(values.shape[position]) // (values.shape[position] // shards_of)).reshape((-1,) + (1,) * (values.ndim - 1 - position))

    near = jax.random.permutation(rng, shards_of)[block_of(target)]
    other_side = (block_of(target) + shards_of // 2) % shards_of
    return jnp.where((block_of(source) == near) | (block_of(source) == other_side), factor * values, values)


def block_levels(rng, dims, shards, low, top_value):
    factor_of, own = 1.0, jax.random.fold_in(rng, 6)
    for position, blocks in shards:
        steps = jnp.exp(jax.random.uniform(jax.random.fold_in(own, position), (blocks,), jnp.float32, low / len(shards), top_value / len(shards)))
        factor_of = factor_of * jnp.repeat(steps, dims[position] // blocks).reshape([-1 if axis == position else 1 for axis in range(len(dims))])
    return factor_of


def profile(number_of, total, bound, slope):
    weights = [(1 << 20) // math.isqrt(rank ** slope) + 1 for rank in range(2, number_of + 1)]
    spare, given = total - bound - (number_of - 1), [1] * (number_of - 1)
    while spare > 0:
        candidates = [i for i in range(number_of - 1) if given[i] < bound]
        mass, budget = sum([weights[i] for i in candidates]), spare
        for i in candidates:
            addition = min(bound - given[i], max(1, budget * weights[i] // mass), spare)
            given[i] = given[i] + addition
            spare = spare - addition
    return np.array([bound] + given)


def uneven_parts(rng, count, total, limit, skew):
    if count == 2:
        one = jax.random.randint(rng, (), max(1, total - limit), min(limit, total - 1) + 1)
        return jnp.stack([one, total - one])
    tallies = jnp.asarray(profile(count, total, limit, skew), jnp.int32)
    pairs = (count - 1) // 2
    source_of, receiver = tallies[1:1 + 2 * pairs:2], tallies[2:2 + 2 * pairs:2]
    room = jnp.minimum(source_of - 1, limit - receiver)
    shifted = jax.random.randint(jax.random.fold_in(rng, 1), (pairs,), 0, 1 << 20) % (room + 1)
    tallies = tallies.at[1:1 + 2 * pairs:2].set(source_of - shifted).at[2:2 + 2 * pairs:2].set(receiver + shifted)
    return tallies[jax.random.permutation(jax.random.fold_in(rng, 2), count)]


def shared_out(stream_key, own, number, rows, number_of, top, limit, slope):
    ranking = jax.random.permutation(stream_key, number_of)
    packed, usual = portions_of(number_of, rows * top, limit, slope, True), portions_of(number_of, rows * top, limit, slope, False)
    places = jnp.arange(number_of)

    def named(sizes, turn):
        used = int((sizes > 0).sum())
        fixed = max(1, used // 4)
        shifted = fixed + (places - fixed + turn * (used - fixed)) % max(1, number_of - fixed)
        return jnp.zeros((number_of,), jnp.int32).at[ranking[jnp.where(places < fixed, places, shifted)]].set(jnp.asarray(sizes, jnp.int32))

    sizes = jnp.where(number % 4 == 0, named(packed, number // 4), named(usual, number - number // 4 - 1))
    mixed = jax.random.permutation(jax.random.fold_in(own, 3), number_of)
    source_of, receiver = mixed[0:number_of // 2 * 2:2], mixed[1:number_of // 2 * 2:2]
    margin = jnp.minimum(sizes[source_of] - 1, limit - sizes[receiver]) // 2
    margin = jnp.where((source_of == ranking[0]) | (receiver == ranking[0]) | (sizes[receiver] == 0), 0, jnp.maximum(margin, 0))
    shifted = jax.random.randint(jax.random.fold_in(own, 4), (number_of // 2,), 0, 1 << 20) % (margin + 1)
    sizes = sizes.at[source_of].add(-shifted).at[receiver].add(shifted)
    members = jnp.searchsorted(jnp.cumsum(sizes), jnp.arange(rows * top), side="right").astype(jnp.int32)
    table = members.reshape(top, rows).T
    table = table[jax.random.permutation(jax.random.fold_in(own, 1), rows)]
    turn = jax.random.randint(jax.random.fold_in(own, 2), (rows, 1), 0, top)
    return jnp.take_along_axis(table, (jnp.arange(top)[None, :] + turn) % top, axis=1)


def portions_of(number_of, total, reach, skew, full):
    loads = [(1 << 20) // math.isqrt(standing ** skew) + 1 for standing in range(1, number_of + 1)]
    largest = reach if full else min(reach, max(-(-total // number_of), total * loads[0] // sum(loads)))
    least = 1 if total - largest >= number_of - 1 else 0
    holding, rest = [largest] + [least] * (number_of - 1), total - largest - least * (number_of - 1)
    while rest > 0:
        movable = [i for i in range(1, number_of) if holding[i] < largest] or [i for i in range(1, number_of) if holding[i] < reach]
        pool, remaining = sum([loads[i] for i in movable]), rest
        for i in movable:
            more = min(reach - holding[i], max(1, remaining * loads[i] // pool), rest)
            holding[i] = holding[i] + more
            rest = rest - more
    return np.array(holding)


def gaussian(own_key, extent, width, most, shards=(), kind=jnp.bfloat16):
    level = block_levels(own_key, extent, shards, -0.22, 0.18) if shards else 1.0
    entries = jax.random.normal(own_key, extent, jnp.float32) * width * level
    return jnp.minimum(jnp.maximum(entries, -most), most).astype(kind)


def heavy_noise(stream_key, dims, deviation, limit, cuts, heavy, held_as=jnp.bfloat16):
    values = deviation * jax.random.normal(stream_key, dims, jnp.float32)
    if cuts:
        values = values * block_levels(stream_key, dims, cuts, -0.22, 0.18)
    return jnp.clip(with_spikes(values, jax.random.fold_in(stream_key, 3), *heavy), -limit, limit).astype(held_as)


def setup_inputs(seed: int = 0) -> dict:
    seeds = jax.random.split(jax.random.key(seed), 15)
    tokens = heavy_noise(seeds[0], (STREAM_TOKENS, MODEL_WIDTH), 1.0, 8.0, ((0, 32),), (0, 1, 32, 2.75))
    cotangent = gaussian(seeds[1], (STREAM_TOKENS, MODEL_WIDTH), 1.0, 8.0, ((0, 32),))
    routes_keys = jax.random.split(jax.random.fold_in(seeds[2], 1), STREAM_TOKENS // TOK_DEV)
    routes_turns = jax.random.permutation(jax.random.fold_in(seeds[2], 3), STREAM_TOKENS // TOK_DEV)
    routes = jax.vmap(lambda own, number: shared_out(jax.random.fold_in(seeds[2], 2), own, number, TOK_DEV, EXPERTS, TOP, CAP, 1))(routes_keys, routes_turns).reshape((STREAM_TOKENS, TOP))
    doc_lengths = uneven_parts(seeds[3], DOCS, STREAM_TOKENS, DOC_MOST, 2).astype(jnp.int32)
    attn_norm = jnp.clip(1.0 + 0.15 * jax.random.normal(seeds[4], (MODEL_WIDTH,), jnp.float32), 0.25, 1.75)
    w_query = gaussian(seeds[5], (MODEL_WIDTH, QUERY_HEADS * HEAD_WIDTH), MODEL_WIDTH ** -0.5, 0.15625, ((0, 32),), jnp.float32)
    key_weight = gaussian(seeds[6], (MODEL_WIDTH, KEY_VALUE_HEADS * HEAD_WIDTH), MODEL_WIDTH ** -0.5, 0.15625, ((0, 32),), jnp.float32)
    value_weight = gaussian(seeds[7], (MODEL_WIDTH, KEY_VALUE_HEADS * HEAD_WIDTH), MODEL_WIDTH ** -0.5, 0.15625, ((0, 32),), jnp.float32)
    w_output = gaussian(seeds[8], (QUERY_HEADS * HEAD_WIDTH, MODEL_WIDTH), (QUERY_HEADS * HEAD_WIDTH // 256) ** -0.5, 2.5, ((0, 32),), jnp.float32)
    ffn_norm = jnp.clip(1.0 + 0.15 * jax.random.normal(seeds[9], (MODEL_WIDTH,), jnp.float32), 0.25, 1.75)
    w_router = gaussian(seeds[10], (MODEL_WIDTH, EXPERTS), (4 * MODEL_WIDTH) ** -0.5, 0.078125, ((0, 32),), jnp.float32)
    w_gate = gaussian(seeds[11], (EXPERTS, MODEL_WIDTH, FF), MODEL_WIDTH ** -0.5, 0.15625, ((0, 4), (1, 8)), jnp.float32)
    w_up = gaussian(seeds[12], (EXPERTS, MODEL_WIDTH, FF), MODEL_WIDTH ** -0.5, 0.15625, ((0, 4), (1, 8)), jnp.float32)
    w_down = gaussian(seeds[13], (EXPERTS, FF, MODEL_WIDTH), FF ** -0.5, 0.1875, ((0, 4), (1, 8)), jnp.float32)
    return {"tokens": tokens, "cotangent": cotangent, "routes": routes, "doc_lengths": doc_lengths, "attn_norm": attn_norm, "w_query": w_query, "key_weight": key_weight, "value_weight": value_weight, "w_output": w_output, "ffn_norm": ffn_norm, "w_router": w_router, "w_gate": w_gate, "w_up": w_up, "w_down": w_down}


@jax.custom_vjp
def low(v):
    return lax.optimization_barrier(v.astype(jnp.bfloat16)).astype(jnp.float32)

@jax.custom_vjp
def low_back(v):
    return v

def low_keep(v):
    return (low(v), None)

def low_pass(kept, grad):
    return (grad,)

def back_keep(v):
    return (v, None)

def back_low(kept, grad):
    return (low(grad),)
low.defvjp(low_keep, low_pass)
low_back.defvjp(back_keep, back_low)
epsilon_norm = 1e-05
highest = lax.Precision.HIGHEST
masked_score = -1e+30

def rms_scale(value_matrix, gain):
    inverse = lax.rsqrt(lax.optimization_barrier(jnp.mean(value_matrix * value_matrix, axis=-1, keepdims=True)) + epsilon_norm)
    return value_matrix * inverse * gain

def product(left, right):
    return jnp.dot(left, right, precision=highest, preferred_element_type=jnp.float32)

def document_of(positions, ends):
    return lax.optimization_barrier(jnp.sum((positions[:, None] >= ends[None, :]).astype(jnp.int32), axis=1))

def attention(query_matrix, key_matrix, value_matrix, docid):
    rows_per_block = min(512, STREAM_TOKENS)
    query_group = QUERY_HEADS // KEY_VALUE_HEADS
    positions = jnp.arange(STREAM_TOKENS, dtype=jnp.int32)
    blocks_of_query = query_matrix.reshape(STREAM_TOKENS // rows_per_block, rows_per_block, KEY_VALUE_HEADS, query_group, HEAD_WIDTH)
    heads_of_key = jnp.transpose(key_matrix.reshape(STREAM_TOKENS, KEY_VALUE_HEADS, HEAD_WIDTH), (1, 0, 2))
    heads_of_value = jnp.transpose(value_matrix.reshape(STREAM_TOKENS, KEY_VALUE_HEADS, HEAD_WIDTH), (1, 0, 2))

    def one_block(inputs):
        block, block_pos, block_doc = inputs
        allowed = (block_doc[:, None] == docid[None, :]) & (positions[None, :] <= block_pos[:, None])

        def one_group(parts):
            query_part, key_part, value_part = parts
            raw = jnp.einsum('ngd,md->ngm', query_part, key_part, precision=highest)
            scores = jnp.where(allowed[:, None, :], low_back(raw) * 0.125, masked_score)
            peak = lax.optimization_barrier(jnp.max(scores, axis=-1, keepdims=True))
            total = peak + jnp.log(lax.optimization_barrier(jnp.sum(jnp.exp(scores - peak), axis=-1, keepdims=True)))
            probs = low(jnp.exp(scores - total))
            return jnp.einsum('ngm,md->ngd', probs, value_part, precision=highest)
        grouped = lax.map(jax.checkpoint(one_group), (jnp.transpose(block, (1, 0, 2, 3)), heads_of_key, heads_of_value))
        return jnp.transpose(grouped, (1, 0, 2, 3))
    result = lax.map(jax.checkpoint(one_block), (blocks_of_query, positions.reshape(-1, rows_per_block), docid.reshape(-1, rows_per_block)))
    return result.reshape(STREAM_TOKENS, QUERY_HEADS * HEAD_WIDTH)

def run_expert(rows, gate_w, up_w, down_w):
    gate_pre = low_back(jnp.einsum('ntd,df->ntf', rows, gate_w, precision=highest))
    up_pre = low_back(jnp.einsum('ntd,df->ntf', rows, up_w, precision=highest))
    inner = low(gate_pre * jax.nn.sigmoid(gate_pre) * up_pre)
    return low_back(low(jnp.einsum('ntf,fd->ntd', inner, down_w, precision=highest)))

def layer(start, params, routes, docid):
    gain_one, query_w, key_w, value_w, output_w, gain_two, router_w, gate_w, up_w, down_w = [low(p) for p in params]
    normed = low(rms_scale(start, gain_one))
    query_matrix = low_back(low(product(normed, query_w)))
    key_matrix = low_back(low(product(normed, key_w)))
    value_matrix = low_back(low(product(normed, value_w)))
    attended = low_back(low(attention(query_matrix, key_matrix, value_matrix, docid)))
    hidden = start + low_back(product(attended, output_w))
    normed_ffn = low(rms_scale(hidden, gain_two))
    logits = product(normed_ffn, router_w)
    onehot = (routes[:, :, None] == jnp.arange(EXPERTS, dtype=jnp.int32)[None, None, :]).astype(jnp.float32)
    chosen = lax.optimization_barrier(jnp.sum(onehot * logits[:, None, :], axis=-1))
    peak = lax.optimization_barrier(jnp.max(chosen, axis=-1, keepdims=True))
    raised = jnp.exp(chosen - peak)
    gates = raised / lax.optimization_barrier(jnp.sum(raised, axis=-1, keepdims=True))
    rows = low_back(jnp.broadcast_to(normed_ffn[:, None, :], (STREAM_TOKENS, TOP, MODEL_WIDTH)))
    expert_step = jax.checkpoint(run_expert)
    combined = jnp.zeros((STREAM_TOKENS, TOP, MODEL_WIDTH), jnp.float32)
    for expert in range(EXPERTS):
        combined = combined + onehot[:, :, expert:expert + 1] * expert_step(rows, gate_w[expert], up_w[expert], down_w[expert])
    return hidden + lax.optimization_barrier(jnp.sum(gates[:, :, None] * combined, axis=1))

def reference(tokens, cotangent, routes, doc_lengths, attn_norm, w_query, key_weight, value_weight, w_output, ffn_norm, w_router, w_gate, w_up, w_down):
    ends = jnp.cumsum(doc_lengths).astype(jnp.int32)
    docid = document_of(jnp.arange(STREAM_TOKENS, dtype=jnp.int32), ends)
    params = (attn_norm, w_query, key_weight, value_weight, w_output, ffn_norm, w_router, w_gate, w_up, w_down)

    def apply(start, weights):
        return layer(start, weights, routes, docid)
    result, pull = jax.vjp(apply, tokens.astype(jnp.float32), params)
    grad_start, grads = pull(cotangent.astype(jnp.float32))
    return (result.astype(jnp.bfloat16), grad_start.astype(jnp.bfloat16), grads[0], grads[1], grads[2], grads[3], grads[4], grads[5], grads[6], grads[7], grads[8], grads[9])
```

```python
import functools

import jax
import jax.numpy as jnp
from jax import lax
from jax.experimental import pallas as pl
from jax.experimental.pallas import tpu as pltpu
from jax.sharding import PartitionSpec as P

QUERY_HEADS = 24
KEY_VALUE_HEADS = 8
HEAD_WIDTH = 64
CAP = 96
HEADS = 4
GROUP = QUERY_HEADS // KEY_VALUE_HEADS
KV_LOCAL = KEY_VALUE_HEADS // HEADS
Q_LOCAL = KV_LOCAL * GROUP
Q_COLS = Q_LOCAL * HEAD_WIDTH
K_COLS = KV_LOCAL * HEAD_WIDTH
STEP = 256

epsilon_norm = 1e-05
highest = lax.Precision.HIGHEST
masked_score = -1e30
bf16 = jnp.bfloat16
f32 = jnp.float32
BOTH = ("heads", "blk")
VMEM_LIMIT = 60 * 1024 * 1024


def swap(value, heads_bits, blk_bits):
    count, blocks = lax.axis_size("heads"), lax.axis_size("blk")
    pairs = []
    for i in range(count * blocks):
        h, b = divmod(i, blocks)
        pairs.append((i, (h ^ heads_bits) * blocks + (b ^ blk_bits)))
    return lax.ppermute(value, BOTH, pairs)


def heads_gather(value):
    far = swap(value, 2, 0)
    near = swap(value, 1, 0)
    return jnp.stack([value, near, far, swap(far, 1, 0)])


def heads_reduce(parts):
    got = swap(jnp.stack([parts[1], parts[3]]), 1, 0)
    onward = (parts[2].astype(f32) + got[1].astype(f32)).astype(parts.dtype)
    far = swap(onward, 2, 0)
    return parts[0].astype(f32) + got[0].astype(f32) + far.astype(f32)


def blk_gather(value):
    blocks = lax.axis_size("blk")
    if blocks > 8:
        whole = lax.all_gather(value, "blk", axis=0, tiled=False)
        return jnp.take(whole, lax.axis_index("blk") ^ jnp.arange(blocks), axis=0)
    pieces = [None] * blocks
    for r in range(0, blocks, 2):
        piece = swap(value, 0, r) if r else value
        pieces[r] = piece
        pieces[r + 1] = swap(piece, 0, 1)
    return jnp.stack(pieces)


def blk_reduce(parts):
    blocks = lax.axis_size("blk")
    if blocks > 8:
        whole = jnp.take(parts, lax.axis_index("blk") ^ jnp.arange(blocks), axis=0)
        return lax.psum_scatter(whole, "blk", scatter_dimension=0, tiled=False).astype(f32)
    total = None
    for r in range(blocks - 2, -1, -2):
        got = swap(parts[r + 1], 0, 1)
        here = parts[r].astype(f32) + got.astype(f32)
        if r:
            here = swap(here.astype(parts.dtype), 0, r).astype(f32)
        total = here if total is None else total + here
    return total


def blk_unshuffle(pieces):
    blocks = pieces.shape[0]
    b = lax.axis_index("blk")
    return jnp.stack(
        [lax.dynamic_index_in_dim(pieces, b ^ i, 0, keepdims=False) for i in range(blocks)]
    )


def z_groups(blocks):
    return [[i for i in range(blocks) if i % 2 == y] for y in range(2)]


def expand_heads(transposed, dtype):
    rows = []
    n = transposed.shape[1]
    zero = jnp.zeros((HEAD_WIDTH, n), dtype)
    for g in range(KV_LOCAL):
        columns = []
        for head in range(Q_LOCAL):
            if head // GROUP == g:
                columns.append(transposed[head * HEAD_WIDTH : (head + 1) * HEAD_WIDTH].astype(dtype))
            else:
                columns.append(zero)
        rows.append(jnp.concatenate(columns, axis=1))
    return jnp.concatenate(rows, axis=0)


def collapse_heads(wide, n):
    pieces = []
    for head in range(Q_LOCAL):
        g = head // GROUP
        pieces.append(wide[g * HEAD_WIDTH : (g + 1) * HEAD_WIDTH, head * n : (head + 1) * n])
    return jnp.concatenate(pieces, axis=0)


def key_rows(kv_ref, r, j, low, high):
    return jnp.concatenate(
        [kv_ref[r, j, :, low:high], kv_ref[r + 1, j, :, low:high]], axis=0
    )


def step_place(t, h, b, blocks, tok_dev):
    half = blocks // 2
    owner_h = t // half
    owner_z = t % half
    j = owner_h ^ h
    r = (owner_z ^ (b // 2)) * 2
    y = b % 2
    row = lax.broadcasted_iota(jnp.int32, (2 * tok_dev, 1), 0)
    base = (owner_h * blocks + owner_z * 2) * tok_dev
    second = row >= tok_dev
    position = base + jnp.where(
        second, row - tok_dev + (1 - y) * tok_dev, row + y * tok_dev
    )
    return r, j, position


def attend_kernel(blocks, scal_ref, q_ref, kv_ref, start_ref, att_ref, lse_ref, top_ref, sum_ref, acc_ref):
    tok_dev = q_ref.shape[1]
    h, b = scal_ref[0], scal_ref[1]

    def one(j, unused):
        block = (h ^ j) * blocks + b
        queries = (q_ref[j].astype(f32) * 0.125).T
        wide = expand_heads(queries, bf16)
        lane = lax.broadcasted_iota(jnp.int32, (1, tok_dev), 1)
        query_pos = jnp.concatenate([block * tok_dev + lane] * Q_LOCAL, axis=1)
        start = jnp.concatenate([start_ref[j]] * Q_LOCAL, axis=1)
        top_ref[...] = jnp.full(top_ref.shape, masked_score, f32)
        sum_ref[...] = jnp.zeros(sum_ref.shape, f32)
        acc_ref[...] = jnp.zeros(acc_ref.shape, f32)

        def step(t, unused):
            r, jk, position = step_place(t, h, b, blocks, tok_dev)
            keys = key_rows(kv_ref, r, jk, 0, K_COLS)
            values = key_rows(kv_ref, r, jk, K_COLS, 2 * K_COLS)
            scores = lax.dot_general(keys, wide, (((1,), (0,)), ((), ())), preferred_element_type=f32)
            allowed = (position >= start) & (position <= query_pos)
            scores = jnp.where(allowed, scores, masked_score)
            old = top_ref[...]
            new = jnp.maximum(old, jnp.max(scores, axis=0, keepdims=True))
            rescale = jnp.exp(old - new)
            weights = jnp.exp(scores - new)
            top_ref[...] = new
            sum_ref[...] = sum_ref[...] * rescale + jnp.sum(weights, axis=0, keepdims=True)
            acc_ref[...] = acc_ref[...] * rescale + lax.dot_general(
                values, weights.astype(bf16), (((0,), (0,)), ((), ())), preferred_element_type=f32
            )
            return unused

        lax.fori_loop(scal_ref[2 + j], block // 2 + 1, step, 0)
        total = sum_ref[...]
        out = collapse_heads(acc_ref[...] / total, tok_dev)
        att_ref[j] = out.T.astype(bf16)
        lse_ref[j] = top_ref[...] + jnp.log(total)
        return unused

    lax.fori_loop(0, HEADS, one, 0)


def attend(scal, queries, kv, start):
    blocks, tok_dev = kv.shape[0], kv.shape[2]
    wide = Q_LOCAL * tok_dev
    return pl.pallas_call(
        functools.partial(attend_kernel, blocks),
        out_shape=(
            jax.ShapeDtypeStruct((HEADS, tok_dev, Q_COLS), bf16),
            jax.ShapeDtypeStruct((HEADS, 1, wide), f32),
        ),
        in_specs=[
            pl.BlockSpec(memory_space=pltpu.SMEM),
            pl.BlockSpec(memory_space=pltpu.VMEM),
            pl.BlockSpec(memory_space=pltpu.VMEM),
            pl.BlockSpec(memory_space=pltpu.VMEM),
        ],
        out_specs=(
            pl.BlockSpec(memory_space=pltpu.VMEM),
            pl.BlockSpec(memory_space=pltpu.VMEM),
        ),
        scratch_shapes=[
            pltpu.VMEM((1, wide), f32),
            pltpu.VMEM((1, wide), f32),
            pltpu.VMEM((K_COLS, wide), f32),
        ],
        compiler_params=pltpu.CompilerParams(vmem_limit_bytes=VMEM_LIMIT),
        name="attend",
    )(scal, queries, kv, start)


def attend_back_kernel(blocks, scal_ref, q_ref, kv_ref, start_ref, att_ref, lse_ref, grad_ref, dq_ref, dkv_ref, acc_ref, term_ref):
    tok_dev = q_ref.shape[1]
    h, b = scal_ref[0], scal_ref[1]
    term_ref[...] = jnp.zeros(term_ref.shape, f32)

    def one(j, unused):
        block = (h ^ j) * blocks + b
        wide = expand_heads((q_ref[j].astype(f32) * 0.125).T, bf16)
        grad_t = grad_ref[j].astype(f32).T
        wide_grad = expand_heads(grad_t, bf16)
        product = grad_t * att_ref[j].astype(f32).T
        delta = jnp.concatenate(
            [
                jnp.sum(product[head * HEAD_WIDTH : (head + 1) * HEAD_WIDTH], axis=0, keepdims=True)
                for head in range(Q_LOCAL)
            ],
            axis=1,
        )
        lse = lse_ref[j]
        lane = lax.broadcasted_iota(jnp.int32, (1, tok_dev), 1)
        query_pos = jnp.concatenate([block * tok_dev + lane] * Q_LOCAL, axis=1)
        start = jnp.concatenate([start_ref[j]] * Q_LOCAL, axis=1)
        acc_ref[...] = jnp.zeros(acc_ref.shape, f32)

        def step(t, unused):
            r, jk, position = step_place(t, h, b, blocks, tok_dev)
            keys = key_rows(kv_ref, r, jk, 0, K_COLS)
            values = key_rows(kv_ref, r, jk, K_COLS, 2 * K_COLS)
            scores = lax.dot_general(keys, wide, (((1,), (0,)), ((), ())), preferred_element_type=f32)
            allowed = (position >= start) & (position <= query_pos)
            probs = jnp.exp(jnp.where(allowed, scores - lse, masked_score))
            grad_probs = lax.dot_general(
                values, wide_grad, (((1,), (0,)), ((), ())), preferred_element_type=f32
            )
            grad_scores = (probs * (grad_probs - delta)).astype(bf16)
            acc_ref[...] += lax.dot_general(
                keys, grad_scores, (((0,), (0,)), ((), ())), preferred_element_type=f32
            )
            key_term = lax.dot_general(
                grad_scores, wide, (((1,), (1,)), ((), ())), preferred_element_type=f32
            )
            value_term = lax.dot_general(
                probs.astype(bf16), wide_grad, (((1,), (1,)), ((), ())), preferred_element_type=f32
            )
            both = jnp.concatenate([key_term, value_term], axis=1)
            term_ref[r, jk] += both[:tok_dev]
            term_ref[r + 1, jk] += both[tok_dev:]
            return unused

        lax.fori_loop(scal_ref[2 + j], block // 2 + 1, step, 0)
        dq_ref[j] = (collapse_heads(acc_ref[...], tok_dev) * 0.125).T.astype(bf16)
        return unused

    lax.fori_loop(0, HEADS, one, 0)
    dkv_ref[...] = term_ref[...].astype(bf16)


def attend_back(scal, queries, kv, start, att, lse, grad):
    blocks, tok_dev = kv.shape[0], kv.shape[2]
    wide = Q_LOCAL * tok_dev
    return pl.pallas_call(
        functools.partial(attend_back_kernel, blocks),
        out_shape=(
            jax.ShapeDtypeStruct((HEADS, tok_dev, Q_COLS), bf16),
            jax.ShapeDtypeStruct(kv.shape, bf16),
        ),
        in_specs=[pl.BlockSpec(memory_space=pltpu.SMEM)] + [pl.BlockSpec(memory_space=pltpu.VMEM)] * 6,
        out_specs=(
            pl.BlockSpec(memory_space=pltpu.VMEM),
            pl.BlockSpec(memory_space=pltpu.VMEM),
        ),
        scratch_shapes=[
            pltpu.VMEM((K_COLS, wide), f32),
            pltpu.VMEM(kv.shape, f32),
        ],
        compiler_params=pltpu.CompilerParams(vmem_limit_bytes=VMEM_LIMIT),
        name="attend_back",
    )(scal, queries, kv, start, att, lse, grad)


def small_share(values):
    devices = lax.axis_size("heads") * lax.axis_size("blk")
    n, width = values.shape
    padded = jnp.pad(values, ((0, 8 - n), (0, 128 - width)))
    got = lax.all_to_all(
        jnp.broadcast_to(padded[None], (devices, 8, 128)), BOTH, 0, 0, tiled=True
    )
    return jnp.transpose(got[:, :n, :width], (1, 0, 2)).reshape(n, devices * width)


def small_sum(values):
    devices = lax.axis_size("heads") * lax.axis_size("blk")
    n = values.shape[0]
    width = values.shape[1] // devices
    parts = jnp.transpose(values.reshape(n, devices, width), (1, 0, 2))
    padded = jnp.pad(parts, ((0, 0), (0, 8 - n), (0, 128 - width)))
    got = lax.all_to_all(padded, BOTH, 0, 0, tiled=True)
    return jnp.sum(got, axis=0)[:n, :width]


def expert_route(value, core_is_y, back):
    count, blocks = lax.axis_size("heads"), lax.axis_size("blk")
    pairs = []
    for i in range(count * blocks):
        h, b = divmod(i, blocks)
        if h % 2 == b % 2:
            pairs.append((i, i))
        else:
            pairs.append((i, (h ^ 1) * blocks + (b ^ 1)))
    return lax.ppermute(value, BOTH, pairs)


def pair_order(columns, group):
    rows = columns.shape[0]
    return jnp.swapaxes(columns.reshape(rows, -1, 2, group), 1, 2).reshape(rows, -1)


def pair_order_back(columns, group):
    rows = columns.shape[0]
    return jnp.swapaxes(columns.reshape(rows, 2, -1, group), 1, 2).reshape(rows, -1)


def halves(columns, core):
    half = columns.shape[1] // 2
    first, second = columns[:, :half], columns[:, half:]
    return jnp.where(core == 0, first, second), jnp.where(core == 0, second, first)


def unhalve(own, other, core):
    return jnp.concatenate(
        [jnp.where(core == 0, own, other), jnp.where(core == 0, other, own)], axis=1
    )


def dot(a, b):
    return jnp.dot(a, b, preferred_element_type=f32)


def dot_tn(a, b):
    return lax.dot_general(a, b, (((0,), (0,)), ((), ())), preferred_element_type=f32)


def dot_nt(a, b):
    return lax.dot_general(a, b, (((1,), (1,)), ((), ())), preferred_element_type=f32)


def unpack_expert(buffer, drows, frows):
    def piece(low, high):
        return buffer[:, low:high].reshape(-1, buffer.shape[2])
    gate = jnp.concatenate([piece(0, drows), piece(drows, 2 * drows)], axis=1)
    up = jnp.concatenate([piece(2 * drows, 3 * drows), piece(3 * drows, 4 * drows)], axis=1)
    base = 4 * drows
    down = jnp.concatenate([piece(base + k * frows, base + (k + 1) * frows) for k in range(3)], axis=1)
    return gate, up, down


def pack_expert(gate, up, down, count):
    pieces = []
    for matrix in (gate, up, down):
        rows = matrix.shape[0] // count
        for k in range(matrix.shape[1] // 512):
            pieces.append(matrix[:, k * 512 : (k + 1) * 512].reshape(count, rows, 512))
    return jnp.concatenate(pieces, axis=1)


def shards(
    tokens,
    cotangent,
    routes,
    doc_lengths,
    attn_norm,
    w_query,
    key_weight,
    value_weight,
    w_output,
    ffn_norm,
    w_router,
    w_gate,
    w_up,
    w_down,
):
    blocks = lax.axis_size("blk")
    tok_dev, model = tokens.shape
    wrows = w_query.shape[0]
    drows = w_gate.shape[1]
    frows = w_down.shape[1]
    experts = w_router.shape[1]
    h, b = lax.axis_index("heads"), lax.axis_index("blk")
    core, x, y = h % 2, h // 2, b % 2
    zn = blocks // 2

    packed = pack_expert(
        pair_order(w_gate[0].astype(bf16), frows),
        pair_order(w_up[0].astype(bf16), frows),
        w_down[0].astype(bf16),
        1,
    )[0]

    heads_cat = jnp.concatenate(
        [
            w_query.astype(bf16).reshape(wrows, HEADS, Q_COLS),
            key_weight.astype(bf16).reshape(wrows, HEADS, K_COLS),
            value_weight.astype(bf16).reshape(wrows, HEADS, K_COLS),
        ],
        axis=2,
    )
    by_head = lax.all_to_all(jnp.swapaxes(heads_cat, 0, 1), "heads", 0, 0, tiled=True)
    weights = blk_unshuffle(blk_gather(by_head))
    weights = jnp.swapaxes(weights, 0, 1).reshape(model, Q_COLS + 2 * K_COLS)
    small = small_share(
        jnp.concatenate(
            [
                attn_norm.astype(bf16)[None],
                ffn_norm.astype(bf16)[None],
                w_router.astype(bf16).T,
            ],
            axis=0,
        )
    )
    gain_one, gain_two = small[0].astype(f32), small[1].astype(f32)
    router_t = small[2 : 2 + experts]
    all_tokens = heads_gather(tokens)
    routed = expert_route(packed, None, False)
    mine = lax.all_gather(routed, "blk", axis=0, tiled=False, axis_index_groups=z_groups(blocks))
    other = swap(mine, 1, 0)
    output_w = lax.all_gather(w_output.astype(bf16), "blk", axis=0, tiled=True)

    ends = jnp.cumsum(doc_lengths)
    block_of = (h ^ jnp.arange(HEADS, dtype=jnp.int32)) * blocks + b
    query_pos = block_of[:, None] * tok_dev + jnp.arange(tok_dev, dtype=jnp.int32)[None, :]
    start = jnp.max(
        jnp.where(ends[None, None, :] <= query_pos[:, :, None], ends[None, None, :], 0), axis=2
    ).astype(jnp.int32)
    scal = jnp.concatenate(
        [jnp.stack([h, b]).astype(jnp.int32), start[:, 0] // (2 * tok_dev)]
    )
    start = start[:, None, :]

    e_own = x * 2 + y
    e_rel = jnp.arange(experts, dtype=jnp.int32) ^ e_own
    member = jnp.sum((routes[:, :, None] == e_rel[None, None, :]).astype(f32), axis=1)
    lower = (
        jnp.arange(tok_dev)[:, None] > jnp.arange(tok_dev)[None, :]
    ).astype(bf16)
    rank = dot(lower, member.astype(bf16))
    slot = jnp.arange(CAP, dtype=f32)
    table_f = (
        (rank.T[:, None, :] == slot[None, :, None]) & (member.T[:, None, :] > 0)
    ).astype(f32)
    table = table_f.astype(bf16).reshape(experts * CAP, tok_dev)
    flip = (jnp.arange(experts)[:, None] == e_rel[None, :]).astype(f32)

    flat_tokens = all_tokens.reshape(HEADS * tok_dev, model)
    start_f = flat_tokens.astype(f32)
    inverse_one = lax.rsqrt(jnp.mean(start_f * start_f, axis=-1, keepdims=True) + epsilon_norm)
    normed = (start_f * inverse_one * gain_one).astype(bf16)
    projected = dot(normed, weights).astype(bf16).reshape(HEADS, tok_dev, Q_COLS + 2 * K_COLS)
    queries = projected[:, :, :Q_COLS]
    kv = blk_gather(projected[:, :, Q_COLS:])
    att, lse = attend(scal, queries, kv, start)
    flat_att = att.reshape(HEADS * tok_dev, Q_COLS)
    branch = heads_reduce(dot(flat_att, output_w).astype(bf16).reshape(HEADS, tok_dev, model))
    own_f = tokens.astype(f32)
    hidden = own_f + branch
    inverse_two = lax.rsqrt(jnp.mean(hidden * hidden, axis=-1, keepdims=True) + epsilon_norm)
    normed_ffn = (hidden * inverse_two * gain_two).astype(bf16)
    logits = dot_nt(normed_ffn, router_t)
    logits = jnp.dot(logits, flip, precision=highest)
    picked = member > 0
    peak = jnp.max(jnp.where(picked, logits, -jnp.inf), axis=-1, keepdims=True)
    raised = jnp.where(picked, jnp.exp(jnp.where(picked, logits - peak, 0.0)), 0.0)
    gates = raised / jnp.sum(raised, axis=-1, keepdims=True)

    def to_experts(rows):
        pieces = rows.reshape(experts, CAP, model)
        return jnp.concatenate(
            [pieces[0]] + [swap(pieces[e], 2 * (e // 2), e % 2) for e in range(1, experts)], axis=0
        )

    own_half, other_half = halves(pair_order(normed_ffn, drows), core)
    sent = dot(table, jnp.concatenate([own_half, other_half], axis=1)).astype(bf16)
    slot_gate = jnp.sum(table_f * gates.T[:, None, :], axis=2).reshape(experts * CAP, 1)
    grad_sent = (dot(table, cotangent) * slot_gate).astype(bf16)
    arrived = to_experts(sent)
    grad_arrived = to_experts(grad_sent)
    half_d = model // 2
    rows_own, rows_other = arrived[:, :half_d], arrived[:, half_d:]
    gate_m, up_m, down_m = unpack_expert(mine, drows, frows)
    gate_o, up_o, down_o = unpack_expert(other, drows, frows)
    gate_pre = dot(rows_own, gate_m) + dot(rows_other, gate_o)
    up_pre = dot(rows_own, up_m) + dot(rows_other, up_o)
    sig = jax.nn.sigmoid(gate_pre)
    inner = (gate_pre * sig * up_pre).astype(bf16)
    inner_own, inner_other = halves(inner, core)
    produced = (dot(inner_own, down_m) + dot(inner_other, down_o)).astype(bf16)
    returned = to_experts(produced)
    grad_inner = unhalve(dot_nt(grad_arrived, down_m), dot_nt(grad_arrived, down_o), core)
    grad_gate_pre = (grad_inner * up_pre * sig * (1.0 + gate_pre * (1.0 - sig))).astype(bf16)
    grad_up_pre = (grad_inner * gate_pre * sig).astype(bf16)
    grad_in = jnp.concatenate(
        [
            dot_nt(grad_gate_pre, gate_m) + dot_nt(grad_up_pre, up_m),
            dot_nt(grad_gate_pre, gate_o) + dot_nt(grad_up_pre, up_o),
        ],
        axis=1,
    ).astype(bf16)
    grad_returned = to_experts(grad_in)
    grads_own = pack_expert(
        dot_tn(rows_own, grad_gate_pre).astype(bf16),
        dot_tn(rows_own, grad_up_pre).astype(bf16),
        dot_tn(inner_own, grad_arrived).astype(bf16),
        zn,
    )
    grads_other = pack_expert(
        dot_tn(rows_other, grad_gate_pre).astype(bf16),
        dot_tn(rows_other, grad_up_pre).astype(bf16),
        dot_tn(inner_other, grad_arrived).astype(bf16),
        zn,
    )
    chip_grads = (grads_own.astype(f32) + swap(grads_other, 1, 0).astype(f32)).astype(bf16)
    z_grads = lax.psum_scatter(
        chip_grads, "blk", scatter_dimension=0, tiled=False, axis_index_groups=z_groups(blocks)
    )
    home = expert_route(z_grads, None, True)
    grad_gate_w, grad_up_w, grad_down_w = unpack_expert(home[None], drows, frows)
    grad_gate_w = pair_order_back(grad_gate_w.astype(f32), frows)
    grad_up_w = pair_order_back(grad_up_w.astype(f32), frows)
    grad_down_w = grad_down_w.astype(f32)

    combine = (table_f * gates.T[:, None, :]).reshape(experts * CAP, tok_dev)
    mixed = (
        hidden
        + lax.dot_general(
            combine, returned.astype(f32), (((0,), (0,)), ((), ())), precision=highest
        )
    ).astype(bf16)
    grad_out = cotangent.astype(f32)
    scored = dot_nt(returned, cotangent).reshape(experts, CAP, tok_dev)
    grad_gates = jnp.sum(scored * table_f, axis=1).T
    mean_gate = jnp.sum(gates * grad_gates, axis=-1, keepdims=True)
    grad_logits = gates * (grad_gates - mean_gate)
    grad_logits = jnp.dot(grad_logits, flip.T, precision=highest)
    grad_router = lax.dot_general(
        grad_logits, normed_ffn.astype(f32), (((0,), (0,)), ((), ())), precision=highest
    )
    routed_grad = dot_tn(table, grad_returned)
    routed_grad = pair_order_back(
        unhalve(routed_grad[:, :half_d], routed_grad[:, half_d:], core), drows
    )
    grad_nf = routed_grad + jnp.dot(grad_logits, router_t.astype(f32), precision=highest)
    scaled = grad_nf * gain_two
    grad_gain_two = jnp.sum(grad_nf * hidden * inverse_two, axis=0)
    grad_hidden = (
        grad_out
        + inverse_two * scaled
        - hidden
        * (inverse_two * inverse_two * inverse_two)
        * jnp.mean(scaled * hidden, axis=-1, keepdims=True)
    )

    branch_grads = heads_gather(grad_hidden.astype(bf16))
    flat_branch = branch_grads.reshape(HEADS * tok_dev, model)
    grad_att = dot_nt(flat_branch, output_w).astype(bf16)
    grad_wout = dot_tn(flat_att, flat_branch).astype(bf16)
    grad_wout = lax.psum_scatter(grad_wout, "blk", scatter_dimension=0, tiled=True).astype(f32)
    dq, dkv = attend_back(
        scal, queries, kv, start, att, lse, grad_att.reshape(HEADS, tok_dev, Q_COLS)
    )
    dkv_own = blk_reduce(dkv).astype(bf16)
    grads = jnp.concatenate([dq, dkv_own], axis=2).reshape(HEADS * tok_dev, Q_COLS + 2 * K_COLS)
    part_normed = dot_nt(grads, weights)
    grad_gain_one = jnp.sum(part_normed * (start_f * inverse_one), axis=0)
    grad_normed = heads_reduce(part_normed.astype(bf16).reshape(HEADS, tok_dev, model))
    own_inverse = inverse_one[:tok_dev]
    scaled_one = grad_normed * gain_one
    grad_tokens = (
        grad_hidden
        + own_inverse * scaled_one
        - own_f
        * (own_inverse * own_inverse * own_inverse)
        * jnp.mean(scaled_one * own_f, axis=-1, keepdims=True)
    ).astype(bf16)

    part_w = dot_tn(normed, grads).astype(bf16)
    part_w = jnp.swapaxes(part_w.reshape(HEADS, blocks, wrows, -1), 0, 1)
    sum_w = blk_reduce(blk_unshuffle(part_w)).astype(bf16)
    by_row = lax.all_to_all(sum_w, "heads", 0, 0, tiled=True)
    by_row = jnp.swapaxes(by_row, 0, 1).astype(f32)
    grad_wq = by_row[:, :, :Q_COLS].reshape(wrows, -1)
    grad_wk = by_row[:, :, Q_COLS : Q_COLS + K_COLS].reshape(wrows, -1)
    grad_wv = by_row[:, :, Q_COLS + K_COLS :].reshape(wrows, -1)
    small_grads = small_sum(
        jnp.concatenate([grad_gain_one[None], grad_gain_two[None], grad_router], axis=0)
    )
    return (
        mixed,
        grad_tokens,
        small_grads[0],
        grad_wq,
        grad_wk,
        grad_wv,
        grad_wout,
        small_grads[1],
        small_grads[2 : 2 + experts].T,
        grad_gate_w[None],
        grad_up_w[None],
        grad_down_w[None],
    )


def solution(mesh):
    rows = P(("heads", "blk"), None)
    flat = P(("heads", "blk"))
    expert = P("heads", "blk", None)
    return jax.shard_map(
        shards,
        mesh=mesh,
        in_specs=(
            rows, rows, rows, P(), flat, rows, rows, rows, rows, flat, rows, expert, expert, expert,
        ),
        out_specs=(
            rows, rows, flat, rows, rows, rows, rows, flat, rows, expert, expert, expert,
        ),
        check_vma=False,
    )
```

```python
import functools

import jax
import jax.numpy as jnp
from jax import lax
from jax.experimental import pallas as pl
from jax.experimental.pallas import tpu as pltpu
from jax.sharding import PartitionSpec as P

QUERY_HEADS = 24
KEY_VALUE_HEADS = 8
HEAD_WIDTH = 64
CAP = 96
HEADS = 4
GROUP = QUERY_HEADS // KEY_VALUE_HEADS
KV_LOCAL = KEY_VALUE_HEADS // HEADS
Q_LOCAL = KV_LOCAL * GROUP
Q_COLS = Q_LOCAL * HEAD_WIDTH
K_COLS = KV_LOCAL * HEAD_WIDTH
STEP = 256

epsilon_norm = 1e-05
highest = lax.Precision.HIGHEST
masked_score = -1e30
bf16 = jnp.bfloat16
f32 = jnp.float32
BOTH = ("heads", "blk")
VMEM_LIMIT = 60 * 1024 * 1024
LANES = 256


def swap(value, heads_bits, blk_bits):
    count, blocks = lax.axis_size("heads"), lax.axis_size("blk")
    pairs = []
    for i in range(count * blocks):
        h, b = divmod(i, blocks)
        pairs.append((i, (h ^ heads_bits) * blocks + (b ^ blk_bits)))
    return lax.ppermute(value, BOTH, pairs)


def heads_gather(value):
    far = swap(value, 2, 0)
    near = swap(value, 1, 0)
    return jnp.stack([value, near, far, swap(far, 1, 0)])


def heads_reduce(parts):
    got = swap(jnp.stack([parts[1], parts[3]]), 1, 0)
    onward = (parts[2].astype(f32) + got[1].astype(f32)).astype(parts.dtype)
    far = swap(onward, 2, 0)
    return parts[0].astype(f32) + got[0].astype(f32) + far.astype(f32)


def ring_gather(value):
    pieces = []
    for k in range(lax.axis_size("blk") // 2):
        value = ring_step(value) if k else value
        pieces += [value, swap(value, 0, 1)]
    return pieces


def reduce_pieces(evens, odds, wait):
    half = len(evens)
    total, sent = None, []
    for g, stack in enumerate(odds):
        got = swap(stack, 0, 1)
        for i in range(stack.shape[0]):
            zr = half - 1 - (g * (half // 2) + i)
            here = evens[zr].astype(f32) + got[i].astype(f32)
            if zr:
                sent.append(tie(here.astype(bf16), wait))
                here = swap(sent[-1], 0, 2 * zr).astype(f32)
            total = here if total is None else total + here
    return total, sent


def gather_few(value):
    column = [value] + [swap(value, 0, r) for r in range(2, lax.axis_size("blk"), 2)]
    beside = swap(jnp.stack(column), 0, 1)
    pieces = []
    for k, piece in enumerate(column):
        pieces += [piece, beside[k]]
    return pieces


def blk_gather(value):
    blocks = lax.axis_size("blk")
    if blocks > 8:
        whole = lax.all_gather(value, "blk", axis=0, tiled=False)
        return jnp.take(whole, lax.axis_index("blk") ^ jnp.arange(blocks), axis=0)
    pieces = [None] * blocks
    for r in range(0, blocks, 2):
        piece = swap(value, 0, r) if r else value
        pieces[r] = piece
        pieces[r + 1] = swap(piece, 0, 1)
    return jnp.stack(pieces)


def blk_reduce(parts):
    blocks = lax.axis_size("blk")
    if blocks > 8:
        whole = jnp.take(parts, lax.axis_index("blk") ^ jnp.arange(blocks), axis=0)
        return lax.psum_scatter(whole, "blk", scatter_dimension=0, tiled=False).astype(f32)
    total = None
    for r in range(blocks - 2, -1, -2):
        got = swap(parts[r + 1], 0, 1)
        here = parts[r].astype(f32) + got.astype(f32)
        if r:
            here = swap(here.astype(parts.dtype), 0, r).astype(f32)
        total = here if total is None else total + here
    return total


def blk_gather_few(value):
    blocks = lax.axis_size("blk")
    if blocks > 8:
        return blk_gather(value)
    column = jnp.stack([value] + [swap(value, 0, r) for r in range(2, blocks, 2)])
    both = jnp.stack([column, swap(column, 0, 1)], axis=1)
    return both.reshape((blocks,) + value.shape)


def reduce_few(parts, direct, *waits):
    if not direct:
        return lax.psum_scatter(parts, "blk", scatter_dimension=0, tiled=False).astype(f32), parts
    got = swap(parts[1], 0, 1)
    here = parts[0].astype(f32) + got.astype(f32)
    sent = here.astype(parts.dtype)
    if waits:
        sent = tie(sent, *waits)
    total = here[0]
    for k in range(1, parts.shape[1]):
        total = total + swap(sent[k], 0, 2 * k).astype(f32)
    return total, sent


def blk_unshuffle(pieces):
    blocks = pieces.shape[0]
    b = lax.axis_index("blk")
    return jnp.stack(
        [lax.dynamic_index_in_dim(pieces, b ^ i, 0, keepdims=False) for i in range(blocks)]
    )


RING = {0: 1, 1: 3, 3: 2, 2: 0}


def ring_step(value):
    count, blocks = lax.axis_size("heads"), lax.axis_size("blk")
    pairs = []
    for i in range(count * blocks):
        h, b = divmod(i, blocks)
        pairs.append((i, h * blocks + RING[b // 2] * 2 + b % 2))
    return lax.ppermute(value, BOTH, pairs)


def ring_place(z):
    return z ^ (z >> 1)


def ring_owner(z, k):
    place = (ring_place(z) - k) & 3
    return place ^ (place >> 1)


def z_groups(blocks):
    return [[i for i in range(blocks) if i % 2 == y] for y in range(2)]


def expand_heads(transposed, dtype):
    rows = []
    n = transposed.shape[1]
    zero = jnp.zeros((HEAD_WIDTH, n), dtype)
    for g in range(KV_LOCAL):
        columns = []
        for head in range(Q_LOCAL):
            if head // GROUP == g:
                columns.append(transposed[head * HEAD_WIDTH : (head + 1) * HEAD_WIDTH].astype(dtype))
            else:
                columns.append(zero)
        rows.append(jnp.concatenate(columns, axis=1))
    return jnp.concatenate(rows, axis=0)


def collapse_heads(wide, n):
    pieces = []
    for head in range(Q_LOCAL):
        g = head // GROUP
        pieces.append(wide[g * HEAD_WIDTH : (g + 1) * HEAD_WIDTH, head * n : (head + 1) * n])
    return jnp.concatenate(pieces, axis=0)


def key_rows(kv_ref, r, j, low, high):
    return jnp.concatenate(
        [kv_ref[r, j, :, low:high], kv_ref[r + 1, j, :, low:high]], axis=0
    )


def step_place(t, h, b, blocks, tok_dev, direct):
    half = blocks // 2
    owner_h = t // half
    owner_z = t % half
    j = owner_h ^ h
    z, y = b // 2, b % 2
    term = (owner_z ^ z) * 2
    if direct:
        piece = ((ring_place(z) - ring_place(owner_z)) & 3) * 2
    else:
        piece = term
    row = lax.broadcasted_iota(jnp.int32, (2 * tok_dev, 1), 0)
    base = (owner_h * blocks + owner_z * 2) * tok_dev
    second = row >= tok_dev
    position = base + jnp.where(
        second, row - tok_dev + (1 - y) * tok_dev, row + y * tok_dev
    )
    return piece, term, j, position


def fill_pieces(refs, whole_ref):
    for r, ref in enumerate(refs):
        whole_ref[r] = ref[...]


def attend_kernel(blocks, count, *refs):
    scal_ref, q_ref, start_ref = refs[:3]
    pieces = refs[3 : 3 + count]
    att_ref, lse_ref, top_ref, sum_ref, acc_ref = refs[3 + count : 8 + count]
    if count > 1:
        kv_ref = refs[8 + count]
        fill_pieces(pieces, kv_ref)
    else:
        kv_ref = pieces[0]
    tok_dev = q_ref.shape[1]
    h, b = scal_ref[0], scal_ref[1]

    def one(j, unused):
        block = (h ^ j) * blocks + b
        queries = (q_ref[j].astype(f32) * 0.125).T
        wide = expand_heads(queries, bf16)
        lane = lax.broadcasted_iota(jnp.int32, (1, tok_dev), 1)
        query_pos = jnp.concatenate([block * tok_dev + lane] * Q_LOCAL, axis=1)
        start = jnp.concatenate([start_ref[j]] * Q_LOCAL, axis=1)
        top_ref[...] = jnp.full(top_ref.shape, masked_score, f32)
        sum_ref[...] = jnp.zeros(sum_ref.shape, f32)
        acc_ref[...] = jnp.zeros(acc_ref.shape, f32)

        def step(t, unused):
            r, unused_term, jk, position = step_place(t, h, b, blocks, tok_dev, count > 1)
            keys = key_rows(kv_ref, r, jk, 0, K_COLS)
            values = key_rows(kv_ref, r, jk, K_COLS, 2 * K_COLS)
            scores = lax.dot_general(keys, wide, (((1,), (0,)), ((), ())), preferred_element_type=f32)
            allowed = (position >= start) & (position <= query_pos)
            scores = jnp.where(allowed, scores, masked_score)
            old = top_ref[...]
            new = jnp.maximum(old, jnp.max(scores, axis=0, keepdims=True))
            rescale = jnp.exp(old - new)
            weights = jnp.exp(scores - new)
            top_ref[...] = new
            sum_ref[...] = sum_ref[...] * rescale + jnp.sum(weights, axis=0, keepdims=True)
            acc_ref[...] = acc_ref[...] * rescale + lax.dot_general(
                values, weights.astype(bf16), (((0,), (0,)), ((), ())), preferred_element_type=f32
            )
            return unused

        lax.fori_loop(scal_ref[2 + j], block // 2 + 1, step, 0)
        total = sum_ref[...]
        out = collapse_heads(acc_ref[...] / total, tok_dev)
        att_ref[j] = out.T.astype(bf16)
        lse_ref[j] = top_ref[...] + jnp.log(total)
        return unused

    lax.fori_loop(0, HEADS, one, 0)


SMEM = pl.BlockSpec(memory_space=pltpu.SMEM)
VMEM = pl.BlockSpec(memory_space=pltpu.VMEM)
ANY = pl.BlockSpec(memory_space=pl.ANY)


def room_for(arrays, scratch):
    held = sum(a.size * a.dtype.itemsize for a in arrays)
    for s in scratch:
        size = 1
        for n in s.shape:
            size *= n
        held += size * jnp.dtype(s.dtype).itemsize
    return min(VMEM_LIMIT, held + held // 8 + (14 << 20))


def shaped(shape, dtype):
    return jax.ShapeDtypeStruct(shape, dtype)


def call(kernel, name, outs, scalars, arrays, scratch=(), waits=(), cost=4):
    scalars, arrays, waits = list(scalars), list(arrays), list(waits)
    used = len(scalars) + len(arrays)

    def body(*refs):
        kernel(*(refs[:used] + refs[used + len(waits) :]))

    return pl.pallas_call(
        body,
        out_shape=tuple(outs),
        in_specs=[SMEM] * len(scalars) + [VMEM] * len(arrays) + [ANY] * len(waits),
        out_specs=tuple([VMEM] * len(outs)),
        scratch_shapes=list(scratch),
        compiler_params=pltpu.CompilerParams(
            vmem_limit_bytes=room_for(arrays + list(outs), scratch)
        ),
        cost_estimate=pl.CostEstimate(flops=cost * 1000000000, bytes_accessed=1 << 20, transcendentals=0),
        name=name,
    )(*scalars, *arrays, *waits)


def tie(value, *waits):
    def body(*refs):
        pass

    return pl.pallas_call(
        body,
        out_shape=shaped(value.shape, value.dtype),
        in_specs=[ANY] * (1 + len(waits)),
        out_specs=ANY,
        input_output_aliases={0: 0},
        name="tie",
    )(value, *waits)


def attend(scal, queries, kv, start, blocks, waits=()):
    tok_dev = queries.shape[1]
    wide = Q_LOCAL * tok_dev
    scratch = [
        pltpu.VMEM((1, wide), f32),
        pltpu.VMEM((1, wide), f32),
        pltpu.VMEM((K_COLS, wide), f32),
    ]
    if len(kv) > 1:
        scratch.append(pltpu.VMEM((blocks,) + kv[0].shape, bf16))
    return call(
        functools.partial(attend_kernel, blocks, len(kv)),
        "attend",
        (
            shaped((HEADS, tok_dev, Q_COLS), bf16),
            shaped((HEADS, 1, wide), f32),
        ),
        [scal],
        [queries, start] + list(kv),
        scratch,
        waits=waits,
        cost=12,
    )


def attend_back_kernel(blocks, count, *refs):
    scal_ref, q_ref, start_ref, att_ref, lse_ref, wo_ref = refs[:6]
    branch = refs[6:10]
    pieces = refs[10 : 10 + count]
    dq_ref = refs[10 + count]
    n_outs = count // 2 + 2 if count > 1 else 1
    outs = refs[11 + count : 11 + count + n_outs]
    acc_ref, term_ref, grad_ref = refs[11 + count + n_outs : 14 + count + n_outs]
    if count > 1:
        kv_ref = refs[14 + count + n_outs]
        fill_pieces(pieces, kv_ref)
    else:
        kv_ref = pieces[0]
    tok_dev = q_ref.shape[1]
    h, b = scal_ref[0], scal_ref[1]
    term_ref[...] = jnp.zeros(term_ref.shape, f32)
    for j in range(HEADS):
        grad_ref[j] = dot_nt(branch[j][...], wo_ref[...]).astype(bf16)

    def one(j, unused):
        block = (h ^ j) * blocks + b
        wide = expand_heads((q_ref[j].astype(f32) * 0.125).T, bf16)
        grad_t = grad_ref[j].astype(f32).T
        wide_grad = expand_heads(grad_t, bf16)
        product = grad_t * att_ref[j].astype(f32).T
        delta = jnp.concatenate(
            [
                jnp.sum(product[head * HEAD_WIDTH : (head + 1) * HEAD_WIDTH], axis=0, keepdims=True)
                for head in range(Q_LOCAL)
            ],
            axis=1,
        )
        lse = lse_ref[j]
        lane = lax.broadcasted_iota(jnp.int32, (1, tok_dev), 1)
        query_pos = jnp.concatenate([block * tok_dev + lane] * Q_LOCAL, axis=1)
        start = jnp.concatenate([start_ref[j]] * Q_LOCAL, axis=1)
        acc_ref[...] = jnp.zeros(acc_ref.shape, f32)

        def step(t, unused):
            r, rt, jk, position = step_place(t, h, b, blocks, tok_dev, count > 1)
            keys = key_rows(kv_ref, r, jk, 0, K_COLS)
            values = key_rows(kv_ref, r, jk, K_COLS, 2 * K_COLS)
            scores = lax.dot_general(keys, wide, (((1,), (0,)), ((), ())), preferred_element_type=f32)
            allowed = (position >= start) & (position <= query_pos)
            probs = jnp.exp(jnp.where(allowed, scores - lse, masked_score))
            grad_probs = lax.dot_general(
                values, wide_grad, (((1,), (0,)), ((), ())), preferred_element_type=f32
            )
            grad_scores = (probs * (grad_probs - delta)).astype(bf16)
            acc_ref[...] += lax.dot_general(
                keys, grad_scores, (((0,), (0,)), ((), ())), preferred_element_type=f32
            )
            key_term = lax.dot_general(
                grad_scores, wide, (((1,), (1,)), ((), ())), preferred_element_type=f32
            )
            value_term = lax.dot_general(
                probs.astype(bf16), wide_grad, (((1,), (1,)), ((), ())), preferred_element_type=f32
            )
            both = jnp.concatenate([key_term, value_term], axis=1)
            term_ref[rt, jk] += both[:tok_dev]
            term_ref[rt + 1, jk] += both[tok_dev:]
            return unused

        lax.fori_loop(scal_ref[2 + j], block // 2 + 1, step, 0)
        dq_ref[j] = (collapse_heads(acc_ref[...], tok_dev) * 0.125).T.astype(bf16)
        return unused

    lax.fori_loop(0, HEADS, one, 0)
    if count > 1:
        half = count // 2
        for zr in range(half):
            outs[zr][...] = term_ref[2 * zr].astype(bf16)
            back = half - 1 - zr
            outs[half + back // (half // 2)][back % (half // 2)] = term_ref[2 * zr + 1].astype(bf16)
    else:
        outs[0][...] = term_ref[...].astype(bf16)


def attend_back(scal, queries, kv, start, att, lse, output_w, branch, blocks, waits=()):
    tok_dev = queries.shape[1]
    wide = Q_LOCAL * tok_dev
    whole = (blocks, HEADS, tok_dev, 2 * K_COLS)
    scratch = [
        pltpu.VMEM((K_COLS, wide), f32),
        pltpu.VMEM(whole, f32),
        pltpu.VMEM((HEADS, tok_dev, Q_COLS), bf16),
    ]
    terms = [shaped(whole, bf16)]
    if len(kv) > 1:
        scratch.append(pltpu.VMEM(whole, bf16))
        half = blocks // 2
        terms = [shaped(whole[1:], bf16)] * half + [shaped((half // 2,) + whole[1:], bf16)] * 2
    outs = call(
        functools.partial(attend_back_kernel, blocks, len(kv)),
        "attend_back",
        [shaped((HEADS, tok_dev, Q_COLS), bf16)] + terms,
        [scal],
        [queries, start, att, lse, output_w] + list(branch) + list(kv),
        scratch,
        waits=waits,
        cost=17,
    )
    return outs[0], outs[1:]


def dot(a, b):
    return jnp.dot(a, b, preferred_element_type=f32)


def dot_tn(a, b):
    return lax.dot_general(a, b, (((0,), (0,)), ((), ())), preferred_element_type=f32)


def dot_nt(a, b):
    return lax.dot_general(a, b, (((1,), (1,)), ((), ())), preferred_element_type=f32)


def split(value, count):
    terms = []
    for unused in range(count):
        term = value.astype(bf16)
        terms.append(term)
        value = value - term.astype(f32)
    return terms


def own_rows(b, r, source, wrows, blocks):
    return pl.ds(pl.multiple_of((source * blocks + (b ^ r)) * wrows, 16), wrows)


def project_kernel(blocks, count, *refs):
    scal_ref, gain_ref = refs[:2]
    tokens = refs[2:6]
    pieces = refs[6 : 6 + count]
    normed_ref, q_ref, kv_ref = refs[6 + count : 9 + count]
    w_ref = refs[9 + count] if count > 1 else pieces[0]
    b = scal_ref[1]
    if count > 1:
        wrows = pieces[0].shape[1]
        for r in range(count):
            for source in range(HEADS):
                owner = ring_owner(b // 2, r // 2) * 2 + (b % 2 ^ r % 2)
                low = pl.multiple_of((source * blocks + owner) * wrows, 16)
                w_ref[pl.ds(low, wrows), :] = pieces[r][source]
    tok_dev = tokens[0].shape[0]
    for j in range(HEADS):
        value = tokens[j][...].astype(f32)
        inverse = lax.rsqrt(jnp.mean(value * value, axis=-1, keepdims=True) + epsilon_norm)
        normed_ref[j * tok_dev : (j + 1) * tok_dev, :] = (value * inverse * gain_ref[...]).astype(bf16)
    projected = dot(normed_ref[...], w_ref[...]).astype(bf16)
    for j in range(HEADS):
        q_ref[j] = projected[j * tok_dev : (j + 1) * tok_dev, :Q_COLS]
        kv_ref[j] = projected[j * tok_dev : (j + 1) * tok_dev, Q_COLS:]


def project(scal, gain, tokens, pieces, blocks, waits=()):
    tok_dev, model = tokens[0].shape
    outs = [
        shaped((HEADS * tok_dev, model), bf16),
        shaped((HEADS, tok_dev, Q_COLS), bf16),
        shaped((HEADS, tok_dev, 2 * K_COLS), bf16),
    ]
    if len(pieces) > 1:
        outs.append(shaped((model, Q_COLS + 2 * K_COLS), bf16))
    got = call(
        functools.partial(project_kernel, blocks, len(pieces)),
        "project",
        outs,
        [scal],
        [gain] + list(tokens) + list(pieces),
        waits=waits,
    )
    return got[:3] + (got[3] if len(pieces) > 1 else pieces[0],)


def output_kernel(blocks, count, *refs):
    scal_ref, att_ref = refs[:2]
    pieces = refs[2 : 2 + count]
    keep_ref, send_ref = refs[2 + count : 4 + count]
    wo_ref = refs[4 + count] if count > 1 else pieces[0]
    b = scal_ref[1]
    if count > 1:
        wrows = pieces[0].shape[0]
        for r in range(count):
            wo_ref[own_rows(b, r, 0, wrows, blocks), :] = pieces[r][...]
    for j in range(HEADS):
        part = dot(att_ref[j], wo_ref[...]).astype(bf16)
        if j % 2:
            send_ref[j // 2] = part
        else:
            keep_ref[j // 2] = part


def output_parts(scal, att, pieces, model, blocks, waits):
    tok_dev = att.shape[1]
    outs = [shaped((2, tok_dev, model), bf16)] * 2
    if len(pieces) > 1:
        outs.append(shaped((Q_COLS, model), bf16))
    got = call(
        functools.partial(output_kernel, blocks, len(pieces)),
        "output_parts",
        outs,
        [scal],
        [att] + list(pieces),
        waits=waits,
    )
    return got[0], got[1], (got[2] if len(pieces) > 1 else pieces[0])


def heads_sum(keep, send):
    got = swap(send, 1, 0)
    onward = (keep[1].astype(f32) + got[1].astype(f32)).astype(bf16)
    return got, swap(onward, 2, 0)


def route_kernel(
    scal_ref, keep_ref, got_ref, far_ref, tokens_ref, gain_ref, router_ref, member_ref, table_ref, cot_ref,
    s0, s1, s2, s3, g0, g1, g2, g3, hidden_ref, nf_ref, gates_ref, slot_gate_ref, sent_ref, back_ref,
):
    hidden = (
        tokens_ref[...].astype(f32)
        + keep_ref[0].astype(f32)
        + got_ref[0].astype(f32)
        + far_ref[...].astype(f32)
    )
    hidden_ref[...] = hidden
    inverse = lax.rsqrt(jnp.mean(hidden * hidden, axis=-1, keepdims=True) + epsilon_norm)
    nf = (hidden * inverse * gain_ref[...]).astype(bf16)
    nf_ref[...] = nf
    logits = dot_nt(nf, router_ref[...])
    picked = member_ref[...] > 0
    peak = jnp.max(jnp.where(picked, logits, -jnp.inf), axis=-1, keepdims=True)
    raised = jnp.where(picked, jnp.exp(jnp.where(picked, logits - peak, 0.0)), 0.0)
    gates = raised / jnp.sum(raised, axis=-1, keepdims=True)
    gates_ref[...] = gates
    table = table_ref[...]
    sent = dot(table, nf).astype(bf16)
    spread = dot(table, cot_ref[...])
    slot_gates = sum(dot(table, term) for term in split(gates, 3))
    lane = lax.broadcasted_iota(jnp.int32, (CAP, slot_gates.shape[1]), 1)
    sent_ref[...] = sent
    for e in range(4):
        rows = slice(e * CAP, (e + 1) * CAP)
        column = jnp.sum(jnp.where(lane == e, slot_gates[rows], 0.0), axis=1, keepdims=True)
        slot_gate_ref[rows, :] = column
        back_ref[rows, :] = (spread[rows] * column).astype(bf16)
    for r, (s_ref, g_ref) in enumerate(((s0, g0), (s1, g1), (s2, g2), (s3, g3))):
        rows = slot_rows(own_place(scal_ref) ^ r)
        s_ref[...] = sent_ref[rows, :]
        g_ref[...] = back_ref[rows, :]


def gate_up(ref, drows):
    return jnp.concatenate(
        [ref[:, k * drows : (k + 1) * drows, :].reshape(-1, LANES) for k in range(4)], axis=1
    )


def down_half(ref, drows, frows):
    base = 4 * drows
    return jnp.concatenate(
        [ref[:, base + k * frows : base + (k + 1) * frows, :].reshape(-1, LANES) for k in range(3)],
        axis=1,
    )


def lanes(offset, size):
    return pl.ds(pl.multiple_of(offset, 128), size)


def fill_weights(scal_ref, refs, mine_ref, other_ref):
    z = scal_ref[1] // 2
    for pieces, whole_ref in ((refs[:4], mine_ref), (refs[4:], other_ref)):
        for k in range(4):
            for y in range(2):
                whole_ref[ring_owner(z, k) * 2 + y] = pieces[k][y]


def expert_kernel(drows, frows, direct, *refs):
    scal_ref = refs[0]
    if direct:
        p0, p1, p2, p3, gp_ref, up_ref, inner_ref, out_ref, mine_ref, other_ref = refs[13:]
        fill_weights(scal_ref, refs[5:13], mine_ref, other_ref)
    else:
        mine_ref, other_ref, p0, p1, p2, p3, gp_ref, up_ref, inner_ref, out_ref = refs[5:]
    fill_rows(scal_ref, refs[1:5], out_ref)
    core = scal_ref[0] % 2
    rows = out_ref[...]
    for side, ref in ((core, mine_ref), (1 - core, other_ref)):
        both = dot(rows, gate_up(ref, drows))
        gate, up = both[:, : 2 * LANES], both[:, 2 * LANES :]
        place = lanes(side * 2 * LANES, 2 * LANES)
        gp_ref[:, place] = gate
        up_ref[:, place] = up
        inner_ref[:, place] = (gate * jax.nn.sigmoid(gate) * up).astype(bf16)
    inner = inner_ref[...]
    for side, ref in ((core, mine_ref), (1 - core, other_ref)):
        out_ref[:, lanes(side * 3 * LANES, 3 * LANES)] = dot(inner, down_half(ref, drows, frows)).astype(bf16)
    for r, ref in enumerate((p0, p1, p2, p3)):
        ref[...] = out_ref[slot_rows(own_place(scal_ref) ^ r), :]


def own_place(scal_ref):
    return scal_ref[0] // 2 * 2 + scal_ref[1] % 2


def slot_rows(place):
    return pl.ds(pl.multiple_of(place * CAP, 16), CAP)


def fill_rows(scal_ref, refs, rows_ref):
    for r, ref in enumerate(refs):
        rows_ref[slot_rows(own_place(scal_ref) ^ r), :] = ref[...]


def expert_back_kernel(drows, frows, direct, *refs):
    scal_ref = refs[0]
    gp_ref, up_ref = refs[5:7]
    if direct:
        p0, p1, p2, p3, ggp_ref, gup_ref, grad_ref, mine_ref, other_ref = refs[15:]
        fill_weights(scal_ref, refs[7:15], mine_ref, other_ref)
    else:
        mine_ref, other_ref, p0, p1, p2, p3, ggp_ref, gup_ref, grad_ref = refs[7:]
    core = scal_ref[0] % 2
    fill_rows(scal_ref, refs[1:5], grad_ref)
    grad_inner = None
    for side, ref in ((core, mine_ref), (1 - core, other_ref)):
        term = dot_nt(grad_ref[:, lanes(side * 3 * LANES, 3 * LANES)], down_half(ref, drows, frows))
        grad_inner = term if grad_inner is None else grad_inner + term
    gate, up = gp_ref[...], up_ref[...]
    sig = jax.nn.sigmoid(gate)
    ggp_ref[...] = (grad_inner * up * sig * (1.0 + gate * (1.0 - sig))).astype(bf16)
    gup_ref[...] = (grad_inner * gate * sig).astype(bf16)
    total = None
    for side, ref in ((core, mine_ref), (1 - core, other_ref)):
        place = lanes(side * 2 * LANES, 2 * LANES)
        both = jnp.concatenate([ggp_ref[:, place], gup_ref[:, place]], axis=1)
        term = dot_nt(both, gate_up(ref, drows))
        total = term if total is None else total + term
    grad_ref[...] = total.astype(bf16)
    for r, ref in enumerate((p0, p1, p2, p3)):
        ref[...] = grad_ref[slot_rows(own_place(scal_ref) ^ r), :]


def expert_weights_kernel(
    drows, frows, blocks, own, scal_ref, x0, x1, x2, x3, g0, g1, g2, g3, inner_ref, ggp_ref, gup_ref, *rest
):
    if own:
        got_ref, out_ref, grad_ref, rows_ref = rest
    else:
        out_ref, grad_ref, rows_ref = rest
    core, z = scal_ref[0] % 2, scal_ref[1] // 2
    side = core if own else 1 - core
    fill_rows(scal_ref, (g0, g1, g2, g3), grad_ref)
    fill_rows(scal_ref, (x0, x1, x2, x3), rows_ref)
    rows = rows_ref[...]

    def put(low, height, term):
        for k in range(term.shape[1] // LANES):
            piece = term[:, k * LANES : (k + 1) * LANES].reshape(blocks // 2, 2, height, LANES)
            place = slice(low, low + height)
            for at in range(blocks // 2):
                step = (ring_place(at) - ring_place(z)) & 3 if blocks == 8 else at
                value = piece[at]
                if own:
                    value = value + got_ref[step, :, place, :].astype(f32)
                out_ref[step, :, place, :] = value.astype(bf16)
            low += height

    place = lanes(side * 2 * LANES, 2 * LANES)
    both = jnp.concatenate([ggp_ref[:, place], gup_ref[:, place]], axis=1)
    put(0, drows, dot_tn(rows, both))
    put(4 * drows, frows, dot_tn(inner_ref[...], grad_ref[:, lanes(side * 3 * LANES, 3 * LANES)]))


def combine_kernel(
    scal_ref, r0, r1, r2, r3, hidden_ref, nf_ref, gates_ref, slot_gate_ref, table_ref, cot_ref, router_ref,
    mixed_ref, grad_nf_ref, router_grad_ref, ret_ref,
):
    table = table_ref[...]
    fill_rows(scal_ref, (r0, r1, r2, r3), ret_ref)
    returned = ret_ref[...]
    scaled_rows = returned.astype(f32) * slot_gate_ref[...]
    mixed_ref[...] = (hidden_ref[...] + sum(dot_tn(table, t) for t in split(scaled_rows, 2))).astype(bf16)
    scored = dot_nt(returned, cot_ref[...]) * table.astype(f32)
    gates_t = gates_ref[...].T[:8]
    score_rows = [
        jnp.sum(scored[e * CAP : (e + 1) * CAP], axis=0, keepdims=True) for e in range(4)
    ]
    scores = jnp.concatenate(score_rows + [jnp.zeros((4, scored.shape[1]), f32)], axis=0)
    mean_gate = jnp.sum(gates_t * scores, axis=0, keepdims=True)
    grad_logits = gates_t * (scores - mean_gate)
    terms = split(grad_logits, 3)
    router_grad_ref[...] = sum(dot(t, nf_ref[...]) for t in terms)
    grad_nf_ref[...] = sum(dot_tn(t, router_ref[:8, :]) for t in terms)


def norm_back_kernel(
    scal_ref, b0, b1, b2, b3, hidden_ref, table_ref, cot_ref, gain_ref, part_ref,
    grad_hidden_ref, branch_ref, gain_grad_ref, back_ref,
):
    hidden = hidden_ref[...]
    fill_rows(scal_ref, (b0, b1, b2, b3), back_ref)
    grad_nf = dot_tn(table_ref[...], back_ref[...]) + part_ref[...]
    inverse = lax.rsqrt(jnp.mean(hidden * hidden, axis=-1, keepdims=True) + epsilon_norm)
    gain_grad_ref[...] = jnp.sum(grad_nf * hidden * inverse, axis=0, keepdims=True)
    scaled = grad_nf * gain_ref[...]
    grad_hidden = (
        cot_ref[...].astype(f32)
        + inverse * scaled
        - hidden * (inverse * inverse * inverse) * jnp.mean(scaled * hidden, axis=-1, keepdims=True)
    )
    grad_hidden_ref[...] = grad_hidden
    branch_ref[...] = grad_hidden.astype(bf16)


def late_grad_kernel(blocks, wrows, direct, scal_ref, normed_ref, dq_ref, att_ref, b0, b1, b2, b3, out_ref, q_ref, o_ref):
    b = scal_ref[1]
    flat = jnp.concatenate([dq_ref[j] for j in range(HEADS)], axis=0)
    q_ref[...] = dot_tn(normed_ref[...], flat).astype(bf16)
    total = None
    for j, ref in enumerate((b0, b1, b2, b3)):
        term = dot_tn(att_ref[j], ref[...])
        total = term if total is None else total + term
    o_ref[...] = total.astype(bf16)
    for r in range(blocks):
        for source in range(HEADS):
            cols = slice(source * Q_COLS, (source + 1) * Q_COLS)
            if direct:
                out_ref[r % 2, r // 2, :wrows, cols] = q_ref[own_rows(b, r, source, wrows, blocks), :]
            else:
                low = (source * blocks + r) * wrows
                out_ref[r, :wrows, cols] = q_ref[low : low + wrows, :]
        if direct:
            out_ref[r % 2, r // 2, wrows:, :] = o_ref[own_rows(b, r, 0, wrows, blocks), :]
        else:
            out_ref[r, wrows:, :] = o_ref[r * wrows : (r + 1) * wrows, :]


def pair_shape(blocks, rest, direct):
    return ((2, blocks // 2) if direct else (blocks,)) + rest


def column_grad_kernel(blocks, wrows, direct, scal_ref, normed_ref, grad_ref, out_ref, hold_ref):
    b = scal_ref[1]
    flat = jnp.concatenate([grad_ref[j] for j in range(HEADS)], axis=0)
    hold_ref[...] = dot_tn(normed_ref[...], flat).astype(bf16)
    for r in range(blocks):
        for source in range(HEADS):
            if direct:
                out_ref[r % 2, r // 2, source] = hold_ref[own_rows(b, r, source, wrows, blocks), :]
            else:
                low = (source * blocks + r) * wrows
                out_ref[r, source] = hold_ref[low : low + wrows, :]


def normed_back_kernel(dq_ref, dkv_ref, w_ref, t0, t1, t2, t3, keep_ref, send_ref, gain_grad_ref):
    total = None
    for j, ref in enumerate((t0, t1, t2, t3)):
        part = dot_nt(dq_ref[j], w_ref[:, :Q_COLS]) + dot_nt(dkv_ref[j], w_ref[:, Q_COLS:])
        value = ref[...].astype(f32)
        inverse = lax.rsqrt(jnp.mean(value * value, axis=-1, keepdims=True) + epsilon_norm)
        term = jnp.sum(part * (value * inverse), axis=0, keepdims=True)
        total = term if total is None else total + term
        if j % 2:
            send_ref[j // 2] = part.astype(bf16)
        else:
            keep_ref[j // 2] = part.astype(bf16)
    gain_grad_ref[...] = total


def tokens_back_kernel(keep_ref, got_ref, far_ref, tokens_ref, gain_ref, grad_hidden_ref, out_ref):
    grad_normed = keep_ref[0].astype(f32) + got_ref[0].astype(f32) + far_ref[...].astype(f32)
    value = tokens_ref[...].astype(f32)
    inverse = lax.rsqrt(jnp.mean(value * value, axis=-1, keepdims=True) + epsilon_norm)
    scaled = grad_normed * gain_ref[...]
    out_ref[...] = (
        grad_hidden_ref[...]
        + inverse * scaled
        - value * (inverse * inverse * inverse) * jnp.mean(scaled * value, axis=-1, keepdims=True)
    ).astype(bf16)


def small_share(values, wait):
    devices = lax.axis_size("heads") * lax.axis_size("blk")
    n, width = values.shape
    padded = tie(jnp.pad(values, ((0, 8 - n), (0, 128 - width))), wait)
    got = lax.all_to_all(
        jnp.broadcast_to(padded[None], (devices, 8, 128)), BOTH, 0, 0, tiled=True
    )
    return jnp.transpose(got[:, :n, :width], (1, 0, 2)).reshape(n, devices * width)


def small_sum(values, wait):
    devices = lax.axis_size("heads") * lax.axis_size("blk")
    n = values.shape[0]
    width = values.shape[1] // devices
    parts = jnp.transpose(values.reshape(n, devices, width), (1, 0, 2))
    padded = jnp.pad(parts, ((0, 0), (0, 8 - n), (0, 128 - width)))
    got = lax.all_to_all(tie(padded, wait), BOTH, 0, 0, tiled=True)
    return jnp.sum(got, axis=0)[:n, :width]


def halves(columns, core):
    half = columns.shape[1] // 2
    first, second = columns[:, :half], columns[:, half:]
    return jnp.where(core == 0, first, second), jnp.where(core == 0, second, first)


def unhalve(own, other, core):
    return jnp.concatenate(
        [jnp.where(core == 0, own, other), jnp.where(core == 0, other, own)], axis=1
    )


def unpack_half(buffer, drows, frows):
    def piece(low, high):
        return buffer[:, low:high].reshape(-1, LANES)

    matrices, base = [], 0
    for rows, count in ((drows, 2), (drows, 2), (frows, 3)):
        matrices.append(
            jnp.concatenate([piece(base + k * rows, base + (k + 1) * rows) for k in range(count)], axis=1)
        )
        base += rows * count
    return matrices


def pack_half(gate, up, down, count):
    pieces = []
    for matrix in (gate, up, down):
        rows = matrix.shape[0] // count
        for k in range(matrix.shape[1] // LANES):
            pieces.append(matrix[:, k * LANES : (k + 1) * LANES].reshape(count, rows, LANES))
    return jnp.concatenate(pieces, axis=1)


def shards(
    tokens,
    cotangent,
    routes,
    doc_lengths,
    attn_norm,
    w_query,
    key_weight,
    value_weight,
    w_output,
    ffn_norm,
    w_router,
    w_gate,
    w_up,
    w_down,
):
    blocks = lax.axis_size("blk")
    direct = blocks <= 8
    tok_dev, model = tokens.shape
    wrows = w_query.shape[0]
    drows = w_gate.shape[1]
    frows = w_down.shape[1]
    experts = w_router.shape[1]
    h, b = lax.axis_index("heads"), lax.axis_index("blk")
    core, x, y = h % 2, h // 2, b % 2
    zn = blocks // 2
    wide_cols = Q_COLS + 2 * K_COLS

    w_out = w_output.astype(bf16)
    if direct:
        wo_pieces = gather_few(w_out)
    else:
        wo_pieces = [lax.all_gather(w_out, "blk", axis=0, tiled=True)]

    cut = [halves(m, core) for m in (w_gate[0].astype(bf16), w_up[0].astype(bf16), w_down[0].astype(bf16))]
    kept = pack_half(cut[0][0], cut[1][0], cut[2][0], 1)[0]
    given = pack_half(cut[0][1], cut[1][1], cut[2][1], 1)[0]
    at_home = core == y

    heads_cat = jnp.concatenate(
        [
            w_query.astype(bf16).reshape(wrows, HEADS, Q_COLS),
            key_weight.astype(bf16).reshape(wrows, HEADS, K_COLS),
            value_weight.astype(bf16).reshape(wrows, HEADS, K_COLS),
        ],
        axis=2,
    )
    small_own = jnp.concatenate(
        [attn_norm.astype(bf16)[None], ffn_norm.astype(bf16)[None], w_router.astype(bf16).T], axis=0
    )
    by_head = lax.all_to_all(tie(jnp.swapaxes(heads_cat, 0, 1), given), "heads", 0, 0, tiled=True)
    taken = swap(given, 1, 0)
    stay = jnp.where(at_home, kept, taken)
    leave = jnp.where(at_home, taken, kept)
    came = swap(leave, 0, 1)
    small = small_share(small_own, came)
    column = jnp.stack([jnp.where(y == 0, stay, came), jnp.where(y == 0, came, stay)])
    if direct:
        along_z = [wo_pieces[2], wo_pieces[4], wo_pieces[6]]
        w_pieces = ring_gather(tie(by_head, leave, *along_z))
        mine = [column, ring_step(tie(column, w_pieces[6]))]
    else:
        whole = lax.all_gather(by_head, "blk", axis=1, tiled=False)
        w_pieces = [whole.reshape(model, wide_cols)]
        mine = lax.all_gather(column, "blk", axis=0, tiled=False, axis_index_groups=z_groups(blocks))
        mine = mine.reshape((blocks,) + kept.shape)
    gain_one, gain_two = small[0:1].astype(f32), small[1:2].astype(f32)
    far = swap(tokens, 2, 0)
    all_tokens = [tokens, swap(tokens, 1, 0), far, swap(far, 1, 0)]

    ends = jnp.cumsum(doc_lengths)
    block_of = (h ^ jnp.arange(HEADS, dtype=jnp.int32)) * blocks + b
    query_pos = block_of[:, None] * tok_dev + jnp.arange(tok_dev, dtype=jnp.int32)[None, :]
    start = jnp.max(
        jnp.where(ends[None, None, :] <= query_pos[:, :, None], ends[None, None, :], 0), axis=2
    ).astype(jnp.int32)
    scal = jnp.concatenate(
        [
            jnp.stack([h, b]).astype(jnp.int32),
            start[:, 0] // (2 * tok_dev),
        ]
    )
    start = start[:, None, :]

    member = jnp.sum((routes[:, :, None] == jnp.arange(experts)[None, None, :]).astype(f32), axis=1)
    lower = (jnp.arange(tok_dev)[:, None] > jnp.arange(tok_dev)[None, :]).astype(bf16)
    rank = dot(lower, member.astype(bf16))
    slot = jnp.arange(CAP, dtype=f32)
    table = (
        ((rank.T[:, None, :] == slot[None, :, None]) & (member.T[:, None, :] > 0))
        .astype(bf16)
        .reshape(experts * CAP, tok_dev)
    )
    member = jnp.pad(member, ((0, 0), (0, 128 - experts)))
    router_all = jnp.pad(small[2 : 2 + experts], ((0, 128 - experts), (0, 0)))

    normed, queries, kv_own, weights = project(
        scal, gain_one, all_tokens, w_pieces, blocks, [table, member, router_all, gain_two, start]
    )
    if direct:
        kv = ring_gather(kv_own)
        mine.append(ring_step(tie(mine[1], kv[6])))
        mine.append(ring_step(mine[2]))
    else:
        kv = [blk_gather(kv_own)]
    att, lse = attend(scal, queries, kv, start, blocks)
    keep, send, output_w = output_parts(scal, att, wo_pieces, model, blocks, [])
    got, far = heads_sum(keep, send)
    seconds = [swap(piece, 1, 0) for piece in mine[:3]] if direct else []
    slot = shaped((CAP, model), bf16)
    hold = pltpu.VMEM((experts * CAP, model), bf16)
    routed = call(
        route_kernel,
        "route",
        [slot] * 8
        + [
            shaped((tok_dev, model), f32),
            shaped((tok_dev, model), bf16),
            shaped((tok_dev, 128), f32),
            shaped((experts * CAP, 1), f32),
        ],
        [scal],
        [keep, got, far, tokens, gain_two, router_all, member, table, cotangent],
        [hold, hold],
        waits=seconds,
        cost=3,
    )
    sent, grad_sent = routed[:4], routed[4:8]
    hidden, normed_ffn, gates, slot_gate = routed[8:]

    def to_experts(pieces):
        return [pieces[0]] + [swap(pieces[r], r // 2 * 2, r % 2) for r in range(1, experts)]

    arrived = to_experts(sent)
    grad_arrived = to_experts(grad_sent)
    if direct:
        weights_in = mine + seconds + [swap(tie(mine[3], *arrived[1:]), 1, 0)]
        gathered = [pltpu.VMEM((blocks,) + kept.shape, bf16)] * 2
    else:
        mine = tie(mine, sent[0])
        other = swap(mine, 1, 0)
        weights_in, gathered = [mine, other], []
    rows_all = experts * CAP
    ff = frows * blocks
    fwd = call(
        functools.partial(expert_kernel, drows, frows, direct),
        "expert",
        [slot] * 4
        + [shaped((rows_all, ff), f32), shaped((rows_all, ff), f32), shaped((rows_all, ff), bf16)],
        [scal],
        arrived + weights_in,
        [hold] + gathered,
        cost=2,
    )
    gate_pre, up_pre, inner = fwd[4:7]
    returned = to_experts(fwd[:4])
    bwd = call(
        functools.partial(expert_back_kernel, drows, frows, direct),
        "expert_back",
        [slot] * 4
        + [shaped((rows_all, ff), bf16), shaped((rows_all, ff), bf16)],
        [scal],
        grad_arrived + [gate_pre, up_pre] + weights_in,
        [hold] + gathered,
        cost=2,
    )
    grad_returned = to_experts(bwd[:4])

    def expert_weights(own, extra, waits):
        return call(
            functools.partial(expert_weights_kernel, drows, frows, blocks, own),
            "expert_weights",
            [shaped((zn, 2) + kept.shape, bf16)],
            [scal],
            arrived + grad_arrived + [inner, bwd[4], bwd[5]] + extra,
            [hold, hold],
            waits=waits,
            cost=1,
        )[0]

    grads_other = expert_weights(False, [], returned[1:])
    grads_met = swap(grads_other, 1, 0)
    mixed, part_nf, router_grad = call(
        combine_kernel,
        "combine",
        [
            shaped((tok_dev, model), bf16),
            shaped((tok_dev, model), f32),
            shaped((8, model), f32),
        ],
        [scal],
        returned + [hidden, normed_ffn, gates, slot_gate, table, cotangent, router_all],
        [hold],
        waits=[grads_other],
        cost=1,
    )
    chip_grads = expert_weights(True, [grads_met], [mixed] + grad_returned[1:])
    if direct:
        running = ring_step(chip_grads[3])
    else:
        z_grads = lax.psum_scatter(
            chip_grads, "blk", scatter_dimension=0, tiled=False, axis_index_groups=z_groups(blocks)
        )
    grad_hidden, branch, gain_two_grad = call(
        norm_back_kernel,
        "norm_back",
        [
            shaped((tok_dev, model), f32),
            shaped((tok_dev, model), bf16),
            shaped((1, model), f32),
        ],
        [scal],
        grad_returned + [hidden, table, cotangent, gain_two, part_nf],
        [hold],
        waits=[chip_grads],
    )

    far_branch = swap(branch, 2, 0)
    branches = [branch, swap(branch, 1, 0), far_branch, swap(far_branch, 1, 0)]
    dq, dkv = attend_back(scal, queries, kv, start, att, lse, output_w, branches, blocks, [chip_grads])
    if direct:

        def met(k):
            return (running.astype(f32) + chip_grads[k].astype(f32)).astype(bf16)

        second_sum = met(2)
        running = ring_step(second_sum)
        third_sum = met(1)
        odds = [tie(stack, second_sum) for stack in dkv[zn:]]
        dkv_own, onward = reduce_pieces(dkv[:zn], odds, third_sum)
        running = ring_step(third_sum)
        z_grads = met(0)
    else:
        dkv_own, onward = blk_reduce(dkv[0]), [dq]
    dkv_own = dkv_own.astype(bf16)

    def column_grads(name, grad, waits=()):
        cols = grad.shape[2]
        return call(
            functools.partial(column_grad_kernel, blocks, wrows, direct),
            name,
            [shaped(pair_shape(blocks, (HEADS, wrows, cols), direct), bf16)],
            [scal],
            [normed, grad],
            [pltpu.VMEM((model, cols), bf16)],
            waits=waits,
        )[0]

    late_parts = call(
        functools.partial(late_grad_kernel, blocks, wrows, direct),
        "late_grad",
        [shaped(pair_shape(blocks, (2 * wrows, model), direct), bf16)],
        [scal],
        [normed, dq, att] + branches,
        [pltpu.VMEM((model, Q_COLS), bf16), pltpu.VMEM((Q_COLS, model), bf16)],
        waits=onward,
    )[0]
    late_sums, late_sent = reduce_few(late_parts, direct, dkv_own)
    grad_wout = late_sums[wrows:]
    sum_wq = jnp.swapaxes(late_sums[:wrows].reshape(wrows, HEADS, Q_COLS), 0, 1)
    keep, send, gain_one_grad = call(
        normed_back_kernel,
        "normed_back",
        [shaped((2, tok_dev, model), bf16)] * 2 + [shaped((1, model), f32)],
        [],
        [dq, dkv_own, weights] + all_tokens,
        waits=[],
        cost=6,
    )
    got, far = heads_sum(keep, send)
    kv_parts = column_grads("key_value_grad", dkv_own, [send])
    sum_wkv, kv_sent = reduce_few(kv_parts, direct, far)
    stay = jnp.where(y == 0, z_grads[0], z_grads[1])
    came = swap(jnp.where(y == 0, z_grads[1], z_grads[0]), 0, 1)
    kept_grad = jnp.where(at_home, stay, came)
    taken_grad = swap(jnp.where(at_home, came, stay), 1, 0)
    column_sums = jnp.concatenate([sum_wq.astype(bf16), sum_wkv.astype(bf16)], axis=2)
    by_row = lax.all_to_all(tie(column_sums, came), "heads", 0, 0, tiled=True)
    by_row = jnp.swapaxes(by_row, 0, 1).astype(f32)
    grad_wq = by_row[:, :, :Q_COLS].reshape(wrows, -1)
    grad_wk = by_row[:, :, Q_COLS : Q_COLS + K_COLS].reshape(wrows, -1)
    grad_wv = by_row[:, :, Q_COLS + K_COLS :].reshape(wrows, -1)
    grad_tokens = call(
        tokens_back_kernel,
        "tokens_back",
        [shaped((tok_dev, model), bf16)],
        [],
        [keep, got, far, tokens, gain_one, grad_hidden],
        waits=[taken_grad],
    )[0]
    router_back = router_grad[:experts]
    small_grads = small_sum(jnp.concatenate([gain_one_grad, gain_two_grad, router_back], axis=0), far)

    owned = unpack_half(kept_grad[None], drows, frows)
    fetched = unpack_half(taken_grad[None], drows, frows)
    grad_gate_w, grad_up_w, grad_down_w = [
        unhalve(o, f, core).astype(f32) for o, f in zip(owned, fetched)
    ]
    return (
        mixed,
        grad_tokens,
        small_grads[0],
        grad_wq,
        grad_wk,
        grad_wv,
        grad_wout,
        small_grads[1],
        small_grads[2 : 2 + experts].T,
        grad_gate_w[None],
        grad_up_w[None],
        grad_down_w[None],
    )


def solution(mesh):
    rows = P(("heads", "blk"), None)
    flat = P(("heads", "blk"))
    expert = P("heads", "blk", None)
    return jax.shard_map(
        shards,
        mesh=mesh,
        in_specs=(
            rows, rows, rows, P(), flat, rows, rows, rows, rows, flat, rows, expert, expert, expert,
        ),
        out_specs=(
            rows, rows, flat, rows, rows, rows, rows, flat, rows, expert, expert, expert,
        ),
        check_vma=False,
    )
```

```python
import functools

import jax
import jax.numpy as jnp
from jax import lax
from jax.experimental import pallas as pl
from jax.experimental.pallas import tpu as pltpu
from jax.sharding import PartitionSpec as P

QUERY_HEADS = 24
KEY_VALUE_HEADS = 8
HEAD_WIDTH = 64
CAP = 96
HEADS = 4
GROUP = QUERY_HEADS // KEY_VALUE_HEADS
KV_LOCAL = KEY_VALUE_HEADS // HEADS
Q_LOCAL = KV_LOCAL * GROUP
Q_COLS = Q_LOCAL * HEAD_WIDTH
K_COLS = KV_LOCAL * HEAD_WIDTH
STEP = 256

epsilon_norm = 1e-05
highest = lax.Precision.HIGHEST
masked_score = -1e30
bf16 = jnp.bfloat16
f32 = jnp.float32
BOTH = ("heads", "blk")
VMEM_LIMIT = 60 * 1024 * 1024
LANES = 256


def swap(value, heads_bits, blk_bits):
    count, blocks = lax.axis_size("heads"), lax.axis_size("blk")
    pairs = []
    for i in range(count * blocks):
        h, b = divmod(i, blocks)
        pairs.append((i, (h ^ heads_bits) * blocks + (b ^ blk_bits)))
    return lax.ppermute(value, BOTH, pairs)


def heads_gather(value):
    far = swap(value, 2, 0)
    near = swap(value, 1, 0)
    return jnp.stack([value, near, far, swap(far, 1, 0)])


def heads_reduce(parts):
    got = swap(jnp.stack([parts[1], parts[3]]), 1, 0)
    onward = (parts[2].astype(f32) + got[1].astype(f32)).astype(parts.dtype)
    far = swap(onward, 2, 0)
    return parts[0].astype(f32) + got[0].astype(f32) + far.astype(f32)


def ring_gather(value, *waits):
    pieces = []
    for k in range(lax.axis_size("blk") // 2):
        if k and k <= len(waits):
            value = tie(value, *waits[k - 1])
        value = ring_step(value) if k else value
        pieces += [value, swap(value, 0, 1)]
    return pieces


def reduce_pieces(evens, odds, wait):
    half = len(evens)
    total, sent = None, []
    for g, stack in enumerate(odds):
        got = swap(stack, 0, 1)
        for i in range(stack.shape[0]):
            zr = half - 1 - (g * (half // 2) + i)
            here = evens[zr].astype(f32) + got[i].astype(f32)
            if zr:
                sent.append(here.astype(bf16))
                here = swap(tie(sent[-1], wait), 0, 2 * zr).astype(f32)
            total = here if total is None else total + here
    return total, sent


def gather_few(value):
    column = [value] + [swap(value, 0, r) for r in range(2, lax.axis_size("blk"), 2)]
    beside = swap(jnp.stack(column), 0, 1)
    pieces = []
    for k, piece in enumerate(column):
        pieces += [piece, beside[k]]
    return pieces


def blk_gather(value):
    blocks = lax.axis_size("blk")
    if blocks > 8:
        whole = lax.all_gather(value, "blk", axis=0, tiled=False)
        return jnp.take(whole, lax.axis_index("blk") ^ jnp.arange(blocks), axis=0)
    pieces = [None] * blocks
    for r in range(0, blocks, 2):
        piece = swap(value, 0, r) if r else value
        pieces[r] = piece
        pieces[r + 1] = swap(piece, 0, 1)
    return jnp.stack(pieces)


def blk_reduce(parts):
    blocks = lax.axis_size("blk")
    if blocks > 8:
        whole = jnp.take(parts, lax.axis_index("blk") ^ jnp.arange(blocks), axis=0)
        return lax.psum_scatter(whole, "blk", scatter_dimension=0, tiled=False).astype(f32)
    total = None
    for r in range(blocks - 2, -1, -2):
        got = swap(parts[r + 1], 0, 1)
        here = parts[r].astype(f32) + got.astype(f32)
        if r:
            here = swap(here.astype(parts.dtype), 0, r).astype(f32)
        total = here if total is None else total + here
    return total


def blk_gather_few(value):
    blocks = lax.axis_size("blk")
    if blocks > 8:
        return blk_gather(value)
    column = jnp.stack([value] + [swap(value, 0, r) for r in range(2, blocks, 2)])
    both = jnp.stack([column, swap(column, 0, 1)], axis=1)
    return both.reshape((blocks,) + value.shape)


def reduce_few(parts, direct, *waits):
    if not direct:
        return lax.psum_scatter(parts, "blk", scatter_dimension=0, tiled=False).astype(f32), parts
    got = swap(parts[1], 0, 1)
    here = parts[0].astype(f32) + got.astype(f32)
    sent = here.astype(parts.dtype)
    if waits:
        sent = tie(sent, *waits)
    total = here[0]
    for k in range(1, parts.shape[1]):
        total = total + swap(sent[k], 0, 2 * k).astype(f32)
    return total, sent


def reduce_ring(parts, direct, *waits):
    if not direct:
        return lax.psum_scatter(parts, "blk", scatter_dimension=0, tiled=False).astype(f32)
    got = swap(parts[1], 0, 1)
    here = parts[0].astype(f32) + got.astype(f32)
    moving = here[-1].astype(parts.dtype)
    if waits:
        moving = tie(moving, *waits)
    for k in range(parts.shape[1] - 2, -1, -1):
        total = ring_step(moving).astype(f32) + here[k]
        moving = total.astype(parts.dtype)
    return total


def blk_unshuffle(pieces):
    blocks = pieces.shape[0]
    b = lax.axis_index("blk")
    return jnp.stack(
        [lax.dynamic_index_in_dim(pieces, b ^ i, 0, keepdims=False) for i in range(blocks)]
    )


RING = {0: 1, 1: 3, 3: 2, 2: 0}


def ring_step(value):
    count, blocks = lax.axis_size("heads"), lax.axis_size("blk")
    pairs = []
    for i in range(count * blocks):
        h, b = divmod(i, blocks)
        pairs.append((i, h * blocks + RING[b // 2] * 2 + b % 2))
    return lax.ppermute(value, BOTH, pairs)


def ring_place(z):
    return z ^ (z >> 1)


def ring_owner(z, k):
    place = (ring_place(z) - k) & 3
    return place ^ (place >> 1)


def z_groups(blocks):
    return [[i for i in range(blocks) if i % 2 == y] for y in range(2)]


def expand_heads(transposed, dtype):
    rows = []
    n = transposed.shape[1]
    zero = jnp.zeros((HEAD_WIDTH, n), dtype)
    for g in range(KV_LOCAL):
        columns = []
        for head in range(Q_LOCAL):
            if head // GROUP == g:
                columns.append(transposed[head * HEAD_WIDTH : (head + 1) * HEAD_WIDTH].astype(dtype))
            else:
                columns.append(zero)
        rows.append(jnp.concatenate(columns, axis=1))
    return jnp.concatenate(rows, axis=0)


def collapse_heads(wide, n):
    pieces = []
    for head in range(Q_LOCAL):
        g = head // GROUP
        pieces.append(wide[g * HEAD_WIDTH : (g + 1) * HEAD_WIDTH, head * n : (head + 1) * n])
    return jnp.concatenate(pieces, axis=0)


def key_rows(kv_ref, r, j, low, high):
    return jnp.concatenate(
        [kv_ref[r, j, :, low:high], kv_ref[r + 1, j, :, low:high]], axis=0
    )


def step_place(t, h, b, blocks, tok_dev, direct):
    half = blocks // 2
    owner_h = t // half
    owner_z = t % half
    j = owner_h ^ h
    z, y = b // 2, b % 2
    term = (owner_z ^ z) * 2
    if direct:
        piece = ((ring_place(z) - ring_place(owner_z)) & 3) * 2
    else:
        piece = term
    row = lax.broadcasted_iota(jnp.int32, (2 * tok_dev, 1), 0)
    base = (owner_h * blocks + owner_z * 2) * tok_dev
    second = row >= tok_dev
    position = base + jnp.where(
        second, row - tok_dev + (1 - y) * tok_dev, row + y * tok_dev
    )
    return piece, term, j, position


def fill_pieces(refs, whole_ref):
    for r, ref in enumerate(refs):
        whole_ref[r] = ref[...]


def attend_kernel(blocks, count, *refs):
    scal_ref, q_ref, start_ref = refs[:3]
    pieces = refs[3 : 3 + count]
    att_ref, lse_ref, top_ref, sum_ref, acc_ref = refs[3 + count : 8 + count]
    if count > 1:
        kv_ref = refs[8 + count]
        fill_pieces(pieces, kv_ref)
    else:
        kv_ref = pieces[0]
    tok_dev = q_ref.shape[1]
    h, b = scal_ref[0], scal_ref[1]

    def one(j, unused):
        block = (h ^ j) * blocks + b
        queries = (q_ref[j].astype(f32) * 0.125).T
        wide = expand_heads(queries, bf16)
        lane = lax.broadcasted_iota(jnp.int32, (1, tok_dev), 1)
        query_pos = jnp.concatenate([block * tok_dev + lane] * Q_LOCAL, axis=1)
        start = jnp.concatenate([start_ref[j]] * Q_LOCAL, axis=1)
        top_ref[...] = jnp.full(top_ref.shape, masked_score, f32)
        sum_ref[...] = jnp.zeros(sum_ref.shape, f32)
        acc_ref[...] = jnp.zeros(acc_ref.shape, f32)

        def step(t, unused):
            r, unused_term, jk, position = step_place(t, h, b, blocks, tok_dev, count > 1)
            keys = key_rows(kv_ref, r, jk, 0, K_COLS)
            values = key_rows(kv_ref, r, jk, K_COLS, 2 * K_COLS)
            scores = lax.dot_general(keys, wide, (((1,), (0,)), ((), ())), preferred_element_type=f32)
            allowed = (position >= start) & (position <= query_pos)
            scores = jnp.where(allowed, scores, masked_score)
            old = top_ref[...]
            new = jnp.maximum(old, jnp.max(scores, axis=0, keepdims=True))
            rescale = jnp.exp(old - new)
            weights = jnp.exp(scores - new)
            top_ref[...] = new
            sum_ref[...] = sum_ref[...] * rescale + jnp.sum(weights, axis=0, keepdims=True)
            acc_ref[...] = acc_ref[...] * rescale + lax.dot_general(
                values, weights.astype(bf16), (((0,), (0,)), ((), ())), preferred_element_type=f32
            )
            return unused

        lax.fori_loop(scal_ref[2 + j], block // 2 + 1, step, 0)
        total = sum_ref[...]
        out = collapse_heads(acc_ref[...] / total, tok_dev)
        att_ref[j] = out.T.astype(bf16)
        lse_ref[j] = top_ref[...] + jnp.log(total)
        return unused

    lax.fori_loop(0, HEADS, one, 0)


SMEM = pl.BlockSpec(memory_space=pltpu.SMEM)
VMEM = pl.BlockSpec(memory_space=pltpu.VMEM)
ANY = pl.BlockSpec(memory_space=pl.ANY)


def room_for(arrays, scratch):
    held = sum(a.size * a.dtype.itemsize for a in arrays)
    for s in scratch:
        size = 1
        for n in s.shape:
            size *= n
        held += size * jnp.dtype(s.dtype).itemsize
    return min(VMEM_LIMIT, held + held // 8 + (14 << 20))


def shaped(shape, dtype):
    return jax.ShapeDtypeStruct(shape, dtype)


def call(kernel, name, outs, scalars, arrays, scratch=(), waits=(), cost=4):
    scalars, arrays, waits = list(scalars), list(arrays), list(waits)
    used = len(scalars) + len(arrays)

    def body(*refs):
        kernel(*(refs[:used] + refs[used + len(waits) :]))

    return pl.pallas_call(
        body,
        out_shape=tuple(outs),
        in_specs=[SMEM] * len(scalars) + [VMEM] * len(arrays) + [ANY] * len(waits),
        out_specs=tuple([VMEM] * len(outs)),
        scratch_shapes=list(scratch),
        compiler_params=pltpu.CompilerParams(
            vmem_limit_bytes=room_for(arrays + list(outs), scratch)
        ),
        cost_estimate=pl.CostEstimate(flops=cost * 1000000000, bytes_accessed=1 << 20, transcendentals=0),
        name=name,
    )(*scalars, *arrays, *waits)


def tie(value, *waits):
    def body(*refs):
        pass

    return pl.pallas_call(
        body,
        out_shape=shaped(value.shape, value.dtype),
        in_specs=[ANY] * (1 + len(waits)),
        out_specs=ANY,
        input_output_aliases={0: 0},
        name="tie",
    )(value, *waits)


def attend(scal, queries, kv, start, blocks, waits=()):
    tok_dev = queries.shape[1]
    wide = Q_LOCAL * tok_dev
    scratch = [
        pltpu.VMEM((1, wide), f32),
        pltpu.VMEM((1, wide), f32),
        pltpu.VMEM((K_COLS, wide), f32),
    ]
    if len(kv) > 1:
        scratch.append(pltpu.VMEM((blocks,) + kv[0].shape, bf16))
    return call(
        functools.partial(attend_kernel, blocks, len(kv)),
        "attend",
        (
            shaped((HEADS, tok_dev, Q_COLS), bf16),
            shaped((HEADS, 1, wide), f32),
        ),
        [scal],
        [queries, start] + list(kv),
        scratch,
        waits=waits,
        cost=12,
    )


def attend_back_kernel(blocks, count, *refs):
    scal_ref, q_ref, start_ref, att_ref, lse_ref, wo_ref = refs[:6]
    branch = refs[6:10]
    pieces = refs[10 : 10 + count]
    dq_ref = refs[10 + count]
    n_outs = count // 2 + 2 if count > 1 else 1
    outs = refs[11 + count : 11 + count + n_outs]
    acc_ref, term_ref, grad_ref = refs[11 + count + n_outs : 14 + count + n_outs]
    if count > 1:
        kv_ref = refs[14 + count + n_outs]
        fill_pieces(pieces, kv_ref)
    else:
        kv_ref = pieces[0]
    tok_dev = q_ref.shape[1]
    h, b = scal_ref[0], scal_ref[1]
    term_ref[...] = jnp.zeros(term_ref.shape, f32)
    for j in range(HEADS):
        grad_ref[j] = dot_nt(branch[j][...], wo_ref[...]).astype(bf16)

    def one(j, unused):
        block = (h ^ j) * blocks + b
        wide = expand_heads((q_ref[j].astype(f32) * 0.125).T, bf16)
        grad_t = grad_ref[j].astype(f32).T
        wide_grad = expand_heads(grad_t, bf16)
        product = grad_t * att_ref[j].astype(f32).T
        delta = jnp.concatenate(
            [
                jnp.sum(product[head * HEAD_WIDTH : (head + 1) * HEAD_WIDTH], axis=0, keepdims=True)
                for head in range(Q_LOCAL)
            ],
            axis=1,
        )
        lse = lse_ref[j]
        lane = lax.broadcasted_iota(jnp.int32, (1, tok_dev), 1)
        query_pos = jnp.concatenate([block * tok_dev + lane] * Q_LOCAL, axis=1)
        start = jnp.concatenate([start_ref[j]] * Q_LOCAL, axis=1)
        acc_ref[...] = jnp.zeros(acc_ref.shape, f32)

        def step(t, unused):
            r, rt, jk, position = step_place(t, h, b, blocks, tok_dev, count > 1)
            keys = key_rows(kv_ref, r, jk, 0, K_COLS)
            values = key_rows(kv_ref, r, jk, K_COLS, 2 * K_COLS)
            scores = lax.dot_general(keys, wide, (((1,), (0,)), ((), ())), preferred_element_type=f32)
            allowed = (position >= start) & (position <= query_pos)
            probs = jnp.exp(jnp.where(allowed, scores - lse, masked_score))
            grad_probs = lax.dot_general(
                values, wide_grad, (((1,), (0,)), ((), ())), preferred_element_type=f32
            )
            grad_scores = (probs * (grad_probs - delta)).astype(bf16)
            acc_ref[...] += lax.dot_general(
                keys, grad_scores, (((0,), (0,)), ((), ())), preferred_element_type=f32
            )
            key_term = lax.dot_general(
                grad_scores, wide, (((1,), (1,)), ((), ())), preferred_element_type=f32
            )
            value_term = lax.dot_general(
                probs.astype(bf16), wide_grad, (((1,), (1,)), ((), ())), preferred_element_type=f32
            )
            both = jnp.concatenate([key_term, value_term], axis=1)
            term_ref[rt, jk] += both[:tok_dev]
            term_ref[rt + 1, jk] += both[tok_dev:]
            return unused

        lax.fori_loop(scal_ref[2 + j], block // 2 + 1, step, 0)
        dq_ref[j] = (collapse_heads(acc_ref[...], tok_dev) * 0.125).T.astype(bf16)
        return unused

    lax.fori_loop(0, HEADS, one, 0)
    if count > 1:
        half = count // 2
        for zr in range(half):
            outs[zr][...] = term_ref[2 * zr].astype(bf16)
            back = half - 1 - zr
            outs[half + back // (half // 2)][back % (half // 2)] = term_ref[2 * zr + 1].astype(bf16)
    else:
        outs[0][...] = term_ref[...].astype(bf16)


def attend_back(scal, queries, kv, start, att, lse, output_w, branch, blocks, waits=()):
    tok_dev = queries.shape[1]
    wide = Q_LOCAL * tok_dev
    whole = (blocks, HEADS, tok_dev, 2 * K_COLS)
    scratch = [
        pltpu.VMEM((K_COLS, wide), f32),
        pltpu.VMEM(whole, f32),
        pltpu.VMEM((HEADS, tok_dev, Q_COLS), bf16),
    ]
    terms = [shaped(whole, bf16)]
    if len(kv) > 1:
        scratch.append(pltpu.VMEM(whole, bf16))
        half = blocks // 2
        terms = [shaped(whole[1:], bf16)] * half + [shaped((half // 2,) + whole[1:], bf16)] * 2
    outs = call(
        functools.partial(attend_back_kernel, blocks, len(kv)),
        "attend_back",
        [shaped((HEADS, tok_dev, Q_COLS), bf16)] + terms,
        [scal],
        [queries, start, att, lse, output_w] + list(branch) + list(kv),
        scratch,
        waits=waits,
        cost=17,
    )
    return outs[0], outs[1:]


def dot(a, b):
    return jnp.dot(a, b, preferred_element_type=f32)


def dot_tn(a, b):
    return lax.dot_general(a, b, (((0,), (0,)), ((), ())), preferred_element_type=f32)


def dot_nt(a, b):
    return lax.dot_general(a, b, (((1,), (1,)), ((), ())), preferred_element_type=f32)


def split(value, count):
    terms = []
    for unused in range(count):
        term = value.astype(bf16)
        terms.append(term)
        value = value - term.astype(f32)
    return terms


def own_rows(b, r, source, wrows, blocks):
    return pl.ds(pl.multiple_of((source * blocks + (b ^ r)) * wrows, 16), wrows)


def project_kernel(blocks, count, *refs):
    scal_ref, gain_ref = refs[:2]
    tokens = refs[2:6]
    pieces = refs[6 : 6 + count]
    normed_ref, q_ref, kv_ref = refs[6 + count : 9 + count]
    w_ref = refs[9 + count] if count > 1 else pieces[0]
    b = scal_ref[1]
    if count > 1:
        wrows = pieces[0].shape[1]
        for r in range(count):
            for source in range(HEADS):
                owner = ring_owner(b // 2, r // 2) * 2 + (b % 2 ^ r % 2)
                low = pl.multiple_of((source * blocks + owner) * wrows, 16)
                w_ref[pl.ds(low, wrows), :] = pieces[r][source]
    tok_dev = tokens[0].shape[0]
    for j in range(HEADS):
        value = tokens[j][...].astype(f32)
        inverse = lax.rsqrt(jnp.mean(value * value, axis=-1, keepdims=True) + epsilon_norm)
        normed_ref[j * tok_dev : (j + 1) * tok_dev, :] = (value * inverse * gain_ref[...]).astype(bf16)
    projected = dot(normed_ref[...], w_ref[...]).astype(bf16)
    for j in range(HEADS):
        q_ref[j] = projected[j * tok_dev : (j + 1) * tok_dev, :Q_COLS]
        kv_ref[j] = projected[j * tok_dev : (j + 1) * tok_dev, Q_COLS:]


def project(scal, gain, tokens, pieces, blocks, waits=()):
    tok_dev, model = tokens[0].shape
    outs = [
        shaped((HEADS * tok_dev, model), bf16),
        shaped((HEADS, tok_dev, Q_COLS), bf16),
        shaped((HEADS, tok_dev, 2 * K_COLS), bf16),
    ]
    if len(pieces) > 1:
        outs.append(shaped((model, Q_COLS + 2 * K_COLS), bf16))
    got = call(
        functools.partial(project_kernel, blocks, len(pieces)),
        "project",
        outs,
        [scal],
        [gain] + list(tokens) + list(pieces),
        waits=waits,
    )
    return got[:3] + (got[3] if len(pieces) > 1 else pieces[0],)


def output_kernel(blocks, count, *refs):
    scal_ref, att_ref = refs[:2]
    pieces = refs[2 : 2 + count]
    keep_ref, send_ref = refs[2 + count : 4 + count]
    wo_ref = refs[4 + count] if count > 1 else pieces[0]
    b = scal_ref[1]
    if count > 1:
        wrows = pieces[0].shape[0]
        for r in range(count):
            wo_ref[own_rows(b, r, 0, wrows, blocks), :] = pieces[r][...]
    for j in range(HEADS):
        part = dot(att_ref[j], wo_ref[...]).astype(bf16)
        if j % 2:
            send_ref[j // 2] = part
        else:
            keep_ref[j // 2] = part


def output_parts(scal, att, pieces, model, blocks, waits):
    tok_dev = att.shape[1]
    outs = [shaped((2, tok_dev, model), bf16)] * 2
    if len(pieces) > 1:
        outs.append(shaped((Q_COLS, model), bf16))
    got = call(
        functools.partial(output_kernel, blocks, len(pieces)),
        "output_parts",
        outs,
        [scal],
        [att] + list(pieces),
        waits=waits,
    )
    return got[0], got[1], (got[2] if len(pieces) > 1 else pieces[0])


def heads_sum(keep, send):
    got = swap(send, 1, 0)
    onward = (keep[1].astype(f32) + got[1].astype(f32)).astype(bf16)
    return got, swap(onward, 2, 0)


def route_kernel(
    scal_ref, keep_ref, got_ref, far_ref, tokens_ref, gain_ref, router_ref, member_ref, table_ref, cot_ref,
    s0, s1, s2, s3, g0, g1, g2, g3, hidden_ref, nf_ref, gates_ref, slot_gate_ref, sent_ref, back_ref,
):
    hidden = (
        tokens_ref[...].astype(f32)
        + keep_ref[0].astype(f32)
        + got_ref[0].astype(f32)
        + far_ref[...].astype(f32)
    )
    hidden_ref[...] = hidden
    inverse = lax.rsqrt(jnp.mean(hidden * hidden, axis=-1, keepdims=True) + epsilon_norm)
    nf = (hidden * inverse * gain_ref[...]).astype(bf16)
    nf_ref[...] = nf
    logits = dot_nt(nf, router_ref[...])
    picked = member_ref[...] > 0
    peak = jnp.max(jnp.where(picked, logits, -jnp.inf), axis=-1, keepdims=True)
    raised = jnp.where(picked, jnp.exp(jnp.where(picked, logits - peak, 0.0)), 0.0)
    gates = raised / jnp.sum(raised, axis=-1, keepdims=True)
    gates_ref[...] = gates
    table = table_ref[...]
    sent = dot(table, nf).astype(bf16)
    spread = dot(table, cot_ref[...])
    slot_gates = sum(dot(table, term) for term in split(gates, 3))
    lane = lax.broadcasted_iota(jnp.int32, (CAP, slot_gates.shape[1]), 1)
    sent_ref[...] = sent
    for e in range(4):
        rows = slice(e * CAP, (e + 1) * CAP)
        column = jnp.sum(jnp.where(lane == e, slot_gates[rows], 0.0), axis=1, keepdims=True)
        slot_gate_ref[rows, :] = column
        back_ref[rows, :] = (spread[rows] * column).astype(bf16)
    for r, (s_ref, g_ref) in enumerate(((s0, g0), (s1, g1), (s2, g2), (s3, g3))):
        rows = slot_rows(own_place(scal_ref) ^ r)
        s_ref[...] = sent_ref[rows, :]
        g_ref[...] = back_ref[rows, :]


def gate_up(ref, drows):
    return jnp.concatenate(
        [ref[:, k * drows : (k + 1) * drows, :].reshape(-1, LANES) for k in range(4)], axis=1
    )


def down_half(ref, drows, frows):
    base = 4 * drows
    return jnp.concatenate(
        [ref[:, base + k * frows : base + (k + 1) * frows, :].reshape(-1, LANES) for k in range(3)],
        axis=1,
    )


def lanes(offset, size):
    return pl.ds(pl.multiple_of(offset, 128), size)


def fill_weights(scal_ref, refs, mine_ref, other_ref):
    z = scal_ref[1] // 2
    for pieces, whole_ref in ((refs[:4], mine_ref), (refs[4:], other_ref)):
        for k in range(4):
            for y in range(2):
                whole_ref[ring_owner(z, k) * 2 + y] = pieces[k][y]


def expert_kernel(drows, frows, direct, *refs):
    scal_ref = refs[0]
    if direct:
        p0, p1, p2, p3, gp_ref, up_ref, inner_ref, out_ref, mine_ref, other_ref = refs[13:]
        fill_weights(scal_ref, refs[5:13], mine_ref, other_ref)
    else:
        mine_ref, other_ref, p0, p1, p2, p3, gp_ref, up_ref, inner_ref, out_ref = refs[5:]
    fill_rows(scal_ref, refs[1:5], out_ref)
    core = scal_ref[0] % 2
    rows = out_ref[...]
    for side, ref in ((core, mine_ref), (1 - core, other_ref)):
        both = dot(rows, gate_up(ref, drows))
        gate, up = both[:, : 2 * LANES], both[:, 2 * LANES :]
        place = lanes(side * 2 * LANES, 2 * LANES)
        gp_ref[:, place] = gate
        up_ref[:, place] = up
        inner_ref[:, place] = (gate * jax.nn.sigmoid(gate) * up).astype(bf16)
    inner = inner_ref[...]
    for side, ref in ((core, mine_ref), (1 - core, other_ref)):
        out_ref[:, lanes(side * 3 * LANES, 3 * LANES)] = dot(inner, down_half(ref, drows, frows)).astype(bf16)
    for r, ref in enumerate((p0, p1, p2, p3)):
        ref[...] = out_ref[slot_rows(own_place(scal_ref) ^ r), :]


def own_place(scal_ref):
    return scal_ref[0] // 2 * 2 + scal_ref[1] % 2


def slot_rows(place):
    return pl.ds(pl.multiple_of(place * CAP, 16), CAP)


def fill_rows(scal_ref, refs, rows_ref):
    for r, ref in enumerate(refs):
        rows_ref[slot_rows(own_place(scal_ref) ^ r), :] = ref[...]


def weights_of(scal_ref, refs, scratch):
    if not scratch:
        return refs
    fill_weights(scal_ref, refs, *scratch)
    return scratch


def expert_back_kernel(drows, frows, count, *refs):
    scal_ref = refs[0]
    gp_ref, up_ref = refs[5:7]
    ggp_ref, gup_ref, grad_ref = refs[7 + count : 10 + count]
    mine_ref, other_ref = weights_of(scal_ref, refs[7 : 7 + count], refs[10 + count :])
    fill_rows(scal_ref, refs[1:5], grad_ref)
    core = scal_ref[0] % 2
    grad_inner = None
    for side, ref in ((core, mine_ref), (1 - core, other_ref)):
        term = dot_nt(grad_ref[:, lanes(side * 3 * LANES, 3 * LANES)], down_half(ref, drows, frows))
        grad_inner = term if grad_inner is None else grad_inner + term
    gate, up = gp_ref[...], up_ref[...]
    sig = jax.nn.sigmoid(gate)
    ggp_ref[...] = (grad_inner * up * sig * (1.0 + gate * (1.0 - sig))).astype(bf16)
    gup_ref[...] = (grad_inner * gate * sig).astype(bf16)


def expert_input_kernel(drows, frows, count, *refs):
    scal_ref, ggp_ref, gup_ref = refs[:3]
    p0, p1, p2, p3, grad_ref = refs[3 + count : 8 + count]
    mine_ref, other_ref = weights_of(scal_ref, refs[3 : 3 + count], refs[8 + count :])
    core = scal_ref[0] % 2
    total = None
    for side, ref in ((core, mine_ref), (1 - core, other_ref)):
        place = lanes(side * 2 * LANES, 2 * LANES)
        both = jnp.concatenate([ggp_ref[:, place], gup_ref[:, place]], axis=1)
        term = dot_nt(both, gate_up(ref, drows))
        total = term if total is None else total + term
    grad_ref[...] = total.astype(bf16)
    for r, ref in enumerate((p0, p1, p2, p3)):
        ref[...] = grad_ref[slot_rows(own_place(scal_ref) ^ r), :]


def expert_weights_kernel(
    drows, frows, blocks, own, scal_ref, x0, x1, x2, x3, g0, g1, g2, g3, inner_ref, ggp_ref, gup_ref, *rest
):
    if own:
        got_ref, out_ref, grad_ref, rows_ref = rest
    else:
        out_ref, grad_ref, rows_ref = rest
    core, z = scal_ref[0] % 2, scal_ref[1] // 2
    side = core if own else 1 - core
    fill_rows(scal_ref, (g0, g1, g2, g3), grad_ref)
    fill_rows(scal_ref, (x0, x1, x2, x3), rows_ref)
    rows = rows_ref[...]

    def put(low, height, term):
        for k in range(term.shape[1] // LANES):
            piece = term[:, k * LANES : (k + 1) * LANES].reshape(blocks // 2, 2, height, LANES)
            place = slice(low, low + height)
            for at in range(blocks // 2):
                step = (ring_place(at) - ring_place(z)) & 3 if blocks == 8 else at
                value = piece[at]
                if own:
                    value = value + got_ref[step, :, place, :].astype(f32)
                out_ref[step, :, place, :] = value.astype(bf16)
            low += height

    place = lanes(side * 2 * LANES, 2 * LANES)
    both = jnp.concatenate([ggp_ref[:, place], gup_ref[:, place]], axis=1)
    put(0, drows, dot_tn(rows, both))
    put(4 * drows, frows, dot_tn(inner_ref[...], grad_ref[:, lanes(side * 3 * LANES, 3 * LANES)]))


def combine_kernel(
    scal_ref, r0, r1, r2, r3, hidden_ref, nf_ref, gates_ref, slot_gate_ref, table_ref, cot_ref, router_ref,
    mixed_ref, grad_nf_ref, router_grad_ref, ret_ref,
):
    table = table_ref[...]
    fill_rows(scal_ref, (r0, r1, r2, r3), ret_ref)
    returned = ret_ref[...]
    scaled_rows = returned.astype(f32) * slot_gate_ref[...]
    mixed_ref[...] = (hidden_ref[...] + sum(dot_tn(table, t) for t in split(scaled_rows, 2))).astype(bf16)
    scored = dot_nt(returned, cot_ref[...]) * table.astype(f32)
    gates_t = gates_ref[...].T[:8]
    score_rows = [
        jnp.sum(scored[e * CAP : (e + 1) * CAP], axis=0, keepdims=True) for e in range(4)
    ]
    scores = jnp.concatenate(score_rows + [jnp.zeros((4, scored.shape[1]), f32)], axis=0)
    mean_gate = jnp.sum(gates_t * scores, axis=0, keepdims=True)
    grad_logits = gates_t * (scores - mean_gate)
    terms = split(grad_logits, 3)
    router_grad_ref[...] = sum(dot(t, nf_ref[...]) for t in terms)
    grad_nf_ref[...] = sum(dot_tn(t, router_ref[:8, :]) for t in terms)


def norm_back_kernel(
    scal_ref, b0, b1, b2, b3, hidden_ref, table_ref, cot_ref, gain_ref, part_ref,
    grad_hidden_ref, branch_ref, gain_grad_ref, back_ref,
):
    hidden = hidden_ref[...]
    fill_rows(scal_ref, (b0, b1, b2, b3), back_ref)
    grad_nf = dot_tn(table_ref[...], back_ref[...]) + part_ref[...]
    inverse = lax.rsqrt(jnp.mean(hidden * hidden, axis=-1, keepdims=True) + epsilon_norm)
    gain_grad_ref[...] = jnp.sum(grad_nf * hidden * inverse, axis=0, keepdims=True)
    scaled = grad_nf * gain_ref[...]
    grad_hidden = (
        cot_ref[...].astype(f32)
        + inverse * scaled
        - hidden * (inverse * inverse * inverse) * jnp.mean(scaled * hidden, axis=-1, keepdims=True)
    )
    grad_hidden_ref[...] = grad_hidden
    branch_ref[...] = grad_hidden.astype(bf16)


def late_grad_kernel(blocks, wrows, direct, scal_ref, normed_ref, dq_ref, att_ref, b0, b1, b2, b3, out_ref, q_ref, o_ref):
    b = scal_ref[1]
    flat = jnp.concatenate([dq_ref[j] for j in range(HEADS)], axis=0)
    q_ref[...] = dot_tn(normed_ref[...], flat).astype(bf16)
    total = None
    for j, ref in enumerate((b0, b1, b2, b3)):
        term = dot_tn(att_ref[j], ref[...])
        total = term if total is None else total + term
    o_ref[...] = total.astype(bf16)
    for r in range(blocks):
        owner = ring_owner(b // 2, -(r // 2)) * 2 + (b % 2 ^ r % 2)
        for source in range(HEADS):
            cols = slice(source * Q_COLS, (source + 1) * Q_COLS)
            if direct:
                low = pl.multiple_of((source * blocks + owner) * wrows, 16)
                out_ref[r % 2, r // 2, :wrows, cols] = q_ref[pl.ds(low, wrows), :]
            else:
                low = (source * blocks + r) * wrows
                out_ref[r, :wrows, cols] = q_ref[low : low + wrows, :]
        if direct:
            low = pl.multiple_of(owner * wrows, 16)
            out_ref[r % 2, r // 2, wrows:, :] = o_ref[pl.ds(low, wrows), :]
        else:
            out_ref[r, wrows:, :] = o_ref[r * wrows : (r + 1) * wrows, :]


def pair_shape(blocks, rest, direct):
    return ((2, blocks // 2) if direct else (blocks,)) + rest


def column_grad_kernel(blocks, wrows, direct, scal_ref, normed_ref, grad_ref, out_ref, hold_ref):
    b = scal_ref[1]
    flat = jnp.concatenate([grad_ref[j] for j in range(HEADS)], axis=0)
    hold_ref[...] = dot_tn(normed_ref[...], flat).astype(bf16)
    for r in range(blocks):
        for source in range(HEADS):
            if direct:
                out_ref[r % 2, r // 2, source] = hold_ref[own_rows(b, r, source, wrows, blocks), :]
            else:
                low = (source * blocks + r) * wrows
                out_ref[r, source] = hold_ref[low : low + wrows, :]


def normed_back_kernel(dq_ref, dkv_ref, w_ref, t0, t1, t2, t3, keep_ref, send_ref, gain_grad_ref):
    total = None
    for j, ref in enumerate((t0, t1, t2, t3)):
        part = dot_nt(dq_ref[j], w_ref[:, :Q_COLS]) + dot_nt(dkv_ref[j], w_ref[:, Q_COLS:])
        value = ref[...].astype(f32)
        inverse = lax.rsqrt(jnp.mean(value * value, axis=-1, keepdims=True) + epsilon_norm)
        term = jnp.sum(part * (value * inverse), axis=0, keepdims=True)
        total = term if total is None else total + term
        if j % 2:
            send_ref[j // 2] = part.astype(bf16)
        else:
            keep_ref[j // 2] = part.astype(bf16)
    gain_grad_ref[...] = total


def tokens_back_kernel(keep_ref, got_ref, far_ref, tokens_ref, gain_ref, grad_hidden_ref, out_ref):
    grad_normed = keep_ref[0].astype(f32) + got_ref[0].astype(f32) + far_ref[...].astype(f32)
    value = tokens_ref[...].astype(f32)
    inverse = lax.rsqrt(jnp.mean(value * value, axis=-1, keepdims=True) + epsilon_norm)
    scaled = grad_normed * gain_ref[...]
    out_ref[...] = (
        grad_hidden_ref[...]
        + inverse * scaled
        - value * (inverse * inverse * inverse) * jnp.mean(scaled * value, axis=-1, keepdims=True)
    ).astype(bf16)


def small_share(values, wait):
    devices = lax.axis_size("heads") * lax.axis_size("blk")
    n, width = values.shape
    padded = tie(jnp.pad(values, ((0, 8 - n), (0, 128 - width))), wait)
    got = lax.all_to_all(
        jnp.broadcast_to(padded[None], (devices, 8, 128)), BOTH, 0, 0, tiled=True
    )
    return jnp.transpose(got[:, :n, :width], (1, 0, 2)).reshape(n, devices * width)


def small_sum(values, wait):
    devices = lax.axis_size("heads") * lax.axis_size("blk")
    n = values.shape[0]
    width = values.shape[1] // devices
    parts = jnp.transpose(values.reshape(n, devices, width), (1, 0, 2))
    padded = jnp.pad(parts, ((0, 0), (0, 8 - n), (0, 128 - width)))
    got = lax.all_to_all(tie(padded, wait), BOTH, 0, 0, tiled=True)
    return jnp.sum(got, axis=0)[:n, :width]


def halves(columns, core):
    half = columns.shape[1] // 2
    first, second = columns[:, :half], columns[:, half:]
    return jnp.where(core == 0, first, second), jnp.where(core == 0, second, first)


def unhalve(own, other, core):
    return jnp.concatenate(
        [jnp.where(core == 0, own, other), jnp.where(core == 0, other, own)], axis=1
    )


def unpack_half(buffer, drows, frows):
    def piece(low, high):
        return buffer[:, low:high].reshape(-1, LANES)

    matrices, base = [], 0
    for rows, count in ((drows, 2), (drows, 2), (frows, 3)):
        matrices.append(
            jnp.concatenate([piece(base + k * rows, base + (k + 1) * rows) for k in range(count)], axis=1)
        )
        base += rows * count
    return matrices


def pack_half(gate, up, down, count):
    pieces = []
    for matrix in (gate, up, down):
        rows = matrix.shape[0] // count
        for k in range(matrix.shape[1] // LANES):
            pieces.append(matrix[:, k * LANES : (k + 1) * LANES].reshape(count, rows, LANES))
    return jnp.concatenate(pieces, axis=1)


def shards(
    tokens,
    cotangent,
    routes,
    doc_lengths,
    attn_norm,
    w_query,
    key_weight,
    value_weight,
    w_output,
    ffn_norm,
    w_router,
    w_gate,
    w_up,
    w_down,
):
    blocks = lax.axis_size("blk")
    direct = blocks <= 8
    tok_dev, model = tokens.shape
    wrows = w_query.shape[0]
    drows = w_gate.shape[1]
    frows = w_down.shape[1]
    experts = w_router.shape[1]
    h, b = lax.axis_index("heads"), lax.axis_index("blk")
    core, x, y = h % 2, h // 2, b % 2
    zn = blocks // 2
    wide_cols = Q_COLS + 2 * K_COLS

    w_out = w_output.astype(bf16)
    if direct:
        wo_pieces = gather_few(w_out)
    else:
        wo_pieces = [lax.all_gather(w_out, "blk", axis=0, tiled=True)]

    far = swap(tokens, 2, 0)
    all_tokens = [tokens, swap(tokens, 1, 0), far, swap(far, 1, 0)]

    cut = [halves(m, core) for m in (w_gate[0].astype(bf16), w_up[0].astype(bf16), w_down[0].astype(bf16))]
    kept = pack_half(cut[0][0], cut[1][0], cut[2][0], 1)[0]
    given = pack_half(cut[0][1], cut[1][1], cut[2][1], 1)[0]
    at_home = core == y

    heads_cat = jnp.concatenate(
        [
            w_query.astype(bf16).reshape(wrows, HEADS, Q_COLS),
            key_weight.astype(bf16).reshape(wrows, HEADS, K_COLS),
            value_weight.astype(bf16).reshape(wrows, HEADS, K_COLS),
        ],
        axis=2,
    )
    small_own = jnp.concatenate(
        [attn_norm.astype(bf16)[None], ffn_norm.astype(bf16)[None], w_router.astype(bf16).T], axis=0
    )
    by_head = lax.all_to_all(jnp.swapaxes(heads_cat, 0, 1), "heads", 0, 0, tiled=True)
    taken = swap(given, 1, 0)
    stay = jnp.where(at_home, kept, taken)
    leave = jnp.where(at_home, taken, kept)
    came = swap(leave, 0, 1)
    small = small_share(small_own, came)
    column = jnp.stack([jnp.where(y == 0, stay, came), jnp.where(y == 0, came, stay)])
    if direct:
        w_pieces = ring_gather(by_head, [far, all_tokens[1]], [wo_pieces[k] for k in (2, 4, 6)] + [all_tokens[3]])
        mine = [column, ring_step(tie(column, w_pieces[6]))]
    else:
        whole = lax.all_gather(by_head, "blk", axis=1, tiled=False)
        w_pieces = [whole.reshape(model, wide_cols)]
        mine = lax.all_gather(column, "blk", axis=0, tiled=False, axis_index_groups=z_groups(blocks))
        mine = mine.reshape((blocks,) + kept.shape)
    gain_one, gain_two = small[0:1].astype(f32), small[1:2].astype(f32)

    ends = jnp.cumsum(doc_lengths)
    block_of = (h ^ jnp.arange(HEADS, dtype=jnp.int32)) * blocks + b
    query_pos = block_of[:, None] * tok_dev + jnp.arange(tok_dev, dtype=jnp.int32)[None, :]
    start = jnp.max(
        jnp.where(ends[None, None, :] <= query_pos[:, :, None], ends[None, None, :], 0), axis=2
    ).astype(jnp.int32)
    scal = jnp.concatenate(
        [
            jnp.stack([h, b]).astype(jnp.int32),
            start[:, 0] // (2 * tok_dev),
        ]
    )
    start = start[:, None, :]

    member = jnp.sum((routes[:, :, None] == jnp.arange(experts)[None, None, :]).astype(f32), axis=1)
    lower = (jnp.arange(tok_dev)[:, None] > jnp.arange(tok_dev)[None, :]).astype(bf16)
    rank = dot(lower, member.astype(bf16))
    slot = jnp.arange(CAP, dtype=f32)
    table = (
        ((rank.T[:, None, :] == slot[None, :, None]) & (member.T[:, None, :] > 0))
        .astype(bf16)
        .reshape(experts * CAP, tok_dev)
    )
    member = jnp.pad(member, ((0, 0), (0, 128 - experts)))
    router_all = jnp.pad(small[2 : 2 + experts], ((0, 128 - experts), (0, 0)))

    normed, queries, kv_own, weights = project(
        scal, gain_one, all_tokens, w_pieces, blocks, [table, member, router_all, gain_two, start]
    )
    if direct:
        kv = ring_gather(kv_own)
        mine.append(ring_step(tie(mine[1], kv[2])))
        mine.append(ring_step(mine[2]))
    else:
        kv = [blk_gather(kv_own)]
    att, lse = attend(scal, queries, kv, start, blocks)
    keep, send, output_w = output_parts(scal, att, wo_pieces, model, blocks, [])
    got, far = heads_sum(keep, send)
    seconds = [swap(piece, 1, 0) for piece in mine[:3]] if direct else []
    slot = shaped((CAP, model), bf16)
    hold = pltpu.VMEM((experts * CAP, model), bf16)
    routed = call(
        route_kernel,
        "route",
        [slot] * 8
        + [
            shaped((tok_dev, model), f32),
            shaped((tok_dev, model), bf16),
            shaped((tok_dev, 128), f32),
            shaped((experts * CAP, 1), f32),
        ],
        [scal],
        [keep, got, far, tokens, gain_two, router_all, member, table, cotangent],
        [hold, hold],
        waits=seconds,
        cost=3,
    )
    sent, grad_sent = routed[:4], routed[4:8]
    hidden, normed_ffn, gates, slot_gate = routed[8:]

    def to_experts(pieces):
        return [pieces[0]] + [swap(pieces[r], r // 2 * 2, r % 2) for r in range(1, experts)]

    arrived = to_experts(sent)
    grad_arrived = to_experts(grad_sent)
    if direct:
        weights_in = mine + seconds + [swap(tie(mine[3], *arrived[1:]), 1, 0)]
        gathered = [pltpu.VMEM((blocks,) + kept.shape, bf16)] * 2
    else:
        mine = tie(mine, sent[0])
        other = swap(mine, 1, 0)
        weights_in, gathered = [mine, other], []
    rows_all = experts * CAP
    ff = frows * blocks
    fwd = call(
        functools.partial(expert_kernel, drows, frows, direct),
        "expert",
        [slot] * 4
        + [shaped((rows_all, ff), f32), shaped((rows_all, ff), f32), shaped((rows_all, ff), bf16)],
        [scal],
        arrived + weights_in,
        [hold] + gathered,
        cost=2,
    )
    gate_pre, up_pre, inner = fwd[4:7]
    returned = to_experts(fwd[:4])
    grad_pre = call(
        functools.partial(expert_back_kernel, drows, frows, len(weights_in)),
        "expert_back",
        [shaped((rows_all, ff), bf16)] * 2,
        [scal],
        grad_arrived + [gate_pre, up_pre] + weights_in,
        [hold] + gathered,
        cost=2,
    )
    grad_pre = list(grad_pre)

    def expert_weights(own, extra, waits=()):
        return call(
            functools.partial(expert_weights_kernel, drows, frows, blocks, own),
            "expert_weights",
            [shaped((zn, 2) + kept.shape, bf16)],
            [scal],
            arrived + grad_arrived + [inner] + grad_pre + extra,
            [hold, hold],
            waits=waits,
            cost=1,
        )[0]

    grads_other = expert_weights(False, [])
    grads_met = swap(grads_other, 1, 0)
    grad_in = call(
        functools.partial(expert_input_kernel, drows, frows, len(weights_in)),
        "expert_input",
        [slot] * 4,
        [scal],
        grad_pre + weights_in,
        [hold] + gathered,
        waits=[grads_other],
        cost=2,
    )
    grad_returned = to_experts(grad_in)
    chip_grads = expert_weights(True, [grads_met], [grad_in[0]] + returned[1:])

    mixed, part_nf, router_grad = call(
        combine_kernel,
        "combine",
        [
            shaped((tok_dev, model), bf16),
            shaped((tok_dev, model), f32),
            shaped((8, model), f32),
        ],
        [scal],
        returned + [hidden, normed_ffn, gates, slot_gate, table, cotangent, router_all],
        [hold],
        waits=[chip_grads],
        cost=1,
    )
    later = [mixed]
    if direct:

        def met(moving, k):
            return (moving.astype(f32) + chip_grads[k].astype(f32)).astype(bf16)

        second_sum = met(ring_step(chip_grads[3]), 2)
        third_sum = met(ring_step(second_sum), 1)
        later_still = [second_sum]
    else:
        z_grads = lax.psum_scatter(
            chip_grads, "blk", scatter_dimension=0, tiled=False, axis_index_groups=z_groups(blocks)
        )
        later_still = []
    grad_hidden, branch, gain_two_grad = call(
        norm_back_kernel,
        "norm_back",
        [
            shaped((tok_dev, model), f32),
            shaped((tok_dev, model), bf16),
            shaped((1, model), f32),
        ],
        [scal],
        grad_returned + [hidden, table, cotangent, gain_two, part_nf],
        [hold],
        waits=later,
    )

    far_branch = swap(branch, 2, 0)
    branches = [branch, swap(branch, 1, 0), far_branch, swap(far_branch, 1, 0)]
    dq, dkv = attend_back(scal, queries, kv, start, att, lse, output_w, branches, blocks, later_still)
    if direct:
        dkv_own, onward = reduce_pieces(dkv[:zn], dkv[zn:], third_sum)
    else:
        dkv_own, onward = blk_reduce(dkv[0]), [dq]
    dkv_own = dkv_own.astype(bf16)
    if direct:
        z_grads = met(ring_step(tie(third_sum, dkv_own)), 0)

    def column_grads(name, grad, waits=()):
        cols = grad.shape[2]
        return call(
            functools.partial(column_grad_kernel, blocks, wrows, direct),
            name,
            [shaped(pair_shape(blocks, (HEADS, wrows, cols), direct), bf16)],
            [scal],
            [normed, grad],
            [pltpu.VMEM((model, cols), bf16)],
            waits=waits,
        )[0]

    late_parts = call(
        functools.partial(late_grad_kernel, blocks, wrows, direct),
        "late_grad",
        [shaped(pair_shape(blocks, (2 * wrows, model), direct), bf16)],
        [scal],
        [normed, dq, att] + branches,
        [pltpu.VMEM((model, Q_COLS), bf16), pltpu.VMEM((Q_COLS, model), bf16)],
        waits=[dq],
    )[0]
    late_parts = tie(late_parts, *(onward[:2] + ([third_sum] if direct else [])))
    late_sums = reduce_ring(late_parts, direct, dkv_own)
    grad_wout = late_sums[wrows:]
    sum_wq = jnp.swapaxes(late_sums[:wrows].reshape(wrows, HEADS, Q_COLS), 0, 1)
    keep, send, gain_one_grad = call(
        normed_back_kernel,
        "normed_back",
        [shaped((2, tok_dev, model), bf16)] * 2 + [shaped((1, model), f32)],
        [],
        [dq, dkv_own, weights] + all_tokens,
        waits=[],
        cost=6,
    )
    got, far = heads_sum(keep, send)
    kv_parts = column_grads("key_value_grad", dkv_own, [send])
    sum_wkv, kv_sent = reduce_few(kv_parts, direct, far, z_grads)
    stay = jnp.where(y == 0, z_grads[0], z_grads[1])
    came = swap(jnp.where(y == 0, z_grads[1], z_grads[0]), 0, 1)
    kept_grad = jnp.where(at_home, stay, came)
    taken_grad = swap(jnp.where(at_home, came, stay), 1, 0)
    column_sums = jnp.concatenate([sum_wq.astype(bf16), sum_wkv.astype(bf16)], axis=2)
    by_row = lax.all_to_all(tie(column_sums, came), "heads", 0, 0, tiled=True)
    by_row = jnp.swapaxes(by_row, 0, 1).astype(f32)
    grad_wq = by_row[:, :, :Q_COLS].reshape(wrows, -1)
    grad_wk = by_row[:, :, Q_COLS : Q_COLS + K_COLS].reshape(wrows, -1)
    grad_wv = by_row[:, :, Q_COLS + K_COLS :].reshape(wrows, -1)
    grad_tokens = call(
        tokens_back_kernel,
        "tokens_back",
        [shaped((tok_dev, model), bf16)],
        [],
        [keep, got, far, tokens, gain_one, grad_hidden],
        waits=[taken_grad],
    )[0]
    router_back = router_grad[:experts]
    small_grads = small_sum(jnp.concatenate([gain_one_grad, gain_two_grad, router_back], axis=0), far)

    owned = unpack_half(kept_grad[None], drows, frows)
    fetched = unpack_half(taken_grad[None], drows, frows)
    grad_gate_w, grad_up_w, grad_down_w = [
        unhalve(o, f, core).astype(f32) for o, f in zip(owned, fetched)
    ]
    return (
        mixed,
        grad_tokens,
        small_grads[0],
        grad_wq,
        grad_wk,
        grad_wv,
        grad_wout,
        small_grads[1],
        small_grads[2 : 2 + experts].T,
        grad_gate_w[None],
        grad_up_w[None],
        grad_down_w[None],
    )


def solution(mesh):
    rows = P(("heads", "blk"), None)
    flat = P(("heads", "blk"))
    expert = P("heads", "blk", None)
    return jax.shard_map(
        shards,
        mesh=mesh,
        in_specs=(
            rows, rows, rows, P(), flat, rows, rows, rows, rows, flat, rows, expert, expert, expert,
        ),
        out_specs=(
            rows, rows, flat, rows, rows, rows, rows, flat, rows, expert, expert, expert,
        ),
        check_vma=False,
    )
```

```python
import functools

import jax
import jax.numpy as jnp
from jax import lax
from jax.experimental import pallas as pl
from jax.experimental.pallas import tpu as pltpu
from jax.sharding import PartitionSpec as P

QUERY_HEADS = 24
KEY_VALUE_HEADS = 8
HEAD_WIDTH = 64
CAP = 96
HEADS = 4
GROUP = QUERY_HEADS // KEY_VALUE_HEADS
KV_LOCAL = KEY_VALUE_HEADS // HEADS
Q_LOCAL = KV_LOCAL * GROUP
Q_COLS = Q_LOCAL * HEAD_WIDTH
K_COLS = KV_LOCAL * HEAD_WIDTH
STEP = 256

epsilon_norm = 1e-05
highest = lax.Precision.HIGHEST
masked_score = -1e30
bf16 = jnp.bfloat16
f32 = jnp.float32
BOTH = ("heads", "blk")
VMEM_LIMIT = 60 * 1024 * 1024
LANES = 256


def swap(value, heads_bits, blk_bits):
    count, blocks = lax.axis_size("heads"), lax.axis_size("blk")
    pairs = []
    for i in range(count * blocks):
        h, b = divmod(i, blocks)
        pairs.append((i, (h ^ heads_bits) * blocks + (b ^ blk_bits)))
    return lax.ppermute(value, BOTH, pairs)


def heads_gather(value):
    far = swap(value, 2, 0)
    near = swap(value, 1, 0)
    return jnp.stack([value, near, far, swap(far, 1, 0)])


def heads_reduce(parts):
    got = swap(jnp.stack([parts[1], parts[3]]), 1, 0)
    onward = (parts[2].astype(f32) + got[1].astype(f32)).astype(parts.dtype)
    far = swap(onward, 2, 0)
    return parts[0].astype(f32) + got[0].astype(f32) + far.astype(f32)


def ring_gather(value, *waits):
    pieces = []
    for k in range(lax.axis_size("blk") // 2):
        if k and k <= len(waits):
            value = tie(value, *waits[k - 1])
        value = ring_step(value) if k else value
        pieces += [value, swap(value, 0, 1)]
    return pieces


def reduce_pieces(evens, odds, wait):
    half = len(evens)
    total, sent = None, []
    for g, stack in enumerate(odds):
        got = swap(stack, 0, 1)
        for i in range(stack.shape[0]):
            zr = half - 1 - (g * (half // 2) + i)
            here = evens[zr].astype(f32) + got[i].astype(f32)
            if zr:
                sent.append(here.astype(bf16))
                here = swap(tie(sent[-1], wait), 0, 2 * zr).astype(f32)
            total = here if total is None else total + here
    return total, sent


def gather_few(value):
    column = [value] + [swap(value, 0, r) for r in range(2, lax.axis_size("blk"), 2)]
    beside = swap(jnp.stack(column), 0, 1)
    pieces = []
    for k, piece in enumerate(column):
        pieces += [piece, beside[k]]
    return pieces


def blk_gather(value):
    blocks = lax.axis_size("blk")
    if blocks > 8:
        whole = lax.all_gather(value, "blk", axis=0, tiled=False)
        return jnp.take(whole, lax.axis_index("blk") ^ jnp.arange(blocks), axis=0)
    pieces = [None] * blocks
    for r in range(0, blocks, 2):
        piece = swap(value, 0, r) if r else value
        pieces[r] = piece
        pieces[r + 1] = swap(piece, 0, 1)
    return jnp.stack(pieces)


def blk_reduce(parts):
    blocks = lax.axis_size("blk")
    if blocks > 8:
        whole = jnp.take(parts, lax.axis_index("blk") ^ jnp.arange(blocks), axis=0)
        return lax.psum_scatter(whole, "blk", scatter_dimension=0, tiled=False).astype(f32)
    total = None
    for r in range(blocks - 2, -1, -2):
        got = swap(parts[r + 1], 0, 1)
        here = parts[r].astype(f32) + got.astype(f32)
        if r:
            here = swap(here.astype(parts.dtype), 0, r).astype(f32)
        total = here if total is None else total + here
    return total


def blk_gather_few(value):
    blocks = lax.axis_size("blk")
    if blocks > 8:
        return blk_gather(value)
    column = jnp.stack([value] + [swap(value, 0, r) for r in range(2, blocks, 2)])
    both = jnp.stack([column, swap(column, 0, 1)], axis=1)
    return both.reshape((blocks,) + value.shape)


def reduce_few(parts, direct, *waits):
    if not direct:
        return lax.psum_scatter(parts, "blk", scatter_dimension=0, tiled=False).astype(f32), parts
    got = swap(parts[1], 0, 1)
    here = parts[0].astype(f32) + got.astype(f32)
    sent = here.astype(parts.dtype)
    if waits:
        sent = tie(sent, *waits)
    total = here[0]
    for k in range(1, parts.shape[1]):
        total = total + swap(sent[k], 0, 2 * k).astype(f32)
    return total, sent


def reduce_ring(parts, direct, *waits):
    if not direct:
        return lax.psum_scatter(parts, "blk", scatter_dimension=0, tiled=False).astype(f32)
    got = swap(parts[1], 0, 1)
    here = parts[0].astype(f32) + got.astype(f32)
    moving = here[-1].astype(parts.dtype)
    if waits:
        moving = tie(moving, *waits)
    for k in range(parts.shape[1] - 2, -1, -1):
        total = ring_step(moving).astype(f32) + here[k]
        moving = total.astype(parts.dtype)
    return total


def blk_unshuffle(pieces):
    blocks = pieces.shape[0]
    b = lax.axis_index("blk")
    return jnp.stack(
        [lax.dynamic_index_in_dim(pieces, b ^ i, 0, keepdims=False) for i in range(blocks)]
    )


RING = {0: 1, 1: 3, 3: 2, 2: 0}


def ring_step(value):
    count, blocks = lax.axis_size("heads"), lax.axis_size("blk")
    pairs = []
    for i in range(count * blocks):
        h, b = divmod(i, blocks)
        pairs.append((i, h * blocks + RING[b // 2] * 2 + b % 2))
    return lax.ppermute(value, BOTH, pairs)


def ring_place(z):
    return z ^ (z >> 1)


def ring_owner(z, k):
    place = (ring_place(z) - k) & 3
    return place ^ (place >> 1)


def z_groups(blocks):
    return [[i for i in range(blocks) if i % 2 == y] for y in range(2)]


def expand_heads(transposed, dtype):
    rows = []
    n = transposed.shape[1]
    zero = jnp.zeros((HEAD_WIDTH, n), dtype)
    for g in range(KV_LOCAL):
        columns = []
        for head in range(Q_LOCAL):
            if head // GROUP == g:
                columns.append(transposed[head * HEAD_WIDTH : (head + 1) * HEAD_WIDTH].astype(dtype))
            else:
                columns.append(zero)
        rows.append(jnp.concatenate(columns, axis=1))
    return jnp.concatenate(rows, axis=0)


def collapse_heads(wide, n):
    pieces = []
    for head in range(Q_LOCAL):
        g = head // GROUP
        pieces.append(wide[g * HEAD_WIDTH : (g + 1) * HEAD_WIDTH, head * n : (head + 1) * n])
    return jnp.concatenate(pieces, axis=0)


def key_rows(kv_ref, r, j, low, high):
    return jnp.concatenate(
        [kv_ref[r, j, :, low:high], kv_ref[r + 1, j, :, low:high]], axis=0
    )


def step_place(t, h, b, blocks, tok_dev, direct):
    half = blocks // 2
    owner_h = t // half
    owner_z = t % half
    j = owner_h ^ h
    z, y = b // 2, b % 2
    term = (owner_z ^ z) * 2
    if direct:
        piece = ((ring_place(z) - ring_place(owner_z)) & 3) * 2
    else:
        piece = term
    row = lax.broadcasted_iota(jnp.int32, (2 * tok_dev, 1), 0)
    base = (owner_h * blocks + owner_z * 2) * tok_dev
    second = row >= tok_dev
    position = base + jnp.where(
        second, row - tok_dev + (1 - y) * tok_dev, row + y * tok_dev
    )
    return piece, term, j, position


def fill_pieces(refs, whole_ref):
    for r, ref in enumerate(refs):
        whole_ref[r] = ref[...]


def by_pairs(low, high, work):
    def pair(u, unused):
        work([low + 2 * u, low + 2 * u + 1])
        return unused

    lax.fori_loop(0, (high - low) // 2, pair, 0)

    @pl.when((high - low) % 2 == 1)
    def rest():
        work([high - 1])


def attend_kernel(blocks, count, *refs):
    scal_ref, q_ref, start_ref = refs[:3]
    pieces = refs[3 : 3 + count]
    att_ref, lse_ref, top_ref, sum_ref, acc_ref = refs[3 + count : 8 + count]
    if count > 1:
        kv_ref = refs[8 + count]
        fill_pieces(pieces, kv_ref)
    else:
        kv_ref = pieces[0]
    tok_dev = q_ref.shape[1]
    h, b = scal_ref[0], scal_ref[1]

    def one(j, unused):
        block = (h ^ j) * blocks + b
        queries = (q_ref[j].astype(f32) * 0.125).T
        wide = expand_heads(queries, bf16)
        lane = lax.broadcasted_iota(jnp.int32, (1, tok_dev), 1)
        query_pos = jnp.concatenate([block * tok_dev + lane] * Q_LOCAL, axis=1)
        start = jnp.concatenate([start_ref[j]] * Q_LOCAL, axis=1)
        top_ref[...] = jnp.full(top_ref.shape, masked_score, f32)
        sum_ref[...] = jnp.zeros(sum_ref.shape, f32)
        acc_ref[...] = jnp.zeros(acc_ref.shape, f32)

        def work(steps):
            places = [step_place(t, h, b, blocks, tok_dev, count > 1) for t in steps]
            keys = jnp.concatenate([key_rows(kv_ref, p[0], p[2], 0, K_COLS) for p in places], axis=0)
            values = jnp.concatenate(
                [key_rows(kv_ref, p[0], p[2], K_COLS, 2 * K_COLS) for p in places], axis=0
            )
            position = jnp.concatenate([p[3] for p in places], axis=0)
            scores = lax.dot_general(keys, wide, (((1,), (0,)), ((), ())), preferred_element_type=f32)
            allowed = (position >= start) & (position <= query_pos)
            scores = jnp.where(allowed, scores, masked_score)
            old = top_ref[...]
            new = jnp.maximum(old, jnp.max(scores, axis=0, keepdims=True))
            rescale = jnp.exp(old - new)
            weights = jnp.exp(scores - new)
            top_ref[...] = new
            sum_ref[...] = sum_ref[...] * rescale + jnp.sum(weights, axis=0, keepdims=True)
            acc_ref[...] = acc_ref[...] * rescale + lax.dot_general(
                values, weights.astype(bf16), (((0,), (0,)), ((), ())), preferred_element_type=f32
            )

        by_pairs(scal_ref[2 + j], block // 2 + 1, work)
        total = sum_ref[...]
        out = collapse_heads(acc_ref[...] / total, tok_dev)
        att_ref[j] = out.T.astype(bf16)
        lse_ref[j] = top_ref[...] + jnp.log(total)
        return unused

    lax.fori_loop(0, HEADS, one, 0)


SMEM = pl.BlockSpec(memory_space=pltpu.SMEM)
VMEM = pl.BlockSpec(memory_space=pltpu.VMEM)
ANY = pl.BlockSpec(memory_space=pl.ANY)


def room_for(arrays, scratch):
    held = sum(a.size * a.dtype.itemsize for a in arrays)
    for s in scratch:
        size = 1
        for n in s.shape:
            size *= n
        held += size * jnp.dtype(s.dtype).itemsize
    return min(VMEM_LIMIT, held + held // 8 + (14 << 20))


def shaped(shape, dtype):
    return jax.ShapeDtypeStruct(shape, dtype)


def call(kernel, name, outs, scalars, arrays, scratch=(), waits=(), cost=4):
    scalars, arrays, waits = list(scalars), list(arrays), list(waits)
    used = len(scalars) + len(arrays)

    def body(*refs):
        kernel(*(refs[:used] + refs[used + len(waits) :]))

    return pl.pallas_call(
        body,
        out_shape=tuple(outs),
        in_specs=[SMEM] * len(scalars) + [VMEM] * len(arrays) + [ANY] * len(waits),
        out_specs=tuple([VMEM] * len(outs)),
        scratch_shapes=list(scratch),
        compiler_params=pltpu.CompilerParams(
            vmem_limit_bytes=room_for(arrays + list(outs), scratch)
        ),
        cost_estimate=pl.CostEstimate(flops=cost * 1000000000, bytes_accessed=1 << 20, transcendentals=0),
        name=name,
    )(*scalars, *arrays, *waits)


def tie(value, *waits):
    def body(*refs):
        pass

    return pl.pallas_call(
        body,
        out_shape=shaped(value.shape, value.dtype),
        in_specs=[ANY] * (1 + len(waits)),
        out_specs=ANY,
        input_output_aliases={0: 0},
        name="tie",
    )(value, *waits)


def attend(scal, queries, kv, start, blocks, waits=()):
    tok_dev = queries.shape[1]
    wide = Q_LOCAL * tok_dev
    scratch = [
        pltpu.VMEM((1, wide), f32),
        pltpu.VMEM((1, wide), f32),
        pltpu.VMEM((K_COLS, wide), f32),
    ]
    if len(kv) > 1:
        scratch.append(pltpu.VMEM((blocks,) + kv[0].shape, bf16))
    return call(
        functools.partial(attend_kernel, blocks, len(kv)),
        "attend",
        (
            shaped((HEADS, tok_dev, Q_COLS), bf16),
            shaped((HEADS, 1, wide), f32),
        ),
        [scal],
        [queries, start] + list(kv),
        scratch,
        waits=waits,
        cost=12,
    )


def attend_back_kernel(blocks, count, *refs):
    scal_ref, q_ref, start_ref, att_ref, lse_ref, wo_ref = refs[:6]
    branch = refs[6:10]
    pieces = refs[10 : 10 + count]
    dq_ref = refs[10 + count]
    n_outs = count // 2 + 2 if count > 1 else 1
    outs = refs[11 + count : 11 + count + n_outs]
    acc_ref, term_ref, grad_ref = refs[11 + count + n_outs : 14 + count + n_outs]
    if count > 1:
        kv_ref = refs[14 + count + n_outs]
        fill_pieces(pieces, kv_ref)
    else:
        kv_ref = pieces[0]
    tok_dev = q_ref.shape[1]
    h, b = scal_ref[0], scal_ref[1]
    term_ref[...] = jnp.zeros(term_ref.shape, f32)
    for j in range(HEADS):
        grad_ref[j] = dot_nt(branch[j][...], wo_ref[...]).astype(bf16)

    def one(j, unused):
        block = (h ^ j) * blocks + b
        wide = expand_heads((q_ref[j].astype(f32) * 0.125).T, bf16)
        grad_t = grad_ref[j].astype(f32).T
        wide_grad = expand_heads(grad_t, bf16)
        product = grad_t * att_ref[j].astype(f32).T
        delta = jnp.concatenate(
            [
                jnp.sum(product[head * HEAD_WIDTH : (head + 1) * HEAD_WIDTH], axis=0, keepdims=True)
                for head in range(Q_LOCAL)
            ],
            axis=1,
        )
        lse = lse_ref[j]
        lane = lax.broadcasted_iota(jnp.int32, (1, tok_dev), 1)
        query_pos = jnp.concatenate([block * tok_dev + lane] * Q_LOCAL, axis=1)
        start = jnp.concatenate([start_ref[j]] * Q_LOCAL, axis=1)
        acc_ref[...] = jnp.zeros(acc_ref.shape, f32)

        def work(steps):
            places = [step_place(t, h, b, blocks, tok_dev, count > 1) for t in steps]
            keys = jnp.concatenate([key_rows(kv_ref, p[0], p[2], 0, K_COLS) for p in places], axis=0)
            values = jnp.concatenate(
                [key_rows(kv_ref, p[0], p[2], K_COLS, 2 * K_COLS) for p in places], axis=0
            )
            position = jnp.concatenate([p[3] for p in places], axis=0)
            scores = lax.dot_general(keys, wide, (((1,), (0,)), ((), ())), preferred_element_type=f32)
            allowed = (position >= start) & (position <= query_pos)
            probs = jnp.exp(jnp.where(allowed, scores - lse, masked_score))
            grad_probs = lax.dot_general(
                values, wide_grad, (((1,), (0,)), ((), ())), preferred_element_type=f32
            )
            grad_scores = (probs * (grad_probs - delta)).astype(bf16)
            acc_ref[...] += lax.dot_general(
                keys, grad_scores, (((0,), (0,)), ((), ())), preferred_element_type=f32
            )
            key_term = lax.dot_general(
                grad_scores, wide, (((1,), (1,)), ((), ())), preferred_element_type=f32
            )
            value_term = lax.dot_general(
                probs.astype(bf16), wide_grad, (((1,), (1,)), ((), ())), preferred_element_type=f32
            )
            both = jnp.concatenate([key_term, value_term], axis=1)
            for i, (unused_piece, term, jk, unused_position) in enumerate(places):
                low = 2 * i * tok_dev
                term_ref[term, jk] += both[low : low + tok_dev]
                term_ref[term + 1, jk] += both[low + tok_dev : low + 2 * tok_dev]

        by_pairs(scal_ref[2 + j], block // 2 + 1, work)
        dq_ref[j] = (collapse_heads(acc_ref[...], tok_dev) * 0.125).T.astype(bf16)
        return unused

    lax.fori_loop(0, HEADS, one, 0)
    if count > 1:
        half = count // 2
        for zr in range(half):
            outs[zr][...] = term_ref[2 * zr].astype(bf16)
            back = half - 1 - zr
            outs[half + back // (half // 2)][back % (half // 2)] = term_ref[2 * zr + 1].astype(bf16)
    else:
        outs[0][...] = term_ref[...].astype(bf16)


def attend_back(scal, queries, kv, start, att, lse, output_w, branch, blocks, waits=()):
    tok_dev = queries.shape[1]
    wide = Q_LOCAL * tok_dev
    whole = (blocks, HEADS, tok_dev, 2 * K_COLS)
    scratch = [
        pltpu.VMEM((K_COLS, wide), f32),
        pltpu.VMEM(whole, f32),
        pltpu.VMEM((HEADS, tok_dev, Q_COLS), bf16),
    ]
    terms = [shaped(whole, bf16)]
    if len(kv) > 1:
        scratch.append(pltpu.VMEM(whole, bf16))
        half = blocks // 2
        terms = [shaped(whole[1:], bf16)] * half + [shaped((half // 2,) + whole[1:], bf16)] * 2
    outs = call(
        functools.partial(attend_back_kernel, blocks, len(kv)),
        "attend_back",
        [shaped((HEADS, tok_dev, Q_COLS), bf16)] + terms,
        [scal],
        [queries, start, att, lse, output_w] + list(branch) + list(kv),
        scratch,
        waits=waits,
        cost=17,
    )
    return outs[0], outs[1:]


def dot(a, b):
    return jnp.dot(a, b, preferred_element_type=f32)


def dot_tn(a, b):
    return lax.dot_general(a, b, (((0,), (0,)), ((), ())), preferred_element_type=f32)


def dot_nt(a, b):
    return lax.dot_general(a, b, (((1,), (1,)), ((), ())), preferred_element_type=f32)


def split(value, count):
    terms = []
    for unused in range(count):
        term = value.astype(bf16)
        terms.append(term)
        value = value - term.astype(f32)
    return terms


def own_rows(b, r, source, wrows, blocks):
    return pl.ds(pl.multiple_of((source * blocks + (b ^ r)) * wrows, 16), wrows)


W_COLS = Q_COLS + 2 * K_COLS
SMALL = 128


def project_kernel(blocks, count, *refs):
    scal_ref = refs[0]
    tokens = refs[1:5]
    pieces = refs[5 : 5 + count]
    normed_ref, q_ref, kv_ref, gains_ref, router_ref = refs[5 + count : 10 + count]
    w_ref = refs[10 + count] if count > 1 else pieces[0]
    b = scal_ref[1]
    if count > 1:
        wrows = pieces[0].shape[1]
        for r in range(count):
            for source in range(HEADS):
                owner = ring_owner(b // 2, r // 2) * 2 + (b % 2 ^ r % 2)
                low = pl.multiple_of((source * blocks + owner) * wrows, 16)
                w_ref[pl.ds(low, wrows), :] = pieces[r][source]
    small = w_ref[:, W_COLS:].astype(f32).T
    gains_ref[...] = small[:8]
    shifted = jnp.concatenate([small[2:], small[:2]], axis=0)
    row = lax.broadcasted_iota(jnp.int32, (SMALL, 1), 0)
    router_ref[...] = jnp.where(row < 4, shifted, 0.0).astype(bf16)
    gain = small[0:1]
    tok_dev = tokens[0].shape[0]
    for j in range(HEADS):
        value = tokens[j][...].astype(f32)
        inverse = lax.rsqrt(jnp.mean(value * value, axis=-1, keepdims=True) + epsilon_norm)
        normed_ref[j * tok_dev : (j + 1) * tok_dev, :] = (value * inverse * gain).astype(bf16)
    projected = dot(normed_ref[...], w_ref[:, :W_COLS]).astype(bf16)
    for j in range(HEADS):
        q_ref[j] = projected[j * tok_dev : (j + 1) * tok_dev, :Q_COLS]
        kv_ref[j] = projected[j * tok_dev : (j + 1) * tok_dev, Q_COLS:]


def project(scal, tokens, pieces, blocks, waits=()):
    tok_dev, model = tokens[0].shape
    outs = [
        shaped((HEADS * tok_dev, model), bf16),
        shaped((HEADS, tok_dev, Q_COLS), bf16),
        shaped((HEADS, tok_dev, 2 * K_COLS), bf16),
        shaped((8, model), f32),
        shaped((SMALL, model), bf16),
    ]
    if len(pieces) > 1:
        outs.append(shaped((model, W_COLS + SMALL), bf16))
    got = call(
        functools.partial(project_kernel, blocks, len(pieces)),
        "project",
        outs,
        [scal],
        list(tokens) + list(pieces),
        waits=waits,
    )
    return got[:5] + (got[5] if len(pieces) > 1 else pieces[0],)


def output_kernel(blocks, count, *refs):
    scal_ref, att_ref = refs[:2]
    pieces = refs[2 : 2 + count]
    keep_ref, send_ref = refs[2 + count : 4 + count]
    wo_ref = refs[4 + count] if count > 1 else pieces[0]
    b = scal_ref[1]
    if count > 1:
        wrows = pieces[0].shape[0]
        for r in range(count):
            wo_ref[own_rows(b, r, 0, wrows, blocks), :] = pieces[r][...]
    for j in range(HEADS):
        part = dot(att_ref[j], wo_ref[...]).astype(bf16)
        if j % 2:
            send_ref[j // 2] = part
        else:
            keep_ref[j // 2] = part


def output_parts(scal, att, pieces, model, blocks, waits):
    tok_dev = att.shape[1]
    outs = [shaped((2, tok_dev, model), bf16)] * 2
    if len(pieces) > 1:
        outs.append(shaped((Q_COLS, model), bf16))
    got = call(
        functools.partial(output_kernel, blocks, len(pieces)),
        "output_parts",
        outs,
        [scal],
        [att] + list(pieces),
        waits=waits,
    )
    return got[0], got[1], (got[2] if len(pieces) > 1 else pieces[0])


def heads_sum(keep, send):
    got = swap(send, 1, 0)
    onward = (keep[1].astype(f32) + got[1].astype(f32)).astype(bf16)
    return got, swap(onward, 2, 0)


def route_kernel(
    scal_ref, keep_ref, got_ref, far_ref, tokens_ref, gain_ref, router_ref, member_ref, table_ref, cot_ref,
    s0, s1, s2, s3, g0, g1, g2, g3, hidden_ref, nf_ref, gates_ref, slot_gate_ref, sent_ref, back_ref,
):
    hidden = (
        tokens_ref[...].astype(f32)
        + keep_ref[0].astype(f32)
        + got_ref[0].astype(f32)
        + far_ref[...].astype(f32)
    )
    hidden_ref[...] = hidden
    inverse = lax.rsqrt(jnp.mean(hidden * hidden, axis=-1, keepdims=True) + epsilon_norm)
    nf = (hidden * inverse * gain_ref[1:2, :]).astype(bf16)
    nf_ref[...] = nf
    logits = dot_nt(nf, router_ref[...])
    picked = member_ref[...] > 0
    peak = jnp.max(jnp.where(picked, logits, -jnp.inf), axis=-1, keepdims=True)
    raised = jnp.where(picked, jnp.exp(jnp.where(picked, logits - peak, 0.0)), 0.0)
    gates = raised / jnp.sum(raised, axis=-1, keepdims=True)
    gates_ref[...] = gates
    table = table_ref[...]
    sent = dot(table, nf).astype(bf16)
    spread = dot(table, cot_ref[...])
    slot_gates = sum(dot(table, term) for term in split(gates, 3))
    lane = lax.broadcasted_iota(jnp.int32, (CAP, slot_gates.shape[1]), 1)
    sent_ref[...] = sent
    for e in range(4):
        rows = slice(e * CAP, (e + 1) * CAP)
        column = jnp.sum(jnp.where(lane == e, slot_gates[rows], 0.0), axis=1, keepdims=True)
        slot_gate_ref[rows, :] = column
        back_ref[rows, :] = (spread[rows] * column).astype(bf16)
    for r, (s_ref, g_ref) in enumerate(((s0, g0), (s1, g1), (s2, g2), (s3, g3))):
        rows = slot_rows(own_place(scal_ref) ^ r)
        s_ref[...] = sent_ref[rows, :]
        g_ref[...] = back_ref[rows, :]


def gate_up(ref, drows):
    return jnp.concatenate(
        [ref[:, k * drows : (k + 1) * drows, :].reshape(-1, LANES) for k in range(4)], axis=1
    )


def down_half(ref, drows, frows):
    base = 4 * drows
    return jnp.concatenate(
        [ref[:, base + k * frows : base + (k + 1) * frows, :].reshape(-1, LANES) for k in range(3)],
        axis=1,
    )


def lanes(offset, size):
    return pl.ds(pl.multiple_of(offset, 128), size)


def fill_weights(scal_ref, refs, mine_ref, other_ref):
    z = scal_ref[1] // 2
    for pieces, whole_ref in ((refs[:4], mine_ref), (refs[4:], other_ref)):
        for k in range(4):
            for y in range(2):
                whole_ref[ring_owner(z, k) * 2 + y] = pieces[k][y]


def expert_kernel(drows, frows, direct, *refs):
    scal_ref = refs[0]
    if direct:
        p0, p1, p2, p3, gp_ref, up_ref, inner_ref, out_ref, mine_ref, other_ref = refs[13:]
        fill_weights(scal_ref, refs[5:13], mine_ref, other_ref)
    else:
        mine_ref, other_ref, p0, p1, p2, p3, gp_ref, up_ref, inner_ref, out_ref = refs[5:]
    fill_rows(scal_ref, refs[1:5], out_ref)
    core = scal_ref[0] % 2
    rows = out_ref[...]
    for side, ref in ((core, mine_ref), (1 - core, other_ref)):
        both = dot(rows, gate_up(ref, drows))
        gate, up = both[:, : 2 * LANES], both[:, 2 * LANES :]
        place = lanes(side * 2 * LANES, 2 * LANES)
        gp_ref[:, place] = gate
        up_ref[:, place] = up
        inner_ref[:, place] = (gate * jax.nn.sigmoid(gate) * up).astype(bf16)
    inner = inner_ref[...]
    for side, ref in ((core, mine_ref), (1 - core, other_ref)):
        out_ref[:, lanes(side * 3 * LANES, 3 * LANES)] = dot(inner, down_half(ref, drows, frows)).astype(bf16)
    for r, ref in enumerate((p0, p1, p2, p3)):
        ref[...] = out_ref[slot_rows(own_place(scal_ref) ^ r), :]


def own_place(scal_ref):
    return scal_ref[0] // 2 * 2 + scal_ref[1] % 2


def slot_rows(place):
    return pl.ds(pl.multiple_of(place * CAP, 16), CAP)


def fill_rows(scal_ref, refs, rows_ref):
    for r, ref in enumerate(refs):
        rows_ref[slot_rows(own_place(scal_ref) ^ r), :] = ref[...]


def weights_of(scal_ref, refs, scratch):
    if not scratch:
        return refs
    fill_weights(scal_ref, refs, *scratch)
    return scratch


def expert_back_kernel(drows, frows, count, *refs):
    scal_ref = refs[0]
    gp_ref, up_ref = refs[5:7]
    ggp_ref, gup_ref, grad_ref = refs[7 + count : 10 + count]
    mine_ref, other_ref = weights_of(scal_ref, refs[7 : 7 + count], refs[10 + count :])
    fill_rows(scal_ref, refs[1:5], grad_ref)
    core = scal_ref[0] % 2
    grad_inner = None
    for side, ref in ((core, mine_ref), (1 - core, other_ref)):
        term = dot_nt(grad_ref[:, lanes(side * 3 * LANES, 3 * LANES)], down_half(ref, drows, frows))
        grad_inner = term if grad_inner is None else grad_inner + term
    gate, up = gp_ref[...], up_ref[...]
    sig = jax.nn.sigmoid(gate)
    ggp_ref[...] = (grad_inner * up * sig * (1.0 + gate * (1.0 - sig))).astype(bf16)
    gup_ref[...] = (grad_inner * gate * sig).astype(bf16)


def expert_input_kernel(drows, frows, count, *refs):
    scal_ref, ggp_ref, gup_ref = refs[:3]
    p0, p1, p2, p3, grad_ref = refs[3 + count : 8 + count]
    mine_ref, other_ref = weights_of(scal_ref, refs[3 : 3 + count], refs[8 + count :])
    core = scal_ref[0] % 2
    total = None
    for side, ref in ((core, mine_ref), (1 - core, other_ref)):
        place = lanes(side * 2 * LANES, 2 * LANES)
        both = jnp.concatenate([ggp_ref[:, place], gup_ref[:, place]], axis=1)
        term = dot_nt(both, gate_up(ref, drows))
        total = term if total is None else total + term
    grad_ref[...] = total.astype(bf16)
    for r, ref in enumerate((p0, p1, p2, p3)):
        ref[...] = grad_ref[slot_rows(own_place(scal_ref) ^ r), :]


def expert_weights_kernel(
    drows, frows, blocks, own, scal_ref, x0, x1, x2, x3, g0, g1, g2, g3, inner_ref, ggp_ref, gup_ref, *rest
):
    if own:
        got_ref, out_ref, grad_ref, rows_ref = rest
    else:
        out_ref, grad_ref, rows_ref = rest
    core, z = scal_ref[0] % 2, scal_ref[1] // 2
    side = core if own else 1 - core
    fill_rows(scal_ref, (g0, g1, g2, g3), grad_ref)
    fill_rows(scal_ref, (x0, x1, x2, x3), rows_ref)
    rows = rows_ref[...]

    def put(low, height, term):
        for k in range(term.shape[1] // LANES):
            piece = term[:, k * LANES : (k + 1) * LANES].reshape(blocks // 2, 2, height, LANES)
            place = slice(low, low + height)
            for at in range(blocks // 2):
                step = (ring_place(at) - ring_place(z)) & 3 if blocks == 8 else at
                value = piece[at]
                if own:
                    value = value + got_ref[step, :, place, :].astype(f32)
                out_ref[step, :, place, :] = value.astype(bf16)
            low += height

    place = lanes(side * 2 * LANES, 2 * LANES)
    both = jnp.concatenate([ggp_ref[:, place], gup_ref[:, place]], axis=1)
    put(0, drows, dot_tn(rows, both))
    put(4 * drows, frows, dot_tn(inner_ref[...], grad_ref[:, lanes(side * 3 * LANES, 3 * LANES)]))


def combine_kernel(
    scal_ref, r0, r1, r2, r3, hidden_ref, nf_ref, gates_ref, slot_gate_ref, table_ref, cot_ref, router_ref,
    mixed_ref, grad_nf_ref, router_grad_ref, ret_ref,
):
    table = table_ref[...]
    fill_rows(scal_ref, (r0, r1, r2, r3), ret_ref)
    returned = ret_ref[...]
    scaled_rows = returned.astype(f32) * slot_gate_ref[...]
    mixed_ref[...] = (hidden_ref[...] + sum(dot_tn(table, t) for t in split(scaled_rows, 2))).astype(bf16)
    scored = dot_nt(returned, cot_ref[...]) * table.astype(f32)
    gates_t = gates_ref[...].T[:8]
    score_rows = [
        jnp.sum(scored[e * CAP : (e + 1) * CAP], axis=0, keepdims=True) for e in range(4)
    ]
    scores = jnp.concatenate(score_rows + [jnp.zeros((4, scored.shape[1]), f32)], axis=0)
    mean_gate = jnp.sum(gates_t * scores, axis=0, keepdims=True)
    grad_logits = gates_t * (scores - mean_gate)
    terms = split(grad_logits, 3)
    router_grad_ref[...] = sum(dot(t, nf_ref[...]) for t in terms)
    grad_nf_ref[...] = sum(dot_tn(t, router_ref[:8, :]) for t in terms)


def norm_back_kernel(
    scal_ref, b0, b1, b2, b3, hidden_ref, table_ref, cot_ref, gain_ref, part_ref,
    grad_hidden_ref, branch_ref, gain_grad_ref, back_ref,
):
    hidden = hidden_ref[...]
    fill_rows(scal_ref, (b0, b1, b2, b3), back_ref)
    grad_nf = dot_tn(table_ref[...], back_ref[...]) + part_ref[...]
    inverse = lax.rsqrt(jnp.mean(hidden * hidden, axis=-1, keepdims=True) + epsilon_norm)
    gain_grad_ref[...] = jnp.sum(grad_nf * hidden * inverse, axis=0, keepdims=True)
    scaled = grad_nf * gain_ref[1:2, :]
    grad_hidden = (
        cot_ref[...].astype(f32)
        + inverse * scaled
        - hidden * (inverse * inverse * inverse) * jnp.mean(scaled * hidden, axis=-1, keepdims=True)
    )
    grad_hidden_ref[...] = grad_hidden
    branch_ref[...] = grad_hidden.astype(bf16)


def late_grad_kernel(blocks, wrows, direct, scal_ref, normed_ref, dq_ref, att_ref, b0, b1, b2, b3, out_ref, q_ref, o_ref):
    b = scal_ref[1]
    flat = jnp.concatenate([dq_ref[j] for j in range(HEADS)], axis=0)
    q_ref[...] = dot_tn(normed_ref[...], flat).astype(bf16)
    total = None
    for j, ref in enumerate((b0, b1, b2, b3)):
        term = dot_tn(att_ref[j], ref[...])
        total = term if total is None else total + term
    o_ref[...] = total.astype(bf16)
    for r in range(blocks):
        owner = ring_owner(b // 2, -(r // 2)) * 2 + (b % 2 ^ r % 2)
        for source in range(HEADS):
            cols = slice(source * Q_COLS, (source + 1) * Q_COLS)
            if direct:
                low = pl.multiple_of((source * blocks + owner) * wrows, 16)
                out_ref[r % 2, r // 2, :wrows, cols] = q_ref[pl.ds(low, wrows), :]
            else:
                low = (source * blocks + r) * wrows
                out_ref[r, :wrows, cols] = q_ref[low : low + wrows, :]
        if direct:
            low = pl.multiple_of(owner * wrows, 16)
            out_ref[r % 2, r // 2, wrows:, :] = o_ref[pl.ds(low, wrows), :]
        else:
            out_ref[r, wrows:, :] = o_ref[r * wrows : (r + 1) * wrows, :]


def pair_shape(blocks, rest, direct):
    return ((2, blocks // 2) if direct else (blocks,)) + rest


def column_grad_kernel(blocks, wrows, direct, scal_ref, normed_ref, grad_ref, out_ref, hold_ref):
    b = scal_ref[1]
    flat = jnp.concatenate([grad_ref[j] for j in range(HEADS)], axis=0)
    hold_ref[...] = dot_tn(normed_ref[...], flat).astype(bf16)
    for r in range(blocks):
        for source in range(HEADS):
            if direct:
                out_ref[r % 2, r // 2, source] = hold_ref[own_rows(b, r, source, wrows, blocks), :]
            else:
                low = (source * blocks + r) * wrows
                out_ref[r, source] = hold_ref[low : low + wrows, :]


def normed_back_kernel(dq_ref, dkv_ref, w_ref, t0, t1, t2, t3, keep_ref, send_ref, gain_grad_ref):
    total = None
    for j, ref in enumerate((t0, t1, t2, t3)):
        part = dot_nt(dq_ref[j], w_ref[:, :Q_COLS]) + dot_nt(dkv_ref[j], w_ref[:, Q_COLS:W_COLS])
        value = ref[...].astype(f32)
        inverse = lax.rsqrt(jnp.mean(value * value, axis=-1, keepdims=True) + epsilon_norm)
        term = jnp.sum(part * (value * inverse), axis=0, keepdims=True)
        total = term if total is None else total + term
        if j % 2:
            send_ref[j // 2] = part.astype(bf16)
        else:
            keep_ref[j // 2] = part.astype(bf16)
    gain_grad_ref[...] = total


def tokens_back_kernel(keep_ref, got_ref, far_ref, tokens_ref, gain_ref, grad_hidden_ref, out_ref):
    grad_normed = keep_ref[0].astype(f32) + got_ref[0].astype(f32) + far_ref[...].astype(f32)
    value = tokens_ref[...].astype(f32)
    inverse = lax.rsqrt(jnp.mean(value * value, axis=-1, keepdims=True) + epsilon_norm)
    scaled = grad_normed * gain_ref[0:1, :]
    out_ref[...] = (
        grad_hidden_ref[...]
        + inverse * scaled
        - value * (inverse * inverse * inverse) * jnp.mean(scaled * value, axis=-1, keepdims=True)
    ).astype(bf16)


def small_sum(values, wait):
    devices = lax.axis_size("heads") * lax.axis_size("blk")
    n = values.shape[0]
    width = values.shape[1] // devices
    parts = jnp.transpose(values.reshape(n, devices, width), (1, 0, 2))
    padded = jnp.pad(parts, ((0, 0), (0, 8 - n), (0, 128 - width)))
    got = lax.all_to_all(tie(padded, wait), BOTH, 0, 0, tiled=True)
    return jnp.sum(got, axis=0)[:n, :width]


def halves(columns, core):
    half = columns.shape[1] // 2
    first, second = columns[:, :half], columns[:, half:]
    return jnp.where(core == 0, first, second), jnp.where(core == 0, second, first)


def unhalve(own, other, core):
    return jnp.concatenate(
        [jnp.where(core == 0, own, other), jnp.where(core == 0, other, own)], axis=1
    )


def unpack_half(buffer, drows, frows):
    def piece(low, high):
        return buffer[:, low:high].reshape(-1, LANES)

    matrices, base = [], 0
    for rows, count in ((drows, 2), (drows, 2), (frows, 3)):
        matrices.append(
            jnp.concatenate([piece(base + k * rows, base + (k + 1) * rows) for k in range(count)], axis=1)
        )
        base += rows * count
    return matrices


def pack_half(gate, up, down, count):
    pieces = []
    for matrix in (gate, up, down):
        rows = matrix.shape[0] // count
        for k in range(matrix.shape[1] // LANES):
            pieces.append(matrix[:, k * LANES : (k + 1) * LANES].reshape(count, rows, LANES))
    return jnp.concatenate(pieces, axis=1)


def shards(
    tokens,
    cotangent,
    routes,
    doc_lengths,
    attn_norm,
    w_query,
    key_weight,
    value_weight,
    w_output,
    ffn_norm,
    w_router,
    w_gate,
    w_up,
    w_down,
):
    blocks = lax.axis_size("blk")
    direct = blocks <= 8
    tok_dev, model = tokens.shape
    wrows = w_query.shape[0]
    drows = w_gate.shape[1]
    frows = w_down.shape[1]
    experts = w_router.shape[1]
    h, b = lax.axis_index("heads"), lax.axis_index("blk")
    core, x, y = h % 2, h // 2, b % 2
    zn = blocks // 2
    wide_cols = Q_COLS + 2 * K_COLS

    w_out = w_output.astype(bf16)
    if direct:
        wo_pieces = gather_few(w_out)
    else:
        wo_pieces = [lax.all_gather(w_out, "blk", axis=0, tiled=True)]

    far = swap(tokens, 2, 0)
    all_tokens = [tokens, swap(tokens, 1, 0), far, swap(far, 1, 0)]

    cut = [halves(m, core) for m in (w_gate[0].astype(bf16), w_up[0].astype(bf16), w_down[0].astype(bf16))]
    kept = pack_half(cut[0][0], cut[1][0], cut[2][0], 1)[0]
    given = pack_half(cut[0][1], cut[1][1], cut[2][1], 1)[0]
    at_home = core == y

    small_own = jnp.concatenate(
        [attn_norm.astype(bf16)[None], ffn_norm.astype(bf16)[None], w_router.astype(bf16).T], axis=0
    )
    small_own = jnp.pad(small_own.T, ((0, 0), (0, SMALL - 2 - experts)))
    heads_cat = jnp.concatenate(
        [
            w_query.astype(bf16).reshape(wrows, HEADS, Q_COLS),
            key_weight.astype(bf16).reshape(wrows, HEADS, K_COLS),
            value_weight.astype(bf16).reshape(wrows, HEADS, K_COLS),
            jnp.broadcast_to(small_own[:, None, :], (wrows, HEADS, SMALL)),
        ],
        axis=2,
    )
    by_head = lax.all_to_all(jnp.swapaxes(heads_cat, 0, 1), "heads", 0, 0, tiled=True)
    taken = swap(given, 1, 0)
    stay = jnp.where(at_home, kept, taken)
    leave = jnp.where(at_home, taken, kept)
    came = swap(leave, 0, 1)
    column = jnp.stack([jnp.where(y == 0, stay, came), jnp.where(y == 0, came, stay)])
    if direct:
        w_pieces = ring_gather(by_head, [far, all_tokens[1]], [wo_pieces[k] for k in (2, 4, 6)] + [all_tokens[3]])
        mine = [column, ring_step(tie(column, w_pieces[6]))]
    else:
        whole = lax.all_gather(by_head, "blk", axis=1, tiled=False)
        w_pieces = [whole.reshape(model, W_COLS + SMALL)]
        mine = lax.all_gather(column, "blk", axis=0, tiled=False, axis_index_groups=z_groups(blocks))
        mine = mine.reshape((blocks,) + kept.shape)

    ends = jnp.cumsum(doc_lengths)
    block_of = (h ^ jnp.arange(HEADS, dtype=jnp.int32)) * blocks + b
    query_pos = block_of[:, None] * tok_dev + jnp.arange(tok_dev, dtype=jnp.int32)[None, :]
    start = jnp.max(
        jnp.where(ends[None, None, :] <= query_pos[:, :, None], ends[None, None, :], 0), axis=2
    ).astype(jnp.int32)
    scal = jnp.concatenate(
        [
            jnp.stack([h, b]).astype(jnp.int32),
            start[:, 0] // (2 * tok_dev),
        ]
    )
    start = start[:, None, :]

    member = jnp.sum((routes[:, :, None] == jnp.arange(experts)[None, None, :]).astype(f32), axis=1)
    lower = (jnp.arange(tok_dev)[:, None] > jnp.arange(tok_dev)[None, :]).astype(bf16)
    rank = dot(lower, member.astype(bf16))
    slot = jnp.arange(CAP, dtype=f32)
    table = (
        ((rank.T[:, None, :] == slot[None, :, None]) & (member.T[:, None, :] > 0))
        .astype(bf16)
        .reshape(experts * CAP, tok_dev)
    )
    member = jnp.pad(member, ((0, 0), (0, 128 - experts)))

    normed, queries, kv_own, gains, router_all, weights = project(
        scal, all_tokens, w_pieces, blocks, [table, member, start]
    )
    if direct:
        kv = ring_gather(kv_own)
        mine.append(ring_step(tie(mine[1], kv[2])))
        mine.append(ring_step(mine[2]))
    else:
        kv = [blk_gather(kv_own)]
    att, lse = attend(scal, queries, kv, start, blocks)
    keep, send, output_w = output_parts(scal, att, wo_pieces, model, blocks, [])
    got, far = heads_sum(keep, send)
    seconds = [swap(piece, 1, 0) for piece in mine[:3]] if direct else []
    slot = shaped((CAP, model), bf16)
    hold = pltpu.VMEM((experts * CAP, model), bf16)
    routed = call(
        route_kernel,
        "route",
        [slot] * 8
        + [
            shaped((tok_dev, model), f32),
            shaped((tok_dev, model), bf16),
            shaped((tok_dev, 128), f32),
            shaped((experts * CAP, 1), f32),
        ],
        [scal],
        [keep, got, far, tokens, gains, router_all, member, table, cotangent],
        [hold, hold],
        waits=seconds,
        cost=3,
    )
    sent, grad_sent = routed[:4], routed[4:8]
    hidden, normed_ffn, gates, slot_gate = routed[8:]

    def to_experts(pieces):
        return [pieces[0]] + [swap(pieces[r], r // 2 * 2, r % 2) for r in range(1, experts)]

    arrived = to_experts(sent)
    grad_arrived = to_experts(grad_sent)
    if direct:
        weights_in = mine + seconds + [swap(tie(mine[3], *arrived[1:]), 1, 0)]
        gathered = [pltpu.VMEM((blocks,) + kept.shape, bf16)] * 2
    else:
        mine = tie(mine, sent[0])
        other = swap(mine, 1, 0)
        weights_in, gathered = [mine, other], []
    rows_all = experts * CAP
    ff = frows * blocks
    fwd = call(
        functools.partial(expert_kernel, drows, frows, direct),
        "expert",
        [slot] * 4
        + [shaped((rows_all, ff), f32), shaped((rows_all, ff), f32), shaped((rows_all, ff), bf16)],
        [scal],
        arrived + weights_in,
        [hold] + gathered,
        cost=2,
    )
    gate_pre, up_pre, inner = fwd[4:7]
    returned = to_experts(fwd[:4])
    grad_pre = call(
        functools.partial(expert_back_kernel, drows, frows, len(weights_in)),
        "expert_back",
        [shaped((rows_all, ff), bf16)] * 2,
        [scal],
        grad_arrived + [gate_pre, up_pre] + weights_in,
        [hold] + gathered,
        cost=2,
    )
    grad_pre = list(grad_pre)

    def expert_weights(own, extra, waits=()):
        return call(
            functools.partial(expert_weights_kernel, drows, frows, blocks, own),
            "expert_weights",
            [shaped((zn, 2) + kept.shape, bf16)],
            [scal],
            arrived + grad_arrived + [inner] + grad_pre + extra,
            [hold, hold],
            waits=waits,
            cost=1,
        )[0]

    grads_other = expert_weights(False, [])
    grads_met = swap(grads_other, 1, 0)
    grad_in = call(
        functools.partial(expert_input_kernel, drows, frows, len(weights_in)),
        "expert_input",
        [slot] * 4,
        [scal],
        grad_pre + weights_in,
        [hold] + gathered,
        waits=[grads_other],
        cost=2,
    )
    grad_returned = to_experts(grad_in)
    chip_grads = expert_weights(True, [grads_met], [grad_in[0]] + returned[1:])

    mixed, part_nf, router_grad = call(
        combine_kernel,
        "combine",
        [
            shaped((tok_dev, model), bf16),
            shaped((tok_dev, model), f32),
            shaped((8, model), f32),
        ],
        [scal],
        returned + [hidden, normed_ffn, gates, slot_gate, table, cotangent, router_all],
        [hold],
        waits=[chip_grads],
        cost=1,
    )
    later = [mixed]
    if direct:

        def met(moving, k):
            return (moving.astype(f32) + chip_grads[k].astype(f32)).astype(bf16)

        second_sum = met(ring_step(chip_grads[3]), 2)
        third_sum = met(ring_step(second_sum), 1)
        later_still = [second_sum]
    else:
        z_grads = lax.psum_scatter(
            chip_grads, "blk", scatter_dimension=0, tiled=False, axis_index_groups=z_groups(blocks)
        )
        later_still = []
    grad_hidden, branch, gain_two_grad = call(
        norm_back_kernel,
        "norm_back",
        [
            shaped((tok_dev, model), f32),
            shaped((tok_dev, model), bf16),
            shaped((1, model), f32),
        ],
        [scal],
        grad_returned + [hidden, table, cotangent, gains, part_nf],
        [hold],
        waits=later,
    )

    far_branch = swap(branch, 2, 0)
    branches = [branch, swap(branch, 1, 0), far_branch, swap(far_branch, 1, 0)]
    dq, dkv = attend_back(scal, queries, kv, start, att, lse, output_w, branches, blocks, later_still)
    if direct:
        dkv_own, onward = reduce_pieces(dkv[:zn], dkv[zn:], third_sum)
    else:
        dkv_own, onward = blk_reduce(dkv[0]), [dq]
    dkv_own = dkv_own.astype(bf16)
    if direct:
        z_grads = met(ring_step(tie(third_sum, dkv_own)), 0)

    def column_grads(name, grad, waits=()):
        cols = grad.shape[2]
        return call(
            functools.partial(column_grad_kernel, blocks, wrows, direct),
            name,
            [shaped(pair_shape(blocks, (HEADS, wrows, cols), direct), bf16)],
            [scal],
            [normed, grad],
            [pltpu.VMEM((model, cols), bf16)],
            waits=waits,
        )[0]

    late_parts = call(
        functools.partial(late_grad_kernel, blocks, wrows, direct),
        "late_grad",
        [shaped(pair_shape(blocks, (2 * wrows, model), direct), bf16)],
        [scal],
        [normed, dq, att] + branches,
        [pltpu.VMEM((model, Q_COLS), bf16), pltpu.VMEM((Q_COLS, model), bf16)],
        waits=[dq],
    )[0]
    late_parts = tie(late_parts, *(onward[:2] + ([third_sum] if direct else [])))
    late_sums = reduce_ring(late_parts, direct, dkv_own)
    grad_wout = late_sums[wrows:]
    sum_wq = jnp.swapaxes(late_sums[:wrows].reshape(wrows, HEADS, Q_COLS), 0, 1)
    keep, send, gain_one_grad = call(
        normed_back_kernel,
        "normed_back",
        [shaped((2, tok_dev, model), bf16)] * 2 + [shaped((1, model), f32)],
        [],
        [dq, dkv_own, weights] + all_tokens,
        waits=[],
        cost=6,
    )
    got, far = heads_sum(keep, send)
    kv_parts = column_grads("key_value_grad", dkv_own, [send])
    sum_wkv, kv_sent = reduce_few(kv_parts, direct, far, z_grads)
    stay = jnp.where(y == 0, z_grads[0], z_grads[1])
    came = swap(jnp.where(y == 0, z_grads[1], z_grads[0]), 0, 1)
    kept_grad = jnp.where(at_home, stay, came)
    taken_grad = swap(jnp.where(at_home, came, stay), 1, 0)
    column_sums = jnp.concatenate([sum_wq.astype(bf16), sum_wkv.astype(bf16)], axis=2)
    by_row = lax.all_to_all(tie(column_sums, came), "heads", 0, 0, tiled=True)
    by_row = jnp.swapaxes(by_row, 0, 1).astype(f32)
    grad_wq = by_row[:, :, :Q_COLS].reshape(wrows, -1)
    grad_wk = by_row[:, :, Q_COLS : Q_COLS + K_COLS].reshape(wrows, -1)
    grad_wv = by_row[:, :, Q_COLS + K_COLS :].reshape(wrows, -1)
    grad_tokens = call(
        tokens_back_kernel,
        "tokens_back",
        [shaped((tok_dev, model), bf16)],
        [],
        [keep, got, far, tokens, gains, grad_hidden],
        waits=[taken_grad],
    )[0]
    router_back = router_grad[:experts]
    small_grads = small_sum(jnp.concatenate([gain_one_grad, gain_two_grad, router_back], axis=0), far)

    owned = unpack_half(kept_grad[None], drows, frows)
    fetched = unpack_half(taken_grad[None], drows, frows)
    grad_gate_w, grad_up_w, grad_down_w = [
        unhalve(o, f, core).astype(f32) for o, f in zip(owned, fetched)
    ]
    return (
        mixed,
        grad_tokens,
        small_grads[0],
        grad_wq,
        grad_wk,
        grad_wv,
        grad_wout,
        small_grads[1],
        small_grads[2 : 2 + experts].T,
        grad_gate_w[None],
        grad_up_w[None],
        grad_down_w[None],
    )


def solution(mesh):
    rows = P(("heads", "blk"), None)
    flat = P(("heads", "blk"))
    expert = P("heads", "blk", None)
    return jax.shard_map(
        shards,
        mesh=mesh,
        in_specs=(
            rows, rows, rows, P(), flat, rows, rows, rows, rows, flat, rows, expert, expert, expert,
        ),
        out_specs=(
            rows, rows, flat, rows, rows, rows, rows, flat, rows, expert, expert, expert,
        ),
        check_vma=False,
    )
```

```python
import functools

import jax
import jax.numpy as jnp
from jax import lax
from jax.experimental import pallas as pl
from jax.experimental.pallas import tpu as pltpu
from jax.sharding import PartitionSpec as P

QUERY_HEADS = 24
KEY_VALUE_HEADS = 8
HEAD_WIDTH = 64
CAP = 96
HEADS = 4
GROUP = QUERY_HEADS // KEY_VALUE_HEADS
KV_LOCAL = KEY_VALUE_HEADS // HEADS
Q_LOCAL = KV_LOCAL * GROUP
Q_COLS = Q_LOCAL * HEAD_WIDTH
K_COLS = KV_LOCAL * HEAD_WIDTH
STEP = 256

epsilon_norm = 1e-05
highest = lax.Precision.HIGHEST
masked_score = -1e30
bf16 = jnp.bfloat16
f32 = jnp.float32
BOTH = ("heads", "blk")
VMEM_LIMIT = 60 * 1024 * 1024
LANES = 256


def swap(value, heads_bits, blk_bits):
    count, blocks = lax.axis_size("heads"), lax.axis_size("blk")
    pairs = []
    for i in range(count * blocks):
        h, b = divmod(i, blocks)
        pairs.append((i, (h ^ heads_bits) * blocks + (b ^ blk_bits)))
    return lax.ppermute(value, BOTH, pairs)


def heads_gather(value):
    far = swap(value, 2, 0)
    near = swap(value, 1, 0)
    return jnp.stack([value, near, far, swap(far, 1, 0)])


def heads_reduce(parts):
    got = swap(jnp.stack([parts[1], parts[3]]), 1, 0)
    onward = (parts[2].astype(f32) + got[1].astype(f32)).astype(parts.dtype)
    far = swap(onward, 2, 0)
    return parts[0].astype(f32) + got[0].astype(f32) + far.astype(f32)


def ring_gather(value, *waits):
    pieces = []
    for k in range(lax.axis_size("blk") // 2):
        if k and k <= len(waits):
            value = tie(value, *waits[k - 1])
        value = ring_step(value) if k else value
        pieces += [value, swap(value, 0, 1)]
    return pieces


def reduce_pieces(evens, odds, wait):
    half = len(evens)
    total, sent = None, []
    for g, stack in enumerate(odds):
        got = swap(stack, 0, 1)
        for i in range(stack.shape[0]):
            zr = half - 1 - (g * (half // 2) + i)
            here = evens[zr].astype(f32) + got[i].astype(f32)
            if zr:
                sent.append(here.astype(bf16))
                here = swap(tie(sent[-1], wait), 0, 2 * zr).astype(f32)
            total = here if total is None else total + here
    return total, sent


def gather_few(value):
    column = [value] + [swap(value, 0, r) for r in range(2, lax.axis_size("blk"), 2)]
    beside = swap(jnp.stack(column), 0, 1)
    pieces = []
    for k, piece in enumerate(column):
        pieces += [piece, beside[k]]
    return pieces


def blk_gather(value):
    blocks = lax.axis_size("blk")
    if blocks > 8:
        whole = lax.all_gather(value, "blk", axis=0, tiled=False)
        return jnp.take(whole, lax.axis_index("blk") ^ jnp.arange(blocks), axis=0)
    pieces = [None] * blocks
    for r in range(0, blocks, 2):
        piece = swap(value, 0, r) if r else value
        pieces[r] = piece
        pieces[r + 1] = swap(piece, 0, 1)
    return jnp.stack(pieces)


def blk_reduce(parts):
    blocks = lax.axis_size("blk")
    if blocks > 8:
        whole = jnp.take(parts, lax.axis_index("blk") ^ jnp.arange(blocks), axis=0)
        return lax.psum_scatter(whole, "blk", scatter_dimension=0, tiled=False).astype(f32)
    total = None
    for r in range(blocks - 2, -1, -2):
        got = swap(parts[r + 1], 0, 1)
        here = parts[r].astype(f32) + got.astype(f32)
        if r:
            here = swap(here.astype(parts.dtype), 0, r).astype(f32)
        total = here if total is None else total + here
    return total


def blk_gather_few(value):
    blocks = lax.axis_size("blk")
    if blocks > 8:
        return blk_gather(value)
    column = jnp.stack([value] + [swap(value, 0, r) for r in range(2, blocks, 2)])
    both = jnp.stack([column, swap(column, 0, 1)], axis=1)
    return both.reshape((blocks,) + value.shape)


def reduce_few(parts, direct, *waits):
    if not direct:
        return lax.psum_scatter(parts, "blk", scatter_dimension=0, tiled=False).astype(f32), parts
    got = swap(parts[1], 0, 1)
    here = parts[0].astype(f32) + got.astype(f32)
    sent = here.astype(parts.dtype)
    if waits:
        sent = tie(sent, *waits)
    total = here[0]
    for k in range(1, parts.shape[1]):
        total = total + swap(sent[k], 0, 2 * k).astype(f32)
    return total, sent


def reduce_ring(parts, direct, *waits):
    if not direct:
        return lax.psum_scatter(parts, "blk", scatter_dimension=0, tiled=False).astype(f32)
    got = swap(parts[1], 0, 1)
    here = parts[0].astype(f32) + got.astype(f32)
    moving = here[-1].astype(parts.dtype)
    if waits:
        moving = tie(moving, *waits)
    for k in range(parts.shape[1] - 2, -1, -1):
        total = ring_step(moving).astype(f32) + here[k]
        moving = total.astype(parts.dtype)
    return total


def blk_unshuffle(pieces):
    blocks = pieces.shape[0]
    b = lax.axis_index("blk")
    return jnp.stack(
        [lax.dynamic_index_in_dim(pieces, b ^ i, 0, keepdims=False) for i in range(blocks)]
    )


RING = {0: 1, 1: 3, 3: 2, 2: 0}


def ring_step(value):
    count, blocks = lax.axis_size("heads"), lax.axis_size("blk")
    pairs = []
    for i in range(count * blocks):
        h, b = divmod(i, blocks)
        pairs.append((i, h * blocks + RING[b // 2] * 2 + b % 2))
    return lax.ppermute(value, BOTH, pairs)


def ring_place(z):
    return z ^ (z >> 1)


def ring_owner(z, k):
    place = (ring_place(z) - k) & 3
    return place ^ (place >> 1)


def z_groups(blocks):
    return [[i for i in range(blocks) if i % 2 == y] for y in range(2)]


def expand_heads(transposed, dtype):
    rows = []
    n = transposed.shape[1]
    zero = jnp.zeros((HEAD_WIDTH, n), dtype)
    for g in range(KV_LOCAL):
        columns = []
        for head in range(Q_LOCAL):
            if head // GROUP == g:
                columns.append(transposed[head * HEAD_WIDTH : (head + 1) * HEAD_WIDTH].astype(dtype))
            else:
                columns.append(zero)
        rows.append(jnp.concatenate(columns, axis=1))
    return jnp.concatenate(rows, axis=0)


def collapse_heads(wide, n):
    pieces = []
    for head in range(Q_LOCAL):
        g = head // GROUP
        pieces.append(wide[g * HEAD_WIDTH : (g + 1) * HEAD_WIDTH, head * n : (head + 1) * n])
    return jnp.concatenate(pieces, axis=0)


def key_rows(kv_ref, r, j, low, high):
    return jnp.concatenate(
        [kv_ref[r, j, :, low:high], kv_ref[r + 1, j, :, low:high]], axis=0
    )


def step_place(t, h, b, blocks, tok_dev, direct):
    half = blocks // 2
    owner_h = t // half
    owner_z = t % half
    j = owner_h ^ h
    z, y = b // 2, b % 2
    term = (owner_z ^ z) * 2
    if direct:
        piece = ((ring_place(z) - ring_place(owner_z)) & 3) * 2
    else:
        piece = term
    row = lax.broadcasted_iota(jnp.int32, (2 * tok_dev, 1), 0)
    base = (owner_h * blocks + owner_z * 2) * tok_dev
    second = row >= tok_dev
    position = base + jnp.where(
        second, row - tok_dev + (1 - y) * tok_dev, row + y * tok_dev
    )
    return piece, term, j, position


def fill_pieces(refs, whole_ref):
    for r, ref in enumerate(refs):
        whole_ref[r] = ref[...]


def by_pairs(low, high, work):
    count = high - low

    def four(u, unused):
        work([low + 4 * u + k for k in range(4)])
        return unused

    lax.fori_loop(0, count // 4, four, 0)

    @pl.when(count % 4 >= 2)
    def two():
        first = low + count // 4 * 4
        work([first, first + 1])

    @pl.when(count % 2 == 1)
    def rest():
        work([high - 1])


def attend_kernel(blocks, count, *refs):
    scal_ref, q_ref, start_ref = refs[:3]
    pieces = refs[3 : 3 + count]
    att_ref, lse_ref, top_ref, sum_ref, acc_ref = refs[3 + count : 8 + count]
    if count > 1:
        kv_ref = refs[8 + count]
        fill_pieces(pieces, kv_ref)
    else:
        kv_ref = pieces[0]
    tok_dev = q_ref.shape[1]
    h, b = scal_ref[0], scal_ref[1]

    def one(j, unused):
        block = (h ^ j) * blocks + b
        queries = (q_ref[j].astype(f32) * 0.125).T
        wide = expand_heads(queries, bf16)
        lane = lax.broadcasted_iota(jnp.int32, (1, tok_dev), 1)
        query_pos = jnp.concatenate([block * tok_dev + lane] * Q_LOCAL, axis=1)
        start = jnp.concatenate([start_ref[j]] * Q_LOCAL, axis=1)
        top_ref[...] = jnp.full(top_ref.shape, masked_score, f32)
        sum_ref[...] = jnp.zeros(sum_ref.shape, f32)
        acc_ref[...] = jnp.zeros(acc_ref.shape, f32)

        def work(steps):
            places = [step_place(t, h, b, blocks, tok_dev, count > 1) for t in steps]
            keys = jnp.concatenate([key_rows(kv_ref, p[0], p[2], 0, K_COLS) for p in places], axis=0)
            values = jnp.concatenate(
                [key_rows(kv_ref, p[0], p[2], K_COLS, 2 * K_COLS) for p in places], axis=0
            )
            position = jnp.concatenate([p[3] for p in places], axis=0)
            scores = lax.dot_general(keys, wide, (((1,), (0,)), ((), ())), preferred_element_type=f32)
            allowed = (position >= start) & (position <= query_pos)
            scores = jnp.where(allowed, scores, masked_score)
            old = top_ref[...]
            new = jnp.maximum(old, jnp.max(scores, axis=0, keepdims=True))
            rescale = jnp.exp(old - new)
            weights = jnp.exp(scores - new)
            top_ref[...] = new
            sum_ref[...] = sum_ref[...] * rescale + jnp.sum(weights, axis=0, keepdims=True)
            acc_ref[...] = acc_ref[...] * rescale + lax.dot_general(
                values, weights.astype(bf16), (((0,), (0,)), ((), ())), preferred_element_type=f32
            )

        by_pairs(scal_ref[2 + j], block // 2 + 1, work)
        total = sum_ref[...]
        out = collapse_heads(acc_ref[...] / total, tok_dev)
        att_ref[j] = out.T.astype(bf16)
        lse_ref[j] = top_ref[...] + jnp.log(total)
        return unused

    for j in range(HEADS):
        one(j, 0)


SMEM = pl.BlockSpec(memory_space=pltpu.SMEM)
VMEM = pl.BlockSpec(memory_space=pltpu.VMEM)
ANY = pl.BlockSpec(memory_space=pl.ANY)


def room_for(arrays, scratch):
    held = sum(a.size * a.dtype.itemsize for a in arrays)
    for s in scratch:
        size = 1
        for n in s.shape:
            size *= n
        held += size * jnp.dtype(s.dtype).itemsize
    return min(VMEM_LIMIT, held + held // 8 + (14 << 20))


def shaped(shape, dtype):
    return jax.ShapeDtypeStruct(shape, dtype)


def call(kernel, name, outs, scalars, arrays, scratch=(), waits=(), cost=4):
    scalars, arrays, waits = list(scalars), list(arrays), list(waits)
    used = len(scalars) + len(arrays)

    def body(*refs):
        kernel(*(refs[:used] + refs[used + len(waits) :]))

    return pl.pallas_call(
        body,
        out_shape=tuple(outs),
        in_specs=[SMEM] * len(scalars) + [VMEM] * len(arrays) + [ANY] * len(waits),
        out_specs=tuple([VMEM] * len(outs)),
        scratch_shapes=list(scratch),
        compiler_params=pltpu.CompilerParams(
            vmem_limit_bytes=room_for(arrays + list(outs), scratch)
        ),
        cost_estimate=pl.CostEstimate(flops=cost * 1000000000, bytes_accessed=1 << 20, transcendentals=0),
        name=name,
    )(*scalars, *arrays, *waits)


def tie(value, *waits):
    def body(*refs):
        pass

    return pl.pallas_call(
        body,
        out_shape=shaped(value.shape, value.dtype),
        in_specs=[ANY] * (1 + len(waits)),
        out_specs=ANY,
        input_output_aliases={0: 0},
        name="tie",
    )(value, *waits)


def attend(scal, queries, kv, start, blocks, waits=()):
    tok_dev = queries.shape[1]
    wide = Q_LOCAL * tok_dev
    scratch = [
        pltpu.VMEM((1, wide), f32),
        pltpu.VMEM((1, wide), f32),
        pltpu.VMEM((K_COLS, wide), f32),
    ]
    if len(kv) > 1:
        scratch.append(pltpu.VMEM((blocks,) + kv[0].shape, bf16))
    return call(
        functools.partial(attend_kernel, blocks, len(kv)),
        "attend",
        (
            shaped((HEADS, tok_dev, Q_COLS), bf16),
            shaped((HEADS, 1, wide), f32),
        ),
        [scal],
        [queries, start] + list(kv),
        scratch,
        waits=waits,
        cost=12,
    )


def attend_back_kernel(blocks, count, *refs):
    scal_ref, q_ref, start_ref, att_ref, lse_ref, wo_ref = refs[:6]
    branch = refs[6:10]
    pieces = refs[10 : 10 + count]
    dq_ref = refs[10 + count]
    n_outs = count // 2 + 2 if count > 1 else 1
    outs = refs[11 + count : 11 + count + n_outs]
    acc_ref, term_ref, grad_ref = refs[11 + count + n_outs : 14 + count + n_outs]
    if count > 1:
        kv_ref = refs[14 + count + n_outs]
        fill_pieces(pieces, kv_ref)
    else:
        kv_ref = pieces[0]
    tok_dev = q_ref.shape[1]
    h, b = scal_ref[0], scal_ref[1]
    term_ref[...] = jnp.zeros(term_ref.shape, f32)
    for j in range(HEADS):
        grad_ref[j] = dot_nt(branch[j][...], wo_ref[...]).astype(bf16)

    def one(j, unused):
        block = (h ^ j) * blocks + b
        wide = expand_heads((q_ref[j].astype(f32) * 0.125).T, bf16)
        grad_t = grad_ref[j].astype(f32).T
        wide_grad = expand_heads(grad_t, bf16)
        product = grad_t * att_ref[j].astype(f32).T
        delta = jnp.concatenate(
            [
                jnp.sum(product[head * HEAD_WIDTH : (head + 1) * HEAD_WIDTH], axis=0, keepdims=True)
                for head in range(Q_LOCAL)
            ],
            axis=1,
        )
        lse = lse_ref[j]
        lane = lax.broadcasted_iota(jnp.int32, (1, tok_dev), 1)
        query_pos = jnp.concatenate([block * tok_dev + lane] * Q_LOCAL, axis=1)
        start = jnp.concatenate([start_ref[j]] * Q_LOCAL, axis=1)
        acc_ref[...] = jnp.zeros(acc_ref.shape, f32)

        def work(steps):
            places = [step_place(t, h, b, blocks, tok_dev, count > 1) for t in steps]
            keys = jnp.concatenate([key_rows(kv_ref, p[0], p[2], 0, K_COLS) for p in places], axis=0)
            values = jnp.concatenate(
                [key_rows(kv_ref, p[0], p[2], K_COLS, 2 * K_COLS) for p in places], axis=0
            )
            position = jnp.concatenate([p[3] for p in places], axis=0)
            scores = lax.dot_general(keys, wide, (((1,), (0,)), ((), ())), preferred_element_type=f32)
            allowed = (position >= start) & (position <= query_pos)
            probs = jnp.exp(jnp.where(allowed, scores - lse, masked_score))
            grad_probs = lax.dot_general(
                values, wide_grad, (((1,), (0,)), ((), ())), preferred_element_type=f32
            )
            grad_scores = (probs * (grad_probs - delta)).astype(bf16)
            acc_ref[...] += lax.dot_general(
                keys, grad_scores, (((0,), (0,)), ((), ())), preferred_element_type=f32
            )
            key_term = lax.dot_general(
                grad_scores, wide, (((1,), (1,)), ((), ())), preferred_element_type=f32
            )
            value_term = lax.dot_general(
                probs.astype(bf16), wide_grad, (((1,), (1,)), ((), ())), preferred_element_type=f32
            )
            both = jnp.concatenate([key_term, value_term], axis=1)
            for i, (unused_piece, term, jk, unused_position) in enumerate(places):
                low = 2 * i * tok_dev
                term_ref[term, jk] += both[low : low + tok_dev]
                term_ref[term + 1, jk] += both[low + tok_dev : low + 2 * tok_dev]

        by_pairs(scal_ref[2 + j], block // 2 + 1, work)
        dq_ref[j] = (collapse_heads(acc_ref[...], tok_dev) * 0.125).T.astype(bf16)
        return unused

    lax.fori_loop(0, HEADS, one, 0)
    if count > 1:
        half = count // 2
        for zr in range(half):
            outs[zr][...] = term_ref[2 * zr].astype(bf16)
            back = half - 1 - zr
            outs[half + back // (half // 2)][back % (half // 2)] = term_ref[2 * zr + 1].astype(bf16)
    else:
        outs[0][...] = term_ref[...].astype(bf16)


def attend_back(scal, queries, kv, start, att, lse, output_w, branch, blocks, waits=()):
    tok_dev = queries.shape[1]
    wide = Q_LOCAL * tok_dev
    whole = (blocks, HEADS, tok_dev, 2 * K_COLS)
    scratch = [
        pltpu.VMEM((K_COLS, wide), f32),
        pltpu.VMEM(whole, f32),
        pltpu.VMEM((HEADS, tok_dev, Q_COLS), bf16),
    ]
    terms = [shaped(whole, bf16)]
    if len(kv) > 1:
        scratch.append(pltpu.VMEM(whole, bf16))
        half = blocks // 2
        terms = [shaped(whole[1:], bf16)] * half + [shaped((half // 2,) + whole[1:], bf16)] * 2
    outs = call(
        functools.partial(attend_back_kernel, blocks, len(kv)),
        "attend_back",
        [shaped((HEADS, tok_dev, Q_COLS), bf16)] + terms,
        [scal],
        [queries, start, att, lse, output_w] + list(branch) + list(kv),
        scratch,
        waits=waits,
        cost=17,
    )
    return outs[0], outs[1:]


def dot(a, b):
    return jnp.dot(a, b, preferred_element_type=f32)


def dot_tn(a, b):
    return lax.dot_general(a, b, (((0,), (0,)), ((), ())), preferred_element_type=f32)


def dot_nt(a, b):
    return lax.dot_general(a, b, (((1,), (1,)), ((), ())), preferred_element_type=f32)


def split(value, count):
    terms = []
    for unused in range(count):
        term = value.astype(bf16)
        terms.append(term)
        value = value - term.astype(f32)
    return terms


def own_rows(b, r, source, wrows, blocks):
    return pl.ds(pl.multiple_of((source * blocks + (b ^ r)) * wrows, 16), wrows)


W_COLS = Q_COLS + 2 * K_COLS
SMALL = 128


def project_kernel(blocks, count, *refs):
    scal_ref = refs[0]
    tokens = refs[1:5]
    pieces = refs[5 : 5 + count]
    normed_ref, q_ref, kv_ref, gains_ref, router_ref = refs[5 + count : 10 + count]
    w_ref = refs[10 + count] if count > 1 else pieces[0]
    b = scal_ref[1]
    if count > 1:
        wrows = pieces[0].shape[1]
        for r in range(count):
            for source in range(HEADS):
                owner = ring_owner(b // 2, r // 2) * 2 + (b % 2 ^ r % 2)
                low = pl.multiple_of((source * blocks + owner) * wrows, 16)
                w_ref[pl.ds(low, wrows), :] = pieces[r][source]
    small = w_ref[:, W_COLS:].astype(f32).T
    gains_ref[...] = small[:8]
    shifted = jnp.concatenate([small[2:], small[:2]], axis=0)
    row = lax.broadcasted_iota(jnp.int32, (SMALL, 1), 0)
    router_ref[...] = jnp.where(row < 4, shifted, 0.0).astype(bf16)
    gain = small[0:1]
    tok_dev = tokens[0].shape[0]
    for j in range(HEADS):
        value = tokens[j][...].astype(f32)
        inverse = lax.rsqrt(jnp.mean(value * value, axis=-1, keepdims=True) + epsilon_norm)
        normed_ref[j * tok_dev : (j + 1) * tok_dev, :] = (value * inverse * gain).astype(bf16)
    projected = dot(normed_ref[...], w_ref[:, :W_COLS]).astype(bf16)
    for j in range(HEADS):
        q_ref[j] = projected[j * tok_dev : (j + 1) * tok_dev, :Q_COLS]
        kv_ref[j] = projected[j * tok_dev : (j + 1) * tok_dev, Q_COLS:]


def project(scal, tokens, pieces, blocks, waits=()):
    tok_dev, model = tokens[0].shape
    outs = [
        shaped((HEADS * tok_dev, model), bf16),
        shaped((HEADS, tok_dev, Q_COLS), bf16),
        shaped((HEADS, tok_dev, 2 * K_COLS), bf16),
        shaped((8, model), f32),
        shaped((SMALL, model), bf16),
    ]
    if len(pieces) > 1:
        outs.append(shaped((model, W_COLS + SMALL), bf16))
    got = call(
        functools.partial(project_kernel, blocks, len(pieces)),
        "project",
        outs,
        [scal],
        list(tokens) + list(pieces),
        waits=waits,
    )
    return got[:5] + (got[5] if len(pieces) > 1 else pieces[0],)


def output_kernel(blocks, count, *refs):
    scal_ref, att_ref = refs[:2]
    pieces = refs[2 : 2 + count]
    keep_ref, send_ref = refs[2 + count : 4 + count]
    wo_ref = refs[4 + count] if count > 1 else pieces[0]
    b = scal_ref[1]
    if count > 1:
        wrows = pieces[0].shape[0]
        for r in range(count):
            wo_ref[own_rows(b, r, 0, wrows, blocks), :] = pieces[r][...]
    for j in range(HEADS):
        part = dot(att_ref[j], wo_ref[...]).astype(bf16)
        if j % 2:
            send_ref[j // 2] = part
        else:
            keep_ref[j // 2] = part


def output_parts(scal, att, pieces, model, blocks, waits):
    tok_dev = att.shape[1]
    outs = [shaped((2, tok_dev, model), bf16)] * 2
    if len(pieces) > 1:
        outs.append(shaped((Q_COLS, model), bf16))
    got = call(
        functools.partial(output_kernel, blocks, len(pieces)),
        "output_parts",
        outs,
        [scal],
        [att] + list(pieces),
        waits=waits,
    )
    return got[0], got[1], (got[2] if len(pieces) > 1 else pieces[0])


def heads_sum(keep, send):
    got = swap(send, 1, 0)
    onward = (keep[1].astype(f32) + got[1].astype(f32)).astype(bf16)
    return got, swap(onward, 2, 0)


def route_kernel(
    scal_ref, keep_ref, got_ref, far_ref, tokens_ref, gain_ref, router_ref, member_ref, table_ref, cot_ref,
    s0, s1, s2, s3, g0, g1, g2, g3, hidden_ref, nf_ref, gates_ref, slot_gate_ref, sent_ref, back_ref,
):
    hidden = (
        tokens_ref[...].astype(f32)
        + keep_ref[0].astype(f32)
        + got_ref[0].astype(f32)
        + far_ref[...].astype(f32)
    )
    hidden_ref[...] = hidden
    inverse = lax.rsqrt(jnp.mean(hidden * hidden, axis=-1, keepdims=True) + epsilon_norm)
    nf = (hidden * inverse * gain_ref[1:2, :]).astype(bf16)
    nf_ref[...] = nf
    logits = dot_nt(nf, router_ref[...])
    picked = member_ref[...] > 0
    peak = jnp.max(jnp.where(picked, logits, -jnp.inf), axis=-1, keepdims=True)
    raised = jnp.where(picked, jnp.exp(jnp.where(picked, logits - peak, 0.0)), 0.0)
    gates = raised / jnp.sum(raised, axis=-1, keepdims=True)
    gates_ref[...] = gates
    table = table_ref[...]
    sent = dot(table, nf).astype(bf16)
    spread = dot(table, cot_ref[...])
    slot_gates = sum(dot(table, term) for term in split(gates, 3))
    lane = lax.broadcasted_iota(jnp.int32, (CAP, slot_gates.shape[1]), 1)
    sent_ref[...] = sent
    for e in range(4):
        rows = slice(e * CAP, (e + 1) * CAP)
        column = jnp.sum(jnp.where(lane == e, slot_gates[rows], 0.0), axis=1, keepdims=True)
        slot_gate_ref[rows, :] = column
        back_ref[rows, :] = (spread[rows] * column).astype(bf16)
    for r, (s_ref, g_ref) in enumerate(((s0, g0), (s1, g1), (s2, g2), (s3, g3))):
        rows = slot_rows(own_place(scal_ref) ^ r)
        s_ref[...] = sent_ref[rows, :]
        g_ref[...] = back_ref[rows, :]


def gate_up(ref, drows):
    return jnp.concatenate(
        [ref[:, k * drows : (k + 1) * drows, :].reshape(-1, LANES) for k in range(4)], axis=1
    )


def down_half(ref, drows, frows):
    base = 4 * drows
    return jnp.concatenate(
        [ref[:, base + k * frows : base + (k + 1) * frows, :].reshape(-1, LANES) for k in range(3)],
        axis=1,
    )


def lanes(offset, size):
    return pl.ds(pl.multiple_of(offset, 128), size)


def fill_weights(scal_ref, refs, mine_ref, other_ref):
    z = scal_ref[1] // 2
    for pieces, whole_ref in ((refs[:4], mine_ref), (refs[4:], other_ref)):
        for k in range(4):
            for y in range(2):
                whole_ref[ring_owner(z, k) * 2 + y] = pieces[k][y]


def expert_kernel(drows, frows, direct, *refs):
    scal_ref = refs[0]
    if direct:
        p0, p1, p2, p3, gp_ref, up_ref, inner_ref, out_ref, mine_ref, other_ref = refs[13:]
        fill_weights(scal_ref, refs[5:13], mine_ref, other_ref)
    else:
        mine_ref, other_ref, p0, p1, p2, p3, gp_ref, up_ref, inner_ref, out_ref = refs[5:]
    fill_rows(scal_ref, refs[1:5], out_ref)
    core = scal_ref[0] % 2
    rows = out_ref[...]
    for side, ref in ((core, mine_ref), (1 - core, other_ref)):
        both = dot(rows, gate_up(ref, drows))
        gate, up = both[:, : 2 * LANES], both[:, 2 * LANES :]
        place = lanes(side * 2 * LANES, 2 * LANES)
        gp_ref[:, place] = gate
        up_ref[:, place] = up
        inner_ref[:, place] = (gate * jax.nn.sigmoid(gate) * up).astype(bf16)
    inner = inner_ref[...]
    for side, ref in ((core, mine_ref), (1 - core, other_ref)):
        out_ref[:, lanes(side * 3 * LANES, 3 * LANES)] = dot(inner, down_half(ref, drows, frows)).astype(bf16)
    for r, ref in enumerate((p0, p1, p2, p3)):
        ref[...] = out_ref[slot_rows(own_place(scal_ref) ^ r), :]


def own_place(scal_ref):
    return scal_ref[0] // 2 * 2 + scal_ref[1] % 2


def slot_rows(place):
    return pl.ds(pl.multiple_of(place * CAP, 16), CAP)


def fill_rows(scal_ref, refs, rows_ref):
    for r, ref in enumerate(refs):
        rows_ref[slot_rows(own_place(scal_ref) ^ r), :] = ref[...]


def weights_of(scal_ref, refs, scratch):
    if not scratch:
        return refs
    fill_weights(scal_ref, refs, *scratch)
    return scratch


def expert_back_kernel(drows, frows, count, *refs):
    scal_ref = refs[0]
    gp_ref, up_ref = refs[5:7]
    ggp_ref, gup_ref, grad_ref = refs[7 + count : 10 + count]
    mine_ref, other_ref = weights_of(scal_ref, refs[7 : 7 + count], refs[10 + count :])
    fill_rows(scal_ref, refs[1:5], grad_ref)
    core = scal_ref[0] % 2
    grad_inner = None
    for side, ref in ((core, mine_ref), (1 - core, other_ref)):
        term = dot_nt(grad_ref[:, lanes(side * 3 * LANES, 3 * LANES)], down_half(ref, drows, frows))
        grad_inner = term if grad_inner is None else grad_inner + term
    gate, up = gp_ref[...], up_ref[...]
    sig = jax.nn.sigmoid(gate)
    ggp_ref[...] = (grad_inner * up * sig * (1.0 + gate * (1.0 - sig))).astype(bf16)
    gup_ref[...] = (grad_inner * gate * sig).astype(bf16)


def expert_input_kernel(drows, frows, count, *refs):
    scal_ref, ggp_ref, gup_ref = refs[:3]
    p0, p1, p2, p3, grad_ref = refs[3 + count : 8 + count]
    mine_ref, other_ref = weights_of(scal_ref, refs[3 : 3 + count], refs[8 + count :])
    core = scal_ref[0] % 2
    total = None
    for side, ref in ((core, mine_ref), (1 - core, other_ref)):
        place = lanes(side * 2 * LANES, 2 * LANES)
        both = jnp.concatenate([ggp_ref[:, place], gup_ref[:, place]], axis=1)
        term = dot_nt(both, gate_up(ref, drows))
        total = term if total is None else total + term
    grad_ref[...] = total.astype(bf16)
    for r, ref in enumerate((p0, p1, p2, p3)):
        ref[...] = grad_ref[slot_rows(own_place(scal_ref) ^ r), :]


def expert_weights_kernel(
    drows, frows, blocks, own, scal_ref, x0, x1, x2, x3, g0, g1, g2, g3, inner_ref, ggp_ref, gup_ref, *rest
):
    if own:
        got_ref, out_ref, grad_ref, rows_ref = rest
    else:
        out_ref, grad_ref, rows_ref = rest
    core, z = scal_ref[0] % 2, scal_ref[1] // 2
    side = core if own else 1 - core
    fill_rows(scal_ref, (g0, g1, g2, g3), grad_ref)
    fill_rows(scal_ref, (x0, x1, x2, x3), rows_ref)
    rows = rows_ref[...]

    def put(low, height, term):
        for k in range(term.shape[1] // LANES):
            piece = term[:, k * LANES : (k + 1) * LANES].reshape(blocks // 2, 2, height, LANES)
            place = slice(low, low + height)
            for at in range(blocks // 2):
                step = (ring_place(at) - ring_place(z)) & 3 if blocks == 8 else at
                value = piece[at]
                if own:
                    value = value + got_ref[step, :, place, :].astype(f32)
                out_ref[step, :, place, :] = value.astype(bf16)
            low += height

    place = lanes(side * 2 * LANES, 2 * LANES)
    both = jnp.concatenate([ggp_ref[:, place], gup_ref[:, place]], axis=1)
    put(0, drows, dot_tn(rows, both))
    put(4 * drows, frows, dot_tn(inner_ref[...], grad_ref[:, lanes(side * 3 * LANES, 3 * LANES)]))


def combine_kernel(
    scal_ref, r0, r1, r2, r3, hidden_ref, nf_ref, gates_ref, slot_gate_ref, table_ref, cot_ref, router_ref,
    mixed_ref, grad_nf_ref, router_grad_ref, ret_ref,
):
    table = table_ref[...]
    fill_rows(scal_ref, (r0, r1, r2, r3), ret_ref)
    returned = ret_ref[...]
    scaled_rows = returned.astype(f32) * slot_gate_ref[...]
    mixed_ref[...] = (hidden_ref[...] + sum(dot_tn(table, t) for t in split(scaled_rows, 2))).astype(bf16)
    scored = dot_nt(returned, cot_ref[...]) * table.astype(f32)
    gates_t = gates_ref[...].T[:8]
    score_rows = [
        jnp.sum(scored[e * CAP : (e + 1) * CAP], axis=0, keepdims=True) for e in range(4)
    ]
    scores = jnp.concatenate(score_rows + [jnp.zeros((4, scored.shape[1]), f32)], axis=0)
    mean_gate = jnp.sum(gates_t * scores, axis=0, keepdims=True)
    grad_logits = gates_t * (scores - mean_gate)
    terms = split(grad_logits, 3)
    router_grad_ref[...] = sum(dot(t, nf_ref[...]) for t in terms)
    grad_nf_ref[...] = sum(dot_tn(t, router_ref[:8, :]) for t in terms)


def norm_back_kernel(
    scal_ref, b0, b1, b2, b3, hidden_ref, table_ref, cot_ref, gain_ref, part_ref,
    grad_hidden_ref, branch_ref, gain_grad_ref, back_ref,
):
    hidden = hidden_ref[...]
    fill_rows(scal_ref, (b0, b1, b2, b3), back_ref)
    grad_nf = dot_tn(table_ref[...], back_ref[...]) + part_ref[...]
    inverse = lax.rsqrt(jnp.mean(hidden * hidden, axis=-1, keepdims=True) + epsilon_norm)
    gain_grad_ref[...] = jnp.sum(grad_nf * hidden * inverse, axis=0, keepdims=True)
    scaled = grad_nf * gain_ref[1:2, :]
    grad_hidden = (
        cot_ref[...].astype(f32)
        + inverse * scaled
        - hidden * (inverse * inverse * inverse) * jnp.mean(scaled * hidden, axis=-1, keepdims=True)
    )
    grad_hidden_ref[...] = grad_hidden
    branch_ref[...] = grad_hidden.astype(bf16)


def late_grad_kernel(blocks, wrows, direct, scal_ref, normed_ref, dq_ref, att_ref, b0, b1, b2, b3, out_ref, q_ref, o_ref):
    b = scal_ref[1]
    flat = jnp.concatenate([dq_ref[j] for j in range(HEADS)], axis=0)
    q_ref[...] = dot_tn(normed_ref[...], flat).astype(bf16)
    total = None
    for j, ref in enumerate((b0, b1, b2, b3)):
        term = dot_tn(att_ref[j], ref[...])
        total = term if total is None else total + term
    o_ref[...] = total.astype(bf16)
    for r in range(blocks):
        owner = ring_owner(b // 2, -(r // 2)) * 2 + (b % 2 ^ r % 2)
        for source in range(HEADS):
            cols = slice(source * Q_COLS, (source + 1) * Q_COLS)
            if direct:
                low = pl.multiple_of((source * blocks + owner) * wrows, 16)
                out_ref[r % 2, r // 2, :wrows, cols] = q_ref[pl.ds(low, wrows), :]
            else:
                low = (source * blocks + r) * wrows
                out_ref[r, :wrows, cols] = q_ref[low : low + wrows, :]
        if direct:
            low = pl.multiple_of(owner * wrows, 16)
            out_ref[r % 2, r // 2, wrows:, :] = o_ref[pl.ds(low, wrows), :]
        else:
            out_ref[r, wrows:, :] = o_ref[r * wrows : (r + 1) * wrows, :]


def pair_shape(blocks, rest, direct):
    return ((2, blocks // 2) if direct else (blocks,)) + rest


def column_grad_kernel(blocks, wrows, direct, scal_ref, normed_ref, grad_ref, out_ref, hold_ref):
    b = scal_ref[1]
    flat = jnp.concatenate([grad_ref[j] for j in range(HEADS)], axis=0)
    hold_ref[...] = dot_tn(normed_ref[...], flat).astype(bf16)
    for r in range(blocks):
        for source in range(HEADS):
            if direct:
                out_ref[r % 2, r // 2, source] = hold_ref[own_rows(b, r, source, wrows, blocks), :]
            else:
                low = (source * blocks + r) * wrows
                out_ref[r, source] = hold_ref[low : low + wrows, :]


def normed_back_kernel(dq_ref, dkv_ref, w_ref, t0, t1, t2, t3, keep_ref, send_ref, gain_grad_ref):
    total = None
    for j, ref in enumerate((t0, t1, t2, t3)):
        part = dot_nt(dq_ref[j], w_ref[:, :Q_COLS]) + dot_nt(dkv_ref[j], w_ref[:, Q_COLS:W_COLS])
        value = ref[...].astype(f32)
        inverse = lax.rsqrt(jnp.mean(value * value, axis=-1, keepdims=True) + epsilon_norm)
        term = jnp.sum(part * (value * inverse), axis=0, keepdims=True)
        total = term if total is None else total + term
        if j % 2:
            send_ref[j // 2] = part.astype(bf16)
        else:
            keep_ref[j // 2] = part.astype(bf16)
    gain_grad_ref[...] = total


def tokens_back_kernel(keep_ref, got_ref, far_ref, tokens_ref, gain_ref, grad_hidden_ref, out_ref):
    grad_normed = keep_ref[0].astype(f32) + got_ref[0].astype(f32) + far_ref[...].astype(f32)
    value = tokens_ref[...].astype(f32)
    inverse = lax.rsqrt(jnp.mean(value * value, axis=-1, keepdims=True) + epsilon_norm)
    scaled = grad_normed * gain_ref[0:1, :]
    out_ref[...] = (
        grad_hidden_ref[...]
        + inverse * scaled
        - value * (inverse * inverse * inverse) * jnp.mean(scaled * value, axis=-1, keepdims=True)
    ).astype(bf16)


def small_sum(values, wait):
    devices = lax.axis_size("heads") * lax.axis_size("blk")
    n = values.shape[0]
    width = values.shape[1] // devices
    parts = jnp.transpose(values.reshape(n, devices, width), (1, 0, 2))
    padded = jnp.pad(parts, ((0, 0), (0, 8 - n), (0, 128 - width)))
    got = lax.all_to_all(tie(padded, wait), BOTH, 0, 0, tiled=True)
    return jnp.sum(got, axis=0)[:n, :width]


def halves(columns, core):
    half = columns.shape[1] // 2
    first, second = columns[:, :half], columns[:, half:]
    return jnp.where(core == 0, first, second), jnp.where(core == 0, second, first)


def unhalve(own, other, core):
    return jnp.concatenate(
        [jnp.where(core == 0, own, other), jnp.where(core == 0, other, own)], axis=1
    )


def unpack_half(buffer, drows, frows):
    def piece(low, high):
        return buffer[:, low:high].reshape(-1, LANES)

    matrices, base = [], 0
    for rows, count in ((drows, 2), (drows, 2), (frows, 3)):
        matrices.append(
            jnp.concatenate([piece(base + k * rows, base + (k + 1) * rows) for k in range(count)], axis=1)
        )
        base += rows * count
    return matrices


def pack_half(gate, up, down, count):
    pieces = []
    for matrix in (gate, up, down):
        rows = matrix.shape[0] // count
        for k in range(matrix.shape[1] // LANES):
            pieces.append(matrix[:, k * LANES : (k + 1) * LANES].reshape(count, rows, LANES))
    return jnp.concatenate(pieces, axis=1)


def shards(
    tokens,
    cotangent,
    routes,
    doc_lengths,
    attn_norm,
    w_query,
    key_weight,
    value_weight,
    w_output,
    ffn_norm,
    w_router,
    w_gate,
    w_up,
    w_down,
):
    blocks = lax.axis_size("blk")
    direct = blocks <= 8
    tok_dev, model = tokens.shape
    wrows = w_query.shape[0]
    drows = w_gate.shape[1]
    frows = w_down.shape[1]
    experts = w_router.shape[1]
    h, b = lax.axis_index("heads"), lax.axis_index("blk")
    core, x, y = h % 2, h // 2, b % 2
    zn = blocks // 2
    wide_cols = Q_COLS + 2 * K_COLS

    w_out = w_output.astype(bf16)
    if direct:
        wo_pieces = gather_few(w_out)
    else:
        wo_pieces = [lax.all_gather(w_out, "blk", axis=0, tiled=True)]

    far = swap(tokens, 2, 0)
    all_tokens = [tokens, swap(tokens, 1, 0), far, swap(far, 1, 0)]

    cut = [halves(m, core) for m in (w_gate[0].astype(bf16), w_up[0].astype(bf16), w_down[0].astype(bf16))]
    kept = pack_half(cut[0][0], cut[1][0], cut[2][0], 1)[0]
    given = pack_half(cut[0][1], cut[1][1], cut[2][1], 1)[0]
    at_home = core == y

    small_own = jnp.concatenate(
        [attn_norm.astype(bf16)[None], ffn_norm.astype(bf16)[None], w_router.astype(bf16).T], axis=0
    )
    small_own = jnp.pad(small_own.T, ((0, 0), (0, SMALL - 2 - experts)))
    heads_cat = jnp.concatenate(
        [
            w_query.astype(bf16).reshape(wrows, HEADS, Q_COLS),
            key_weight.astype(bf16).reshape(wrows, HEADS, K_COLS),
            value_weight.astype(bf16).reshape(wrows, HEADS, K_COLS),
            jnp.broadcast_to(small_own[:, None, :], (wrows, HEADS, SMALL)),
        ],
        axis=2,
    )
    by_head = lax.all_to_all(jnp.swapaxes(heads_cat, 0, 1), "heads", 0, 0, tiled=True)
    taken = swap(given, 1, 0)
    stay = jnp.where(at_home, kept, taken)
    leave = jnp.where(at_home, taken, kept)
    came = swap(leave, 0, 1)
    column = jnp.stack([jnp.where(y == 0, stay, came), jnp.where(y == 0, came, stay)])
    if direct:
        w_pieces = ring_gather(by_head, [far, all_tokens[1]], [wo_pieces[k] for k in (2, 4, 6)] + [all_tokens[3]])
        mine = [column, ring_step(tie(column, w_pieces[6]))]
    else:
        whole = lax.all_gather(by_head, "blk", axis=1, tiled=False)
        w_pieces = [whole.reshape(model, W_COLS + SMALL)]
        mine = lax.all_gather(column, "blk", axis=0, tiled=False, axis_index_groups=z_groups(blocks))
        mine = mine.reshape((blocks,) + kept.shape)

    ends = jnp.cumsum(doc_lengths)
    block_of = (h ^ jnp.arange(HEADS, dtype=jnp.int32)) * blocks + b
    query_pos = block_of[:, None] * tok_dev + jnp.arange(tok_dev, dtype=jnp.int32)[None, :]
    start = jnp.max(
        jnp.where(ends[None, None, :] <= query_pos[:, :, None], ends[None, None, :], 0), axis=2
    ).astype(jnp.int32)
    scal = jnp.concatenate(
        [
            jnp.stack([h, b]).astype(jnp.int32),
            start[:, 0] // (2 * tok_dev),
        ]
    )
    start = start[:, None, :]

    member = jnp.sum((routes[:, :, None] == jnp.arange(experts)[None, None, :]).astype(f32), axis=1)
    lower = (jnp.arange(tok_dev)[:, None] > jnp.arange(tok_dev)[None, :]).astype(bf16)
    rank = dot(lower, member.astype(bf16))
    slot = jnp.arange(CAP, dtype=f32)
    table = (
        ((rank.T[:, None, :] == slot[None, :, None]) & (member.T[:, None, :] > 0))
        .astype(bf16)
        .reshape(experts * CAP, tok_dev)
    )
    member = jnp.pad(member, ((0, 0), (0, 128 - experts)))

    normed, queries, kv_own, gains, router_all, weights = project(
        scal, all_tokens, w_pieces, blocks, [table, member, start]
    )
    if direct:
        kv = ring_gather(kv_own)
        mine.append(ring_step(tie(mine[1], kv[2])))
        mine.append(ring_step(mine[2]))
    else:
        kv = [blk_gather(kv_own)]
    att, lse = attend(scal, queries, kv, start, blocks)
    keep, send, output_w = output_parts(scal, att, wo_pieces, model, blocks, [])
    got, far = heads_sum(keep, send)
    seconds = [swap(piece, 1, 0) for piece in mine[:3]] if direct else []
    slot = shaped((CAP, model), bf16)
    hold = pltpu.VMEM((experts * CAP, model), bf16)
    routed = call(
        route_kernel,
        "route",
        [slot] * 8
        + [
            shaped((tok_dev, model), f32),
            shaped((tok_dev, model), bf16),
            shaped((tok_dev, 128), f32),
            shaped((experts * CAP, 1), f32),
        ],
        [scal],
        [keep, got, far, tokens, gains, router_all, member, table, cotangent],
        [hold, hold],
        waits=seconds,
        cost=3,
    )
    sent, grad_sent = routed[:4], routed[4:8]
    hidden, normed_ffn, gates, slot_gate = routed[8:]

    def to_experts(pieces):
        return [pieces[0]] + [swap(pieces[r], r // 2 * 2, r % 2) for r in range(1, experts)]

    arrived = to_experts(sent)
    grad_arrived = to_experts(grad_sent)
    if direct:
        weights_in = mine + seconds + [swap(tie(mine[3], *arrived[1:]), 1, 0)]
        gathered = [pltpu.VMEM((blocks,) + kept.shape, bf16)] * 2
    else:
        mine = tie(mine, sent[0])
        other = swap(mine, 1, 0)
        weights_in, gathered = [mine, other], []
    rows_all = experts * CAP
    ff = frows * blocks
    fwd = call(
        functools.partial(expert_kernel, drows, frows, direct),
        "expert",
        [slot] * 4
        + [shaped((rows_all, ff), f32), shaped((rows_all, ff), f32), shaped((rows_all, ff), bf16)],
        [scal],
        arrived + weights_in,
        [hold] + gathered,
        cost=2,
    )
    gate_pre, up_pre, inner = fwd[4:7]
    returned = to_experts(fwd[:4])
    grad_pre = call(
        functools.partial(expert_back_kernel, drows, frows, len(weights_in)),
        "expert_back",
        [shaped((rows_all, ff), bf16)] * 2,
        [scal],
        grad_arrived + [gate_pre, up_pre] + weights_in,
        [hold] + gathered,
        cost=2,
    )
    grad_pre = list(grad_pre)

    def expert_weights(own, extra, waits=()):
        return call(
            functools.partial(expert_weights_kernel, drows, frows, blocks, own),
            "expert_weights",
            [shaped((zn, 2) + kept.shape, bf16)],
            [scal],
            arrived + grad_arrived + [inner] + grad_pre + extra,
            [hold, hold],
            waits=waits,
            cost=1,
        )[0]

    grads_other = expert_weights(False, [])
    grads_met = swap(grads_other, 1, 0)
    grad_in = call(
        functools.partial(expert_input_kernel, drows, frows, len(weights_in)),
        "expert_input",
        [slot] * 4,
        [scal],
        grad_pre + weights_in,
        [hold] + gathered,
        waits=[grads_other],
        cost=2,
    )
    grad_returned = to_experts(grad_in)
    chip_grads = expert_weights(True, [grads_met], [grad_in[0]] + returned[1:])

    mixed, part_nf, router_grad = call(
        combine_kernel,
        "combine",
        [
            shaped((tok_dev, model), bf16),
            shaped((tok_dev, model), f32),
            shaped((8, model), f32),
        ],
        [scal],
        returned + [hidden, normed_ffn, gates, slot_gate, table, cotangent, router_all],
        [hold],
        waits=[chip_grads],
        cost=1,
    )
    later = [mixed]
    if direct:

        def met(moving, k):
            return (moving.astype(f32) + chip_grads[k].astype(f32)).astype(bf16)

        second_sum = met(ring_step(chip_grads[3]), 2)
        third_sum = met(ring_step(second_sum), 1)
        later_still = [second_sum]
    else:
        z_grads = lax.psum_scatter(
            chip_grads, "blk", scatter_dimension=0, tiled=False, axis_index_groups=z_groups(blocks)
        )
        later_still = []
    grad_hidden, branch, gain_two_grad = call(
        norm_back_kernel,
        "norm_back",
        [
            shaped((tok_dev, model), f32),
            shaped((tok_dev, model), bf16),
            shaped((1, model), f32),
        ],
        [scal],
        grad_returned + [hidden, table, cotangent, gains, part_nf],
        [hold],
        waits=later,
    )

    far_branch = swap(branch, 2, 0)
    branches = [branch, swap(branch, 1, 0), far_branch, swap(far_branch, 1, 0)]
    dq, dkv = attend_back(scal, queries, kv, start, att, lse, output_w, branches, blocks, later_still)
    if direct:
        dkv_own, onward = reduce_pieces(dkv[:zn], dkv[zn:], third_sum)
    else:
        dkv_own, onward = blk_reduce(dkv[0]), [dq]
    dkv_own = dkv_own.astype(bf16)
    if direct:
        z_grads = met(ring_step(tie(third_sum, dkv_own)), 0)

    def column_grads(name, grad, waits=()):
        cols = grad.shape[2]
        return call(
            functools.partial(column_grad_kernel, blocks, wrows, direct),
            name,
            [shaped(pair_shape(blocks, (HEADS, wrows, cols), direct), bf16)],
            [scal],
            [normed, grad],
            [pltpu.VMEM((model, cols), bf16)],
            waits=waits,
        )[0]

    late_parts = call(
        functools.partial(late_grad_kernel, blocks, wrows, direct),
        "late_grad",
        [shaped(pair_shape(blocks, (2 * wrows, model), direct), bf16)],
        [scal],
        [normed, dq, att] + branches,
        [pltpu.VMEM((model, Q_COLS), bf16), pltpu.VMEM((Q_COLS, model), bf16)],
        waits=[dq],
    )[0]
    late_parts = tie(late_parts, *(onward[:2] + ([third_sum] if direct else [])))
    late_sums = reduce_ring(late_parts, direct, dkv_own)
    grad_wout = late_sums[wrows:]
    sum_wq = jnp.swapaxes(late_sums[:wrows].reshape(wrows, HEADS, Q_COLS), 0, 1)
    keep, send, gain_one_grad = call(
        normed_back_kernel,
        "normed_back",
        [shaped((2, tok_dev, model), bf16)] * 2 + [shaped((1, model), f32)],
        [],
        [dq, dkv_own, weights] + all_tokens,
        waits=[],
        cost=6,
    )
    got, far = heads_sum(keep, send)
    kv_parts = column_grads("key_value_grad", dkv_own, [send])
    sum_wkv, kv_sent = reduce_few(kv_parts, direct, far, z_grads)
    stay = jnp.where(y == 0, z_grads[0], z_grads[1])
    came = swap(jnp.where(y == 0, z_grads[1], z_grads[0]), 0, 1)
    kept_grad = jnp.where(at_home, stay, came)
    taken_grad = swap(jnp.where(at_home, came, stay), 1, 0)
    grad_tokens = call(
        tokens_back_kernel,
        "tokens_back",
        [shaped((tok_dev, model), bf16)],
        [],
        [keep, got, far, tokens, gains, grad_hidden],
    )[0]
    column_sums = jnp.concatenate([sum_wq.astype(bf16), sum_wkv.astype(bf16)], axis=2)
    by_row = lax.all_to_all(tie(column_sums, came, grad_tokens), "heads", 0, 0, tiled=True)
    by_row = jnp.swapaxes(by_row, 0, 1).astype(f32)
    grad_wq = by_row[:, :, :Q_COLS].reshape(wrows, -1)
    grad_wk = by_row[:, :, Q_COLS : Q_COLS + K_COLS].reshape(wrows, -1)
    grad_wv = by_row[:, :, Q_COLS + K_COLS :].reshape(wrows, -1)
    router_back = router_grad[:experts]
    small_grads = small_sum(jnp.concatenate([gain_one_grad, gain_two_grad, router_back], axis=0), far)

    owned = unpack_half(kept_grad[None], drows, frows)
    fetched = unpack_half(taken_grad[None], drows, frows)
    grad_gate_w, grad_up_w, grad_down_w = [
        unhalve(o, f, core).astype(f32) for o, f in zip(owned, fetched)
    ]
    return (
        mixed,
        grad_tokens,
        small_grads[0],
        grad_wq,
        grad_wk,
        grad_wv,
        grad_wout,
        small_grads[1],
        small_grads[2 : 2 + experts].T,
        grad_gate_w[None],
        grad_up_w[None],
        grad_down_w[None],
    )


def solution(mesh):
    rows = P(("heads", "blk"), None)
    flat = P(("heads", "blk"))
    expert = P("heads", "blk", None)
    return jax.shard_map(
        shards,
        mesh=mesh,
        in_specs=(
            rows, rows, rows, P(), flat, rows, rows, rows, rows, flat, rows, expert, expert, expert,
        ),
        out_specs=(
            rows, rows, flat, rows, rows, rows, rows, flat, rows, expert, expert, expert,
        ),
        check_vma=False,
    )
```

```python
import functools

import jax
import jax.numpy as jnp
from jax import lax
from jax.experimental import pallas as pl
from jax.experimental.pallas import tpu as pltpu
from jax.sharding import PartitionSpec as P

QUERY_HEADS = 24
KEY_VALUE_HEADS = 8
HEAD_WIDTH = 64
CAP = 96
HEADS = 4
GROUP = QUERY_HEADS // KEY_VALUE_HEADS
KV_LOCAL = KEY_VALUE_HEADS // HEADS
Q_LOCAL = KV_LOCAL * GROUP
Q_COLS = Q_LOCAL * HEAD_WIDTH
K_COLS = KV_LOCAL * HEAD_WIDTH
STEP = 256

epsilon_norm = 1e-05
highest = lax.Precision.HIGHEST
masked_score = -1e30
bf16 = jnp.bfloat16
f32 = jnp.float32
BOTH = ("heads", "blk")
VMEM_LIMIT = 60 * 1024 * 1024
LANES = 256


def swap(value, heads_bits, blk_bits):
    count, blocks = lax.axis_size("heads"), lax.axis_size("blk")
    pairs = []
    for i in range(count * blocks):
        h, b = divmod(i, blocks)
        pairs.append((i, (h ^ heads_bits) * blocks + (b ^ blk_bits)))
    return lax.ppermute(value, BOTH, pairs)


def heads_gather(value):
    far = swap(value, 2, 0)
    near = swap(value, 1, 0)
    return jnp.stack([value, near, far, swap(far, 1, 0)])


def heads_reduce(parts):
    got = swap(jnp.stack([parts[1], parts[3]]), 1, 0)
    onward = (parts[2].astype(f32) + got[1].astype(f32)).astype(parts.dtype)
    far = swap(onward, 2, 0)
    return parts[0].astype(f32) + got[0].astype(f32) + far.astype(f32)


def ring_gather(value, *waits):
    pieces = []
    for k in range(lax.axis_size("blk") // 2):
        if k and k <= len(waits):
            value = tie(value, *waits[k - 1])
        value = ring_step(value) if k else value
        pieces += [value, swap(value, 0, 1)]
    return pieces


def reduce_pieces(evens, odds, wait):
    half = len(evens)
    total, sent = None, []
    for g, stack in enumerate(odds):
        got = swap(stack, 0, 1)
        for i in range(stack.shape[0]):
            zr = half - 1 - (g * (half // 2) + i)
            here = evens[zr].astype(f32) + got[i].astype(f32)
            if zr:
                sent.append(here.astype(bf16))
                here = swap(tie(sent[-1], wait), 0, 2 * zr).astype(f32)
            total = here if total is None else total + here
    return total, sent


def gather_few(value):
    column = [value] + [swap(value, 0, r) for r in range(2, lax.axis_size("blk"), 2)]
    beside = swap(jnp.stack(column), 0, 1)
    pieces = []
    for k, piece in enumerate(column):
        pieces += [piece, beside[k]]
    return pieces


def blk_gather(value):
    blocks = lax.axis_size("blk")
    if blocks > 8:
        whole = lax.all_gather(value, "blk", axis=0, tiled=False)
        return jnp.take(whole, lax.axis_index("blk") ^ jnp.arange(blocks), axis=0)
    pieces = [None] * blocks
    for r in range(0, blocks, 2):
        piece = swap(value, 0, r) if r else value
        pieces[r] = piece
        pieces[r + 1] = swap(piece, 0, 1)
    return jnp.stack(pieces)


def blk_reduce(parts):
    blocks = lax.axis_size("blk")
    if blocks > 8:
        whole = jnp.take(parts, lax.axis_index("blk") ^ jnp.arange(blocks), axis=0)
        return lax.psum_scatter(whole, "blk", scatter_dimension=0, tiled=False).astype(f32)
    total = None
    for r in range(blocks - 2, -1, -2):
        got = swap(parts[r + 1], 0, 1)
        here = parts[r].astype(f32) + got.astype(f32)
        if r:
            here = swap(here.astype(parts.dtype), 0, r).astype(f32)
        total = here if total is None else total + here
    return total


def blk_gather_few(value):
    blocks = lax.axis_size("blk")
    if blocks > 8:
        return blk_gather(value)
    column = jnp.stack([value] + [swap(value, 0, r) for r in range(2, blocks, 2)])
    both = jnp.stack([column, swap(column, 0, 1)], axis=1)
    return both.reshape((blocks,) + value.shape)


def reduce_few(parts, direct, *waits):
    if not direct:
        return lax.psum_scatter(parts, "blk", scatter_dimension=0, tiled=False).astype(f32), parts
    got = swap(parts[1], 0, 1)
    here = parts[0].astype(f32) + got.astype(f32)
    sent = here.astype(parts.dtype)
    if waits:
        sent = tie(sent, *waits)
    total = here[0]
    for k in range(1, parts.shape[1]):
        total = total + swap(sent[k], 0, 2 * k).astype(f32)
    return total, sent


def reduce_ring(parts, direct, *waits):
    if not direct:
        return lax.psum_scatter(parts, "blk", scatter_dimension=0, tiled=False).astype(f32)
    got = swap(parts[1], 0, 1)
    here = parts[0].astype(f32) + got.astype(f32)
    moving = here[-1].astype(parts.dtype)
    if waits:
        moving = tie(moving, *waits)
    for k in range(parts.shape[1] - 2, -1, -1):
        total = ring_step(moving).astype(f32) + here[k]
        moving = total.astype(parts.dtype)
    return total


def blk_unshuffle(pieces):
    blocks = pieces.shape[0]
    b = lax.axis_index("blk")
    return jnp.stack(
        [lax.dynamic_index_in_dim(pieces, b ^ i, 0, keepdims=False) for i in range(blocks)]
    )


RING = {0: 1, 1: 3, 3: 2, 2: 0}


def ring_step(value):
    count, blocks = lax.axis_size("heads"), lax.axis_size("blk")
    pairs = []
    for i in range(count * blocks):
        h, b = divmod(i, blocks)
        pairs.append((i, h * blocks + RING[b // 2] * 2 + b % 2))
    return lax.ppermute(value, BOTH, pairs)


def ring_place(z):
    return z ^ (z >> 1)


def ring_owner(z, k):
    place = (ring_place(z) - k) & 3
    return place ^ (place >> 1)


def z_groups(blocks):
    return [[i for i in range(blocks) if i % 2 == y] for y in range(2)]


def expand_heads(transposed, dtype):
    rows = []
    n = transposed.shape[1]
    zero = jnp.zeros((HEAD_WIDTH, n), dtype)
    for g in range(KV_LOCAL):
        columns = []
        for head in range(Q_LOCAL):
            if head // GROUP == g:
                columns.append(transposed[head * HEAD_WIDTH : (head + 1) * HEAD_WIDTH].astype(dtype))
            else:
                columns.append(zero)
        rows.append(jnp.concatenate(columns, axis=1))
    return jnp.concatenate(rows, axis=0)


def collapse_heads(wide, n):
    pieces = []
    for head in range(Q_LOCAL):
        g = head // GROUP
        pieces.append(wide[g * HEAD_WIDTH : (g + 1) * HEAD_WIDTH, head * n : (head + 1) * n])
    return jnp.concatenate(pieces, axis=0)


def key_rows(kv_ref, r, j, low, high):
    return jnp.concatenate(
        [kv_ref[r, j, :, low:high], kv_ref[r + 1, j, :, low:high]], axis=0
    )


def step_place(t, h, b, blocks, tok_dev, direct):
    half = blocks // 2
    owner_h = t // half
    owner_z = t % half
    j = owner_h ^ h
    z, y = b // 2, b % 2
    term = (owner_z ^ z) * 2
    if direct:
        piece = ((ring_place(z) - ring_place(owner_z)) & 3) * 2
    else:
        piece = term
    row = lax.broadcasted_iota(jnp.int32, (2 * tok_dev, 1), 0)
    base = (owner_h * blocks + owner_z * 2) * tok_dev
    second = row >= tok_dev
    position = base + jnp.where(
        second, row - tok_dev + (1 - y) * tok_dev, row + y * tok_dev
    )
    return piece, term, j, position


def fill_pieces(refs, whole_ref):
    for r, ref in enumerate(refs):
        whole_ref[r] = ref[...]


def by_pairs(low, high, work):
    count = high - low

    def four(u, unused):
        work([low + 4 * u + k for k in range(4)])
        return unused

    lax.fori_loop(0, count // 4, four, 0)

    @pl.when(count % 4 >= 2)
    def two():
        first = low + count // 4 * 4
        work([first, first + 1])

    @pl.when(count % 2 == 1)
    def rest():
        work([high - 1])


def attend_kernel(blocks, count, *refs):
    scal_ref, q_ref, start_ref = refs[:3]
    pieces = refs[3 : 3 + count]
    att_ref, lse_ref, top_ref, sum_ref, acc_ref = refs[3 + count : 8 + count]
    if count > 1:
        kv_ref = refs[8 + count]
        fill_pieces(pieces, kv_ref)
    else:
        kv_ref = pieces[0]
    tok_dev = q_ref.shape[1]
    h, b = scal_ref[0], scal_ref[1]

    def one(j, unused):
        block = (h ^ j) * blocks + b
        queries = (q_ref[j].astype(f32) * 0.125).T
        wide = expand_heads(queries, bf16)
        lane = lax.broadcasted_iota(jnp.int32, (1, tok_dev), 1)
        query_pos = jnp.concatenate([block * tok_dev + lane] * Q_LOCAL, axis=1)
        start = jnp.concatenate([start_ref[j]] * Q_LOCAL, axis=1)
        top_ref[...] = jnp.full(top_ref.shape, masked_score, f32)
        sum_ref[...] = jnp.zeros(sum_ref.shape, f32)
        acc_ref[...] = jnp.zeros(acc_ref.shape, f32)

        def work(steps):
            places = [step_place(t, h, b, blocks, tok_dev, count > 1) for t in steps]
            keys = jnp.concatenate([key_rows(kv_ref, p[0], p[2], 0, K_COLS) for p in places], axis=0)
            values = jnp.concatenate(
                [key_rows(kv_ref, p[0], p[2], K_COLS, 2 * K_COLS) for p in places], axis=0
            )
            position = jnp.concatenate([p[3] for p in places], axis=0)
            scores = lax.dot_general(keys, wide, (((1,), (0,)), ((), ())), preferred_element_type=f32)
            allowed = (position >= start) & (position <= query_pos)
            scores = jnp.where(allowed, scores, masked_score)
            old = top_ref[...]
            new = jnp.maximum(old, jnp.max(scores, axis=0, keepdims=True))
            rescale = jnp.exp(old - new)
            weights = jnp.exp(scores - new)
            top_ref[...] = new
            sum_ref[...] = sum_ref[...] * rescale + jnp.sum(weights, axis=0, keepdims=True)
            acc_ref[...] = acc_ref[...] * rescale + lax.dot_general(
                values, weights.astype(bf16), (((0,), (0,)), ((), ())), preferred_element_type=f32
            )

        by_pairs(scal_ref[2 + j], block // 2 + 1, work)
        total = sum_ref[...]
        out = collapse_heads(acc_ref[...] / total, tok_dev)
        att_ref[j] = out.T.astype(bf16)
        lse_ref[j] = top_ref[...] + jnp.log(total)
        return unused

    for j in range(HEADS):
        one(j, 0)


SMEM = pl.BlockSpec(memory_space=pltpu.SMEM)
VMEM = pl.BlockSpec(memory_space=pltpu.VMEM)
ANY = pl.BlockSpec(memory_space=pl.ANY)


def room_for(arrays, scratch):
    held = sum(a.size * a.dtype.itemsize for a in arrays)
    for s in scratch:
        size = 1
        for n in s.shape:
            size *= n
        held += size * jnp.dtype(s.dtype).itemsize
    return min(VMEM_LIMIT, held + held // 8 + (14 << 20))


def shaped(shape, dtype):
    return jax.ShapeDtypeStruct(shape, dtype)


def call(kernel, name, outs, scalars, arrays, scratch=(), waits=(), cost=4):
    scalars, arrays, waits = list(scalars), list(arrays), list(waits)
    used = len(scalars) + len(arrays)

    def body(*refs):
        kernel(*(refs[:used] + refs[used + len(waits) :]))

    return pl.pallas_call(
        body,
        out_shape=tuple(outs),
        in_specs=[SMEM] * len(scalars) + [VMEM] * len(arrays) + [ANY] * len(waits),
        out_specs=tuple([VMEM] * len(outs)),
        scratch_shapes=list(scratch),
        compiler_params=pltpu.CompilerParams(
            vmem_limit_bytes=room_for(arrays + list(outs), scratch)
        ),
        cost_estimate=pl.CostEstimate(flops=cost * 1000000000, bytes_accessed=1 << 20, transcendentals=0),
        name=name,
    )(*scalars, *arrays, *waits)


def tie(value, *waits):
    def body(*refs):
        pass

    return pl.pallas_call(
        body,
        out_shape=shaped(value.shape, value.dtype),
        in_specs=[ANY] * (1 + len(waits)),
        out_specs=ANY,
        input_output_aliases={0: 0},
        name="tie",
    )(value, *waits)


def attend(scal, queries, kv, start, blocks, waits=()):
    tok_dev = queries.shape[1]
    wide = Q_LOCAL * tok_dev
    scratch = [
        pltpu.VMEM((1, wide), f32),
        pltpu.VMEM((1, wide), f32),
        pltpu.VMEM((K_COLS, wide), f32),
    ]
    if len(kv) > 1:
        scratch.append(pltpu.VMEM((blocks,) + kv[0].shape, bf16))
    return call(
        functools.partial(attend_kernel, blocks, len(kv)),
        "attend",
        (
            shaped((HEADS, tok_dev, Q_COLS), bf16),
            shaped((HEADS, 1, wide), f32),
        ),
        [scal],
        [queries, start] + list(kv),
        scratch,
        waits=waits,
        cost=12,
    )


def attend_back_kernel(blocks, count, *refs):
    scal_ref, q_ref, start_ref, att_ref, lse_ref, wo_ref = refs[:6]
    branch = refs[6:10]
    pieces = refs[10 : 10 + count]
    dq_ref = refs[10 + count]
    n_outs = count // 2 + 2 if count > 1 else 1
    outs = refs[11 + count : 11 + count + n_outs]
    acc_ref, term_ref, grad_ref = refs[11 + count + n_outs : 14 + count + n_outs]
    if count > 1:
        kv_ref = refs[14 + count + n_outs]
        fill_pieces(pieces, kv_ref)
    else:
        kv_ref = pieces[0]
    tok_dev = q_ref.shape[1]
    h, b = scal_ref[0], scal_ref[1]
    term_ref[...] = jnp.zeros(term_ref.shape, f32)
    for j in range(HEADS):
        grad_ref[j] = dot_nt(branch[j][...], wo_ref[...]).astype(bf16)

    def one(j, unused):
        block = (h ^ j) * blocks + b
        wide = expand_heads((q_ref[j].astype(f32) * 0.125).T, bf16)
        grad_t = grad_ref[j].astype(f32).T
        wide_grad = expand_heads(grad_t, bf16)
        product = grad_t * att_ref[j].astype(f32).T
        delta = jnp.concatenate(
            [
                jnp.sum(product[head * HEAD_WIDTH : (head + 1) * HEAD_WIDTH], axis=0, keepdims=True)
                for head in range(Q_LOCAL)
            ],
            axis=1,
        )
        lse = lse_ref[j]
        lane = lax.broadcasted_iota(jnp.int32, (1, tok_dev), 1)
        query_pos = jnp.concatenate([block * tok_dev + lane] * Q_LOCAL, axis=1)
        start = jnp.concatenate([start_ref[j]] * Q_LOCAL, axis=1)
        acc_ref[...] = jnp.zeros(acc_ref.shape, f32)

        def work(steps):
            places = [step_place(t, h, b, blocks, tok_dev, count > 1) for t in steps]
            keys = jnp.concatenate([key_rows(kv_ref, p[0], p[2], 0, K_COLS) for p in places], axis=0)
            values = jnp.concatenate(
                [key_rows(kv_ref, p[0], p[2], K_COLS, 2 * K_COLS) for p in places], axis=0
            )
            position = jnp.concatenate([p[3] for p in places], axis=0)
            scores = lax.dot_general(keys, wide, (((1,), (0,)), ((), ())), preferred_element_type=f32)
            allowed = (position >= start) & (position <= query_pos)
            probs = jnp.exp(jnp.where(allowed, scores - lse, masked_score))
            grad_probs = lax.dot_general(
                values, wide_grad, (((1,), (0,)), ((), ())), preferred_element_type=f32
            )
            grad_scores = (probs * (grad_probs - delta)).astype(bf16)
            acc_ref[...] += lax.dot_general(
                keys, grad_scores, (((0,), (0,)), ((), ())), preferred_element_type=f32
            )
            key_term = lax.dot_general(
                grad_scores, wide, (((1,), (1,)), ((), ())), preferred_element_type=f32
            )
            value_term = lax.dot_general(
                probs.astype(bf16), wide_grad, (((1,), (1,)), ((), ())), preferred_element_type=f32
            )
            both = jnp.concatenate([key_term, value_term], axis=1)
            for i, (unused_piece, term, jk, unused_position) in enumerate(places):
                low = 2 * i * tok_dev
                term_ref[term, jk] += both[low : low + tok_dev]
                term_ref[term + 1, jk] += both[low + tok_dev : low + 2 * tok_dev]

        by_pairs(scal_ref[2 + j], block // 2 + 1, work)
        dq_ref[j] = (collapse_heads(acc_ref[...], tok_dev) * 0.125).T.astype(bf16)
        return unused

    lax.fori_loop(0, HEADS, one, 0)
    if count > 1:
        half = count // 2
        for zr in range(half):
            outs[zr][...] = term_ref[2 * zr].astype(bf16)
            back = half - 1 - zr
            outs[half + back // (half // 2)][back % (half // 2)] = term_ref[2 * zr + 1].astype(bf16)
    else:
        outs[0][...] = term_ref[...].astype(bf16)


def attend_back(scal, queries, kv, start, att, lse, output_w, branch, blocks, waits=()):
    tok_dev = queries.shape[1]
    wide = Q_LOCAL * tok_dev
    whole = (blocks, HEADS, tok_dev, 2 * K_COLS)
    scratch = [
        pltpu.VMEM((K_COLS, wide), f32),
        pltpu.VMEM(whole, f32),
        pltpu.VMEM((HEADS, tok_dev, Q_COLS), bf16),
    ]
    terms = [shaped(whole, bf16)]
    if len(kv) > 1:
        scratch.append(pltpu.VMEM(whole, bf16))
        half = blocks // 2
        terms = [shaped(whole[1:], bf16)] * half + [shaped((half // 2,) + whole[1:], bf16)] * 2
    outs = call(
        functools.partial(attend_back_kernel, blocks, len(kv)),
        "attend_back",
        [shaped((HEADS, tok_dev, Q_COLS), bf16)] + terms,
        [scal],
        [queries, start, att, lse, output_w] + list(branch) + list(kv),
        scratch,
        waits=waits,
        cost=17,
    )
    return outs[0], outs[1:]


def dot(a, b):
    return jnp.dot(a, b, preferred_element_type=f32)


def dot_tn(a, b):
    return lax.dot_general(a, b, (((0,), (0,)), ((), ())), preferred_element_type=f32)


def dot_nt(a, b):
    return lax.dot_general(a, b, (((1,), (1,)), ((), ())), preferred_element_type=f32)


def split(value, count):
    terms = []
    for unused in range(count):
        term = value.astype(bf16)
        terms.append(term)
        value = value - term.astype(f32)
    return terms


def own_rows(b, r, source, wrows, blocks):
    return pl.ds(pl.multiple_of((source * blocks + (b ^ r)) * wrows, 16), wrows)


W_COLS = Q_COLS + 2 * K_COLS
SMALL = 128


def project_kernel(blocks, count, *refs):
    scal_ref = refs[0]
    tokens = refs[1:5]
    pieces = refs[5 : 5 + count]
    normed_ref, q_ref, kv_ref, gains_ref, router_ref = refs[5 + count : 10 + count]
    w_ref = refs[10 + count] if count > 1 else pieces[0]
    b = scal_ref[1]
    if count > 1:
        wrows = pieces[0].shape[1]
        for r in range(count):
            for source in range(HEADS):
                owner = ring_owner(b // 2, r // 2) * 2 + (b % 2 ^ r % 2)
                low = pl.multiple_of((source * blocks + owner) * wrows, 16)
                w_ref[pl.ds(low, wrows), :] = pieces[r][source]
    small = w_ref[:, W_COLS:].astype(f32).T
    gains_ref[...] = small[:8]
    shifted = jnp.concatenate([small[2:], small[:2]], axis=0)
    row = lax.broadcasted_iota(jnp.int32, (SMALL, 1), 0)
    router_ref[...] = jnp.where(row < 4, shifted, 0.0).astype(bf16)
    gain = small[0:1]
    tok_dev = tokens[0].shape[0]
    for j in range(HEADS):
        value = tokens[j][...].astype(f32)
        inverse = lax.rsqrt(jnp.mean(value * value, axis=-1, keepdims=True) + epsilon_norm)
        normed_ref[j * tok_dev : (j + 1) * tok_dev, :] = (value * inverse * gain).astype(bf16)
    projected = dot(normed_ref[...], w_ref[:, :W_COLS]).astype(bf16)
    for j in range(HEADS):
        q_ref[j] = projected[j * tok_dev : (j + 1) * tok_dev, :Q_COLS]
        kv_ref[j] = projected[j * tok_dev : (j + 1) * tok_dev, Q_COLS:]


def project(scal, tokens, pieces, blocks, waits=()):
    tok_dev, model = tokens[0].shape
    outs = [
        shaped((HEADS * tok_dev, model), bf16),
        shaped((HEADS, tok_dev, Q_COLS), bf16),
        shaped((HEADS, tok_dev, 2 * K_COLS), bf16),
        shaped((8, model), f32),
        shaped((SMALL, model), bf16),
    ]
    if len(pieces) > 1:
        outs.append(shaped((model, W_COLS + SMALL), bf16))
    got = call(
        functools.partial(project_kernel, blocks, len(pieces)),
        "project",
        outs,
        [scal],
        list(tokens) + list(pieces),
        waits=waits,
    )
    return got[:5] + (got[5] if len(pieces) > 1 else pieces[0],)


def output_kernel(blocks, count, *refs):
    scal_ref, att_ref = refs[:2]
    pieces = refs[2 : 2 + count]
    keep_ref, send_ref = refs[2 + count : 4 + count]
    wo_ref = refs[4 + count] if count > 1 else pieces[0]
    b = scal_ref[1]
    if count > 1:
        wrows = pieces[0].shape[0]
        for r in range(count):
            wo_ref[own_rows(b, r, 0, wrows, blocks), :] = pieces[r][...]
    for j in range(HEADS):
        part = dot(att_ref[j], wo_ref[...]).astype(bf16)
        if j % 2:
            send_ref[j // 2] = part
        else:
            keep_ref[j // 2] = part


def output_parts(scal, att, pieces, model, blocks, waits):
    tok_dev = att.shape[1]
    outs = [shaped((2, tok_dev, model), bf16)] * 2
    if len(pieces) > 1:
        outs.append(shaped((Q_COLS, model), bf16))
    got = call(
        functools.partial(output_kernel, blocks, len(pieces)),
        "output_parts",
        outs,
        [scal],
        [att] + list(pieces),
        waits=waits,
    )
    return got[0], got[1], (got[2] if len(pieces) > 1 else pieces[0])


def heads_sum(keep, send):
    got = swap(send, 1, 0)
    onward = (keep[1].astype(f32) + got[1].astype(f32)).astype(bf16)
    return got, swap(onward, 2, 0)


def route_kernel(
    scal_ref, keep_ref, got_ref, far_ref, tokens_ref, gain_ref, router_ref, member_ref, table_ref, cot_ref,
    s0, s1, s2, s3, g0, g1, g2, g3, hidden_ref, nf_ref, gates_ref, slot_gate_ref, sent_ref, back_ref,
):
    hidden = (
        tokens_ref[...].astype(f32)
        + keep_ref[0].astype(f32)
        + got_ref[0].astype(f32)
        + far_ref[...].astype(f32)
    )
    hidden_ref[...] = hidden
    inverse = lax.rsqrt(jnp.mean(hidden * hidden, axis=-1, keepdims=True) + epsilon_norm)
    nf = (hidden * inverse * gain_ref[1:2, :]).astype(bf16)
    nf_ref[...] = nf
    logits = dot_nt(nf, router_ref[...])
    picked = member_ref[...] > 0
    peak = jnp.max(jnp.where(picked, logits, -jnp.inf), axis=-1, keepdims=True)
    raised = jnp.where(picked, jnp.exp(jnp.where(picked, logits - peak, 0.0)), 0.0)
    gates = raised / jnp.sum(raised, axis=-1, keepdims=True)
    gates_ref[...] = gates
    table = table_ref[...]
    sent = dot(table, nf).astype(bf16)
    spread = dot(table, cot_ref[...])
    slot_gates = sum(dot(table, term) for term in split(gates, 3))
    lane = lax.broadcasted_iota(jnp.int32, (CAP, slot_gates.shape[1]), 1)
    sent_ref[...] = sent
    for e in range(4):
        rows = slice(e * CAP, (e + 1) * CAP)
        column = jnp.sum(jnp.where(lane == e, slot_gates[rows], 0.0), axis=1, keepdims=True)
        slot_gate_ref[rows, :] = column
        back_ref[rows, :] = (spread[rows] * column).astype(bf16)
    for r, (s_ref, g_ref) in enumerate(((s0, g0), (s1, g1), (s2, g2), (s3, g3))):
        rows = slot_rows(own_place(scal_ref) ^ r)
        s_ref[...] = sent_ref[rows, :]
        g_ref[...] = back_ref[rows, :]


def gate_up(ref, drows):
    return jnp.concatenate(
        [ref[:, k * drows : (k + 1) * drows, :].reshape(-1, LANES) for k in range(4)], axis=1
    )


def down_half(ref, drows, frows):
    base = 4 * drows
    return jnp.concatenate(
        [ref[:, base + k * frows : base + (k + 1) * frows, :].reshape(-1, LANES) for k in range(3)],
        axis=1,
    )


def lanes(offset, size):
    return pl.ds(pl.multiple_of(offset, 128), size)


def fill_weights(scal_ref, refs, mine_ref, other_ref):
    z = scal_ref[1] // 2
    for pieces, whole_ref in ((refs[:4], mine_ref), (refs[4:], other_ref)):
        for k in range(4):
            for y in range(2):
                whole_ref[ring_owner(z, k) * 2 + y] = pieces[k][y]


def expert_kernel(drows, frows, direct, *refs):
    scal_ref = refs[0]
    if direct:
        p0, p1, p2, p3, gp_ref, up_ref, inner_ref, out_ref, mine_ref, other_ref = refs[13:]
        fill_weights(scal_ref, refs[5:13], mine_ref, other_ref)
    else:
        mine_ref, other_ref, p0, p1, p2, p3, gp_ref, up_ref, inner_ref, out_ref = refs[5:]
    fill_rows(scal_ref, refs[1:5], out_ref)
    core = scal_ref[0] % 2
    rows = out_ref[...]
    for side, ref in ((core, mine_ref), (1 - core, other_ref)):
        both = dot(rows, gate_up(ref, drows))
        gate, up = both[:, : 2 * LANES], both[:, 2 * LANES :]
        place = lanes(side * 2 * LANES, 2 * LANES)
        gp_ref[:, place] = gate
        up_ref[:, place] = up
        inner_ref[:, place] = (gate * jax.nn.sigmoid(gate) * up).astype(bf16)
    inner = inner_ref[...]
    for side, ref in ((core, mine_ref), (1 - core, other_ref)):
        out_ref[:, lanes(side * 3 * LANES, 3 * LANES)] = dot(inner, down_half(ref, drows, frows)).astype(bf16)
    for r, ref in enumerate((p0, p1, p2, p3)):
        ref[...] = out_ref[slot_rows(own_place(scal_ref) ^ r), :]


def own_place(scal_ref):
    return scal_ref[0] // 2 * 2 + scal_ref[1] % 2


def slot_rows(place):
    return pl.ds(pl.multiple_of(place * CAP, 16), CAP)


def fill_rows(scal_ref, refs, rows_ref):
    for r, ref in enumerate(refs):
        rows_ref[slot_rows(own_place(scal_ref) ^ r), :] = ref[...]


def weights_of(scal_ref, refs, scratch):
    if not scratch:
        return refs
    fill_weights(scal_ref, refs, *scratch)
    return scratch


def expert_back_kernel(drows, frows, count, *refs):
    scal_ref = refs[0]
    gp_ref, up_ref = refs[5:7]
    ggp_ref, gup_ref, grad_ref = refs[7 + count : 10 + count]
    mine_ref, other_ref = weights_of(scal_ref, refs[7 : 7 + count], refs[10 + count :])
    fill_rows(scal_ref, refs[1:5], grad_ref)
    core = scal_ref[0] % 2
    grad_inner = None
    for side, ref in ((core, mine_ref), (1 - core, other_ref)):
        term = dot_nt(grad_ref[:, lanes(side * 3 * LANES, 3 * LANES)], down_half(ref, drows, frows))
        grad_inner = term if grad_inner is None else grad_inner + term
    gate, up = gp_ref[...], up_ref[...]
    sig = jax.nn.sigmoid(gate)
    ggp_ref[...] = (grad_inner * up * sig * (1.0 + gate * (1.0 - sig))).astype(bf16)
    gup_ref[...] = (grad_inner * gate * sig).astype(bf16)


def expert_input_kernel(drows, frows, count, *refs):
    scal_ref, ggp_ref, gup_ref = refs[:3]
    p0, p1, p2, p3, grad_ref = refs[3 + count : 8 + count]
    mine_ref, other_ref = weights_of(scal_ref, refs[3 : 3 + count], refs[8 + count :])
    core = scal_ref[0] % 2
    total = None
    for side, ref in ((core, mine_ref), (1 - core, other_ref)):
        place = lanes(side * 2 * LANES, 2 * LANES)
        both = jnp.concatenate([ggp_ref[:, place], gup_ref[:, place]], axis=1)
        term = dot_nt(both, gate_up(ref, drows))
        total = term if total is None else total + term
    grad_ref[...] = total.astype(bf16)
    for r, ref in enumerate((p0, p1, p2, p3)):
        ref[...] = grad_ref[slot_rows(own_place(scal_ref) ^ r), :]


def expert_weights_kernel(
    drows, frows, blocks, own, scal_ref, x0, x1, x2, x3, g0, g1, g2, g3, inner_ref, ggp_ref, gup_ref, *rest
):
    if own:
        got_ref, out_ref, grad_ref, rows_ref = rest
    else:
        out_ref, grad_ref, rows_ref = rest
    core, z = scal_ref[0] % 2, scal_ref[1] // 2
    side = core if own else 1 - core
    fill_rows(scal_ref, (g0, g1, g2, g3), grad_ref)
    fill_rows(scal_ref, (x0, x1, x2, x3), rows_ref)
    rows = rows_ref[...]

    def put(low, height, term):
        for k in range(term.shape[1] // LANES):
            piece = term[:, k * LANES : (k + 1) * LANES].reshape(blocks // 2, 2, height, LANES)
            place = slice(low, low + height)
            for at in range(blocks // 2):
                step = (ring_place(at) - ring_place(z)) & 3 if blocks == 8 else at
                value = piece[at]
                if own:
                    value = value + got_ref[step, :, place, :].astype(f32)
                out_ref[step, :, place, :] = value.astype(bf16)
            low += height

    place = lanes(side * 2 * LANES, 2 * LANES)
    both = jnp.concatenate([ggp_ref[:, place], gup_ref[:, place]], axis=1)
    put(0, drows, dot_tn(rows, both))
    put(4 * drows, frows, dot_tn(inner_ref[...], grad_ref[:, lanes(side * 3 * LANES, 3 * LANES)]))


def combine_kernel(
    scal_ref, r0, r1, r2, r3, hidden_ref, nf_ref, gates_ref, slot_gate_ref, table_ref, cot_ref, router_ref,
    mixed_ref, grad_nf_ref, router_grad_ref, ret_ref,
):
    table = table_ref[...]
    fill_rows(scal_ref, (r0, r1, r2, r3), ret_ref)
    returned = ret_ref[...]
    scaled_rows = returned.astype(f32) * slot_gate_ref[...]
    mixed_ref[...] = (hidden_ref[...] + sum(dot_tn(table, t) for t in split(scaled_rows, 2))).astype(bf16)
    scored = dot_nt(returned, cot_ref[...]) * table.astype(f32)
    gates_t = gates_ref[...].T[:8]
    score_rows = [
        jnp.sum(scored[e * CAP : (e + 1) * CAP], axis=0, keepdims=True) for e in range(4)
    ]
    scores = jnp.concatenate(score_rows + [jnp.zeros((4, scored.shape[1]), f32)], axis=0)
    mean_gate = jnp.sum(gates_t * scores, axis=0, keepdims=True)
    grad_logits = gates_t * (scores - mean_gate)
    terms = split(grad_logits, 3)
    router_grad_ref[...] = sum(dot(t, nf_ref[...]) for t in terms)
    grad_nf_ref[...] = sum(dot_tn(t, router_ref[:8, :]) for t in terms)


def norm_back_kernel(
    scal_ref, b0, b1, b2, b3, hidden_ref, table_ref, cot_ref, gain_ref, part_ref,
    grad_hidden_ref, branch_ref, gain_grad_ref, back_ref,
):
    hidden = hidden_ref[...]
    fill_rows(scal_ref, (b0, b1, b2, b3), back_ref)
    grad_nf = dot_tn(table_ref[...], back_ref[...]) + part_ref[...]
    inverse = lax.rsqrt(jnp.mean(hidden * hidden, axis=-1, keepdims=True) + epsilon_norm)
    gain_grad_ref[...] = jnp.sum(grad_nf * hidden * inverse, axis=0, keepdims=True)
    scaled = grad_nf * gain_ref[1:2, :]
    grad_hidden = (
        cot_ref[...].astype(f32)
        + inverse * scaled
        - hidden * (inverse * inverse * inverse) * jnp.mean(scaled * hidden, axis=-1, keepdims=True)
    )
    grad_hidden_ref[...] = grad_hidden
    branch_ref[...] = grad_hidden.astype(bf16)


def late_grad_kernel(blocks, wrows, direct, scal_ref, normed_ref, dq_ref, att_ref, b0, b1, b2, b3, out_ref, q_ref, o_ref):
    b = scal_ref[1]
    flat = jnp.concatenate([dq_ref[j] for j in range(HEADS)], axis=0)
    q_ref[...] = dot_tn(normed_ref[...], flat).astype(bf16)
    total = None
    for j, ref in enumerate((b0, b1, b2, b3)):
        term = dot_tn(att_ref[j], ref[...])
        total = term if total is None else total + term
    o_ref[...] = total.astype(bf16)
    for r in range(blocks):
        owner = ring_owner(b // 2, -(r // 2)) * 2 + (b % 2 ^ r % 2)
        for source in range(HEADS):
            cols = slice(source * Q_COLS, (source + 1) * Q_COLS)
            if direct:
                low = pl.multiple_of((source * blocks + owner) * wrows, 16)
                out_ref[r % 2, r // 2, :wrows, cols] = q_ref[pl.ds(low, wrows), :]
            else:
                low = (source * blocks + r) * wrows
                out_ref[r, :wrows, cols] = q_ref[low : low + wrows, :]
        if direct:
            low = pl.multiple_of(owner * wrows, 16)
            out_ref[r % 2, r // 2, wrows:, :] = o_ref[pl.ds(low, wrows), :]
        else:
            out_ref[r, wrows:, :] = o_ref[r * wrows : (r + 1) * wrows, :]


def pair_shape(blocks, rest, direct):
    return ((2, blocks // 2) if direct else (blocks,)) + rest


def column_grad_kernel(blocks, wrows, direct, scal_ref, normed_ref, grad_ref, out_ref, hold_ref):
    b = scal_ref[1]
    flat = jnp.concatenate([grad_ref[j] for j in range(HEADS)], axis=0)
    hold_ref[...] = dot_tn(normed_ref[...], flat).astype(bf16)
    for r in range(blocks):
        for source in range(HEADS):
            if direct:
                out_ref[r % 2, r // 2, source] = hold_ref[own_rows(b, r, source, wrows, blocks), :]
            else:
                low = (source * blocks + r) * wrows
                out_ref[r, source] = hold_ref[low : low + wrows, :]


def normed_back_kernel(dq_ref, dkv_ref, w_ref, t0, t1, t2, t3, keep_ref, send_ref, gain_grad_ref):
    total = None
    for j, ref in enumerate((t0, t1, t2, t3)):
        part = dot_nt(dq_ref[j], w_ref[:, :Q_COLS]) + dot_nt(dkv_ref[j], w_ref[:, Q_COLS:W_COLS])
        value = ref[...].astype(f32)
        inverse = lax.rsqrt(jnp.mean(value * value, axis=-1, keepdims=True) + epsilon_norm)
        term = jnp.sum(part * (value * inverse), axis=0, keepdims=True)
        total = term if total is None else total + term
        if j % 2:
            send_ref[j // 2] = part.astype(bf16)
        else:
            keep_ref[j // 2] = part.astype(bf16)
    gain_grad_ref[...] = total


def tokens_back_kernel(keep_ref, got_ref, far_ref, tokens_ref, gain_ref, grad_hidden_ref, out_ref):
    grad_normed = keep_ref[0].astype(f32) + got_ref[0].astype(f32) + far_ref[...].astype(f32)
    value = tokens_ref[...].astype(f32)
    inverse = lax.rsqrt(jnp.mean(value * value, axis=-1, keepdims=True) + epsilon_norm)
    scaled = grad_normed * gain_ref[0:1, :]
    out_ref[...] = (
        grad_hidden_ref[...]
        + inverse * scaled
        - value * (inverse * inverse * inverse) * jnp.mean(scaled * value, axis=-1, keepdims=True)
    ).astype(bf16)


def small_sum(values, wait):
    devices = lax.axis_size("heads") * lax.axis_size("blk")
    n = values.shape[0]
    width = values.shape[1] // devices
    parts = jnp.transpose(values.reshape(n, devices, width), (1, 0, 2))
    padded = jnp.pad(parts, ((0, 0), (0, 8 - n), (0, 128 - width)))
    got = lax.all_to_all(tie(padded, wait), BOTH, 0, 0, tiled=True)
    return jnp.sum(got, axis=0)[:n, :width]


def halves(columns, core):
    half = columns.shape[1] // 2
    first, second = columns[:, :half], columns[:, half:]
    return jnp.where(core == 0, first, second), jnp.where(core == 0, second, first)


def unhalve(own, other, core):
    return jnp.concatenate(
        [jnp.where(core == 0, own, other), jnp.where(core == 0, other, own)], axis=1
    )


def unpack_half(buffer, drows, frows):
    def piece(low, high):
        return buffer[:, low:high].reshape(-1, LANES)

    matrices, base = [], 0
    for rows, count in ((drows, 2), (drows, 2), (frows, 3)):
        matrices.append(
            jnp.concatenate([piece(base + k * rows, base + (k + 1) * rows) for k in range(count)], axis=1)
        )
        base += rows * count
    return matrices


def pack_half(gate, up, down, count):
    pieces = []
    for matrix in (gate, up, down):
        rows = matrix.shape[0] // count
        for k in range(matrix.shape[1] // LANES):
            pieces.append(matrix[:, k * LANES : (k + 1) * LANES].reshape(count, rows, LANES))
    return jnp.concatenate(pieces, axis=1)


def shards(
    tokens,
    cotangent,
    routes,
    doc_lengths,
    attn_norm,
    w_query,
    key_weight,
    value_weight,
    w_output,
    ffn_norm,
    w_router,
    w_gate,
    w_up,
    w_down,
):
    blocks = lax.axis_size("blk")
    direct = blocks <= 8
    tok_dev, model = tokens.shape
    wrows = w_query.shape[0]
    drows = w_gate.shape[1]
    frows = w_down.shape[1]
    experts = w_router.shape[1]
    h, b = lax.axis_index("heads"), lax.axis_index("blk")
    core, x, y = h % 2, h // 2, b % 2
    zn = blocks // 2
    wide_cols = Q_COLS + 2 * K_COLS

    w_out = w_output.astype(bf16)
    if direct:
        wo_pieces = gather_few(w_out)
    else:
        wo_pieces = [lax.all_gather(w_out, "blk", axis=0, tiled=True)]

    far = swap(tokens, 2, 0)
    all_tokens = [tokens, swap(tokens, 1, 0), far, swap(far, 1, 0)]

    cut = [halves(m, core) for m in (w_gate[0].astype(bf16), w_up[0].astype(bf16), w_down[0].astype(bf16))]
    kept = pack_half(cut[0][0], cut[1][0], cut[2][0], 1)[0]
    given = pack_half(cut[0][1], cut[1][1], cut[2][1], 1)[0]
    at_home = core == y

    small_own = jnp.concatenate(
        [attn_norm.astype(bf16)[None], ffn_norm.astype(bf16)[None], w_router.astype(bf16).T], axis=0
    )
    small_own = jnp.pad(small_own.T, ((0, 0), (0, SMALL - 2 - experts)))
    heads_cat = jnp.concatenate(
        [
            w_query.astype(bf16).reshape(wrows, HEADS, Q_COLS),
            key_weight.astype(bf16).reshape(wrows, HEADS, K_COLS),
            value_weight.astype(bf16).reshape(wrows, HEADS, K_COLS),
            jnp.broadcast_to(small_own[:, None, :], (wrows, HEADS, SMALL)),
        ],
        axis=2,
    )
    by_head = lax.all_to_all(jnp.swapaxes(heads_cat, 0, 1), "heads", 0, 0, tiled=True)
    taken = swap(given, 1, 0)
    stay = jnp.where(at_home, kept, taken)
    leave = jnp.where(at_home, taken, kept)
    came = swap(leave, 0, 1)
    column = jnp.stack([jnp.where(y == 0, stay, came), jnp.where(y == 0, came, stay)])
    if direct:
        w_pieces = ring_gather(by_head, [far, all_tokens[1]], [wo_pieces[k] for k in (2, 4, 6)] + [all_tokens[3]])
        mine = [column, ring_step(tie(column, w_pieces[6]))]
    else:
        whole = lax.all_gather(by_head, "blk", axis=1, tiled=False)
        w_pieces = [whole.reshape(model, W_COLS + SMALL)]
        mine = lax.all_gather(column, "blk", axis=0, tiled=False, axis_index_groups=z_groups(blocks))
        mine = mine.reshape((blocks,) + kept.shape)

    ends = jnp.cumsum(doc_lengths)
    block_of = (h ^ jnp.arange(HEADS, dtype=jnp.int32)) * blocks + b
    query_pos = block_of[:, None] * tok_dev + jnp.arange(tok_dev, dtype=jnp.int32)[None, :]
    start = jnp.max(
        jnp.where(ends[None, None, :] <= query_pos[:, :, None], ends[None, None, :], 0), axis=2
    ).astype(jnp.int32)
    scal = jnp.concatenate(
        [
            jnp.stack([h, b]).astype(jnp.int32),
            start[:, 0] // (2 * tok_dev),
        ]
    )
    start = start[:, None, :]

    member = jnp.sum((routes[:, :, None] == jnp.arange(experts)[None, None, :]).astype(f32), axis=1)
    lower = (jnp.arange(tok_dev)[:, None] > jnp.arange(tok_dev)[None, :]).astype(bf16)
    rank = dot(lower, member.astype(bf16))
    slot = jnp.arange(CAP, dtype=f32)
    table = (
        ((rank.T[:, None, :] == slot[None, :, None]) & (member.T[:, None, :] > 0))
        .astype(bf16)
        .reshape(experts * CAP, tok_dev)
    )
    member = jnp.pad(member, ((0, 0), (0, 128 - experts)))

    normed, queries, kv_own, gains, router_all, weights = project(
        scal, all_tokens, w_pieces, blocks, [table, member, start]
    )
    if direct:
        kv = ring_gather(kv_own)
        mine.append(ring_step(tie(mine[1], kv[2])))
        mine.append(ring_step(mine[2]))
    else:
        kv = [blk_gather(kv_own)]
    att, lse = attend(scal, queries, kv, start, blocks)
    keep, send, output_w = output_parts(scal, att, wo_pieces, model, blocks, [])
    got, far = heads_sum(keep, send)
    seconds = [swap(piece, 1, 0) for piece in mine[:3]] if direct else []
    slot = shaped((CAP, model), bf16)
    hold = pltpu.VMEM((experts * CAP, model), bf16)
    routed = call(
        route_kernel,
        "route",
        [slot] * 8
        + [
            shaped((tok_dev, model), f32),
            shaped((tok_dev, model), bf16),
            shaped((tok_dev, 128), f32),
            shaped((experts * CAP, 1), f32),
        ],
        [scal],
        [keep, got, far, tokens, gains, router_all, member, table, cotangent],
        [hold, hold],
        waits=seconds,
        cost=3,
    )
    sent, grad_sent = routed[:4], routed[4:8]
    hidden, normed_ffn, gates, slot_gate = routed[8:]

    def to_experts(pieces):
        return [pieces[0]] + [swap(pieces[r], r // 2 * 2, r % 2) for r in range(1, experts)]

    arrived = to_experts(sent)
    grad_arrived = to_experts(grad_sent)
    if direct:
        weights_in = mine + seconds + [swap(tie(mine[3], *arrived[1:]), 1, 0)]
        gathered = [pltpu.VMEM((blocks,) + kept.shape, bf16)] * 2
    else:
        mine = tie(mine, sent[0])
        other = swap(mine, 1, 0)
        weights_in, gathered = [mine, other], []
    rows_all = experts * CAP
    ff = frows * blocks
    fwd = call(
        functools.partial(expert_kernel, drows, frows, direct),
        "expert",
        [slot] * 4
        + [shaped((rows_all, ff), f32), shaped((rows_all, ff), f32), shaped((rows_all, ff), bf16)],
        [scal],
        arrived + weights_in,
        [hold] + gathered,
        cost=2,
    )
    gate_pre, up_pre, inner = fwd[4:7]
    returned = to_experts(fwd[:4])
    grad_pre = call(
        functools.partial(expert_back_kernel, drows, frows, len(weights_in)),
        "expert_back",
        [shaped((rows_all, ff), bf16)] * 2,
        [scal],
        grad_arrived + [gate_pre, up_pre] + weights_in,
        [hold] + gathered,
        cost=2,
    )
    grad_pre = list(grad_pre)

    def expert_weights(own, extra, waits=()):
        return call(
            functools.partial(expert_weights_kernel, drows, frows, blocks, own),
            "expert_weights",
            [shaped((zn, 2) + kept.shape, bf16)],
            [scal],
            arrived + grad_arrived + [inner] + grad_pre + extra,
            [hold, hold],
            waits=waits,
            cost=1,
        )[0]

    grads_other = expert_weights(False, [])
    grads_met = swap(grads_other, 1, 0)
    grad_in = call(
        functools.partial(expert_input_kernel, drows, frows, len(weights_in)),
        "expert_input",
        [slot] * 4,
        [scal],
        grad_pre + weights_in,
        [hold] + gathered,
        waits=[grads_other],
        cost=2,
    )
    grad_returned = to_experts(grad_in)
    chip_grads = expert_weights(True, [grads_met], [grad_in[0]] + returned[1:])

    mixed, part_nf, router_grad = call(
        combine_kernel,
        "combine",
        [
            shaped((tok_dev, model), bf16),
            shaped((tok_dev, model), f32),
            shaped((8, model), f32),
        ],
        [scal],
        returned + [hidden, normed_ffn, gates, slot_gate, table, cotangent, router_all],
        [hold],
        waits=[chip_grads],
        cost=1,
    )
    later = [mixed]
    if direct:

        def met(moving, k):
            return (moving.astype(f32) + chip_grads[k].astype(f32)).astype(bf16)

        second_sum = met(ring_step(chip_grads[3]), 2)
        third_sum = met(ring_step(second_sum), 1)
        later_still = [second_sum]
    else:
        z_grads = lax.psum_scatter(
            chip_grads, "blk", scatter_dimension=0, tiled=False, axis_index_groups=z_groups(blocks)
        )
        later_still = []
    grad_hidden, branch, gain_two_grad = call(
        norm_back_kernel,
        "norm_back",
        [
            shaped((tok_dev, model), f32),
            shaped((tok_dev, model), bf16),
            shaped((1, model), f32),
        ],
        [scal],
        grad_returned + [hidden, table, cotangent, gains, part_nf],
        [hold],
        waits=later,
    )

    far_branch = swap(branch, 2, 0)
    branches = [branch, swap(branch, 1, 0), far_branch, swap(far_branch, 1, 0)]
    dq, dkv = attend_back(scal, queries, kv, start, att, lse, output_w, branches, blocks, later_still)
    if direct:
        dkv_own, onward = reduce_pieces(dkv[:zn], dkv[zn:], third_sum)
    else:
        dkv_own, onward = blk_reduce(dkv[0]), [dq]
    dkv_own = dkv_own.astype(bf16)
    if direct:
        z_grads = met(ring_step(tie(third_sum, dkv_own)), 0)

    def column_grads(name, grad, waits=()):
        cols = grad.shape[2]
        return call(
            functools.partial(column_grad_kernel, blocks, wrows, direct),
            name,
            [shaped(pair_shape(blocks, (HEADS, wrows, cols), direct), bf16)],
            [scal],
            [normed, grad],
            [pltpu.VMEM((model, cols), bf16)],
            waits=waits,
        )[0]

    late_parts = call(
        functools.partial(late_grad_kernel, blocks, wrows, direct),
        "late_grad",
        [shaped(pair_shape(blocks, (2 * wrows, model), direct), bf16)],
        [scal],
        [normed, dq, att] + branches,
        [pltpu.VMEM((model, Q_COLS), bf16), pltpu.VMEM((Q_COLS, model), bf16)],
        waits=[dq],
    )[0]
    late_parts = tie(late_parts, *(onward[:2] + ([third_sum] if direct else [])))
    late_sums = reduce_ring(late_parts, direct)
    grad_wout = late_sums[wrows:]
    sum_wq = jnp.swapaxes(late_sums[:wrows].reshape(wrows, HEADS, Q_COLS), 0, 1)
    keep, send, gain_one_grad = call(
        normed_back_kernel,
        "normed_back",
        [shaped((2, tok_dev, model), bf16)] * 2 + [shaped((1, model), f32)],
        [],
        [dq, dkv_own, weights] + all_tokens,
        waits=[],
        cost=6,
    )
    got, far = heads_sum(keep, send)
    kv_parts = column_grads("key_value_grad", dkv_own, [send])
    sum_wkv, kv_sent = reduce_few(kv_parts, direct, far, z_grads)
    stay = jnp.where(y == 0, z_grads[0], z_grads[1])
    came = swap(jnp.where(y == 0, z_grads[1], z_grads[0]), 0, 1)
    kept_grad = jnp.where(at_home, stay, came)
    taken_grad = swap(jnp.where(at_home, came, stay), 1, 0)
    grad_tokens = call(
        tokens_back_kernel,
        "tokens_back",
        [shaped((tok_dev, model), bf16)],
        [],
        [keep, got, far, tokens, gains, grad_hidden],
    )[0]
    column_sums = jnp.concatenate([sum_wq.astype(bf16), sum_wkv.astype(bf16)], axis=2)
    by_row = lax.all_to_all(tie(column_sums, came, grad_tokens), "heads", 0, 0, tiled=True)
    by_row = jnp.swapaxes(by_row, 0, 1).astype(f32)
    grad_wq = by_row[:, :, :Q_COLS].reshape(wrows, -1)
    grad_wk = by_row[:, :, Q_COLS : Q_COLS + K_COLS].reshape(wrows, -1)
    grad_wv = by_row[:, :, Q_COLS + K_COLS :].reshape(wrows, -1)
    router_back = router_grad[:experts]
    small_grads = small_sum(jnp.concatenate([gain_one_grad, gain_two_grad, router_back], axis=0), far)

    owned = unpack_half(kept_grad[None], drows, frows)
    fetched = unpack_half(taken_grad[None], drows, frows)
    grad_gate_w, grad_up_w, grad_down_w = [
        unhalve(o, f, core).astype(f32) for o, f in zip(owned, fetched)
    ]
    return (
        mixed,
        grad_tokens,
        small_grads[0],
        grad_wq,
        grad_wk,
        grad_wv,
        grad_wout,
        small_grads[1],
        small_grads[2 : 2 + experts].T,
        grad_gate_w[None],
        grad_up_w[None],
        grad_down_w[None],
    )


def solution(mesh):
    rows = P(("heads", "blk"), None)
    flat = P(("heads", "blk"))
    expert = P("heads", "blk", None)
    return jax.shard_map(
        shards,
        mesh=mesh,
        in_specs=(
            rows, rows, rows, P(), flat, rows, rows, rows, rows, flat, rows, expert, expert, expert,
        ),
        out_specs=(
            rows, rows, flat, rows, rows, rows, rows, flat, rows, expert, expert, expert,
        ),
        check_vma=False,
    )
```
